128 devices in a mesh: dp: 2 (over x_lo), fsdp: 64 (over x_hi, z, y, core).
Axes of the slice: x: 4 (x_hi: 2, x_lo: 2; x = x_hi * 2 + x_lo), y: 4, z: 4, core: 2. Of those that a mesh axis runs over, the one named last changes fastest.
Arguments:
- states: bfloat16 [32768, 1536], P(('dp', 'fsdp')), may hold values from -24 to 24
- policy: bfloat16 [1536, 256], P('fsdp'), may hold values from -0.15625 to 0.15625
- action_embed: bfloat16 [256, 1536], P('fsdp'), may hold values from -0.375 to 0.375
- norm_gain: bfloat16 [1536], P('fsdp'), may hold values from 0.5 to 1.5
- hidden_in: bfloat16 [1536, 3072], P('fsdp'), may hold values from -0.15625 to 0.15625
- hidden_out: bfloat16 [3072, 1536], P('fsdp'), may hold values from -0.109375 to 0.109375
- precision: float32 [256], replicated, may hold values from 0.25 to 4
- gradient: float32 [1536, 256], P('fsdp'), may hold values from -6 to 6
Outputs:
- update: float32 [1536, 256], P('fsdp')
- residual: float32 [1536, 256], P('fsdp')
The draws below stay inside these ranges and needn't reach their ends.
All inputs are finite; a program needn't handle non-finite values.
Results may differ from the reference program's by a relative error of at most 0.01.
Values may be sent and summed in bfloat16 or wider, within the bound.
A program may use at most 128 MiB of HBM per device.

```python
import math
import jax
import jax.numpy as jnp
from jax import lax

D = 1536
FF = 3072
ACT = 256
ITERS = 2
ROWS_DEV = 256
STATES = 32768
N_DP = 2
N_FSDP = 64


def spiked(drawn, key, source, target, parts, factor):
    def block_of(position):
        return (jnp.arange(drawn.shape[position]) // (drawn.shape[position] // parts)).reshape((-1,) + (1,) * (drawn.ndim - 1 - position))

    one_side = jax.random.permutation(key, parts)[block_of(target)]
    second = (block_of(target) + parts // 2) % parts
    return jnp.where((block_of(source) == one_side) | (block_of(source) == second), factor * drawn, drawn)


def block_scale(rng, dims, cuts, smallest, largest):
    level, own = 1.0, jax.random.fold_in(rng, 6)
    for position, blocks in cuts:
        steps = jnp.exp(jax.random.uniform(jax.random.fold_in(own, position), (blocks,), jnp.float32, smallest / len(cuts), largest / len(cuts)))
        level = level * jnp.repeat(steps, dims[position] // blocks).reshape([-1 if axis == position else 1 for axis in range(len(dims))])
    return level


def scatter_about(stream_key, shape, spread, limit, cuts=(), dtype=jnp.bfloat16):
    loudness = block_scale(stream_key, shape, cuts, -0.22, 0.18) if cuts else 1.0
    drawn = jax.random.normal(stream_key, shape, jnp.float32) * spread * loudness
    return jnp.minimum(jnp.maximum(drawn, -limit), limit).astype(dtype)


def bell_draw_with(rng, shape, scale, reach, pieces, heavy, dtype=jnp.bfloat16):
    array = scale * jax.random.normal(rng, shape, jnp.float32)
    if pieces:
        array = array * block_scale(rng, shape, pieces, -0.22, 0.18)
    return jnp.clip(spiked(array, jax.random.fold_in(rng, 3), *heavy), -reach, reach).astype(dtype)


def setup_inputs(seed: int = 0) -> dict:
    key_list = jax.random.split(jax.random.key(seed), 9)
    return {
        "states": bell_draw_with(key_list[0], (STATES, D), 1.0, 24.0, ((0, 128),), (0, 1, 128, 5.5)),
        "policy": scatter_about(key_list[1], (D, ACT), D ** -0.5, 0.15625, ((0, 64),)),
        "action_embed": scatter_about(key_list[2], (ACT, D), ACT ** -0.5, 0.375, ((0, 64),)),
        "norm_gain": jnp.clip(1.0 + 0.1 * jax.random.normal(key_list[3], (D,), jnp.float32), 0.5, 1.5).astype(jnp.bfloat16),
        "hidden_in": scatter_about(key_list[4], (D, FF), D ** -0.5, 0.15625, ((0, 64),)),
        "hidden_out": scatter_about(key_list[5], (FF, D), FF ** -0.5, 0.109375, ((0, 64),)),
        "precision": jnp.clip(jnp.exp(jax.random.uniform(key_list[6], (ACT,), jnp.float32, math.log(0.25), math.log(4.0))), 0.25, 4.0),
        "gradient": scatter_about(key_list[7], (D, ACT), 1.0, 6.0, ((0, 64),), jnp.float32),
    }


EPS = 1e-05
DAMPING = 0.1

def contract_last(left, right):
    return lax.dot_general(left, right, (((1,), (1,)), ((), ())), preferred_element_type=jnp.float32)

def contract_first(left, right):
    return lax.dot_general(left, right, (((0,), (0,)), ((), ())), preferred_element_type=jnp.float32)

def swish_slope(pre):
    sigma = jax.nn.sigmoid(pre)
    return sigma * (1.0 + pre * (1.0 - sigma))

def norm_back(unit, scale, value):
    return scale * (value - unit * lax.optimization_barrier(jnp.mean(unit * value, axis=-1, keepdims=True)))

def imagine(start, policy, embed, gain, inner, outer):
    first = jnp.tanh(jnp.dot(start, policy, preferred_element_type=jnp.float32))
    mixed = start.astype(jnp.float32) + jnp.dot(first.astype(jnp.bfloat16), embed, preferred_element_type=jnp.float32)
    scale = lax.rsqrt(lax.optimization_barrier(jnp.mean(mixed * mixed, axis=-1, keepdims=True)) + EPS)
    unit = mixed * scale
    normed = (unit * gain.astype(jnp.float32)).astype(jnp.bfloat16)
    pre = jnp.dot(normed, inner, preferred_element_type=jnp.float32)
    active = jax.nn.silu(pre).astype(jnp.bfloat16)
    later = (mixed + jnp.dot(active, outer, preferred_element_type=jnp.float32)).astype(jnp.bfloat16)
    second = jnp.tanh(jnp.dot(later, policy, preferred_element_type=jnp.float32))
    return (first, second, later, unit, scale, swish_slope(pre))

def sweeps(start, first, second, later, unit, scale, slope, direction_b, policy, embed, gain, inner, outer, weighting):
    gain_wide = gain.astype(jnp.float32)
    tangent_first = (1.0 - first * first) * jnp.dot(start, direction_b, preferred_element_type=jnp.float32)
    tangent_mix = jnp.dot(tangent_first.astype(jnp.bfloat16), embed, preferred_element_type=jnp.float32)
    tangent_norm = (norm_back(unit, scale, tangent_mix) * gain_wide).astype(jnp.bfloat16)
    tangent_active = (slope * jnp.dot(tangent_norm, inner, preferred_element_type=jnp.float32)).astype(jnp.bfloat16)
    tangent_later = (tangent_mix + jnp.dot(tangent_active, outer, preferred_element_type=jnp.float32)).astype(jnp.bfloat16)
    tangent_second = (1.0 - second * second) * (jnp.dot(tangent_later, policy, preferred_element_type=jnp.float32) + jnp.dot(later, direction_b, preferred_element_type=jnp.float32))
    cot_second = ((1.0 - second * second) * (weighting * tangent_second)).astype(jnp.bfloat16)
    cot_later = contract_last(cot_second, policy)
    cot_pre = (slope * contract_last(cot_later.astype(jnp.bfloat16), outer)).astype(jnp.bfloat16)
    cot_norm = contract_last(cot_pre, inner) * gain_wide
    cot_mix = cot_later + norm_back(unit, scale, cot_norm)
    cot_first = ((1.0 - first * first) * (weighting * tangent_first + contract_last(cot_mix.astype(jnp.bfloat16), embed))).astype(jnp.bfloat16)
    return (cot_first, cot_second)

def reference(states, policy, action_embed, norm_gain, hidden_in, hidden_out, precision, gradient):
    blocks = states.reshape(N_DP * N_FSDP, ROWS_DEV, D)
    caches = lax.map(lambda start: imagine(start, policy, action_embed, norm_gain, hidden_in, hidden_out), blocks)
    weighting = precision / STATES

    def product(direction):
        direction_b = direction.astype(jnp.bfloat16)

        def block_term(item):
            start, first, second, later, unit, scale, slope = item
            cot_first, cot_second = sweeps(start, first, second, later, unit, scale, slope, direction_b, policy, action_embed, norm_gain, hidden_in, hidden_out, weighting)
            return contract_first(start, cot_first) + contract_first(later, cot_second)
        terms = lax.map(block_term, (blocks,) + tuple(caches))
        return lax.optimization_barrier(jnp.sum(terms, axis=0)) + DAMPING * direction
    update = jnp.zeros_like(gradient)
    residual = gradient
    direction = gradient
    norm_now = jnp.sum(gradient * gradient)
    for turn in range(ITERS):
        image = product(direction)
        alpha = norm_now / jnp.sum(direction * image)
        update = update + alpha * direction
        residual = residual - alpha * image
        if turn + 1 < ITERS:
            norm_next = jnp.sum(residual * residual)
            direction = residual + norm_next / norm_now * direction
            norm_now = norm_next
    return (update, residual)
```

```python
import functools

import jax
import jax.numpy as jnp
from jax import lax
from jax.experimental import pallas as pl
from jax.experimental.pallas import tpu as pltpu
from jax.sharding import PartitionSpec as P

MESH = pl.DeviceIdType.MESH
F32 = jnp.float32
BF16 = jnp.bfloat16
EPS = 1e-05
DAMPING = 0.1
ALL = slice(None)

ROWS = 256
D = 1536
FF = 3072
ACT = 256
TOTAL_ROWS = 32768
N_ITEM = 5
ITEM_SEMS = 41
OTHER_SEMS = 2 + 1 + 3 * 10 + 2 * (1 + 6 + 6 + 3) + (6 + 6 + 1) + 1


def nn(left, right):
    return jnp.dot(left, right, preferred_element_type=F32)


def nt(left, right):
    return lax.dot_general(left, right, (((1,), (1,)), ((), ())), preferred_element_type=F32)


def swish_slope(pre, sigma):
    return sigma * (1.0 + pre * (1.0 - sigma))


def kernel(
    states,
    pack,
    embed_in,
    inner_in,
    outer_in,
    precision,
    out_update,
    out_residual,
    S,
    HI,
    HO,
    pack_far,
    inner_wide,
    inner_far,
    policy,
    embed,
    gain,
    gain_tall,
    going,
    start_t,
    later_t,
    NT,
    AA,
    slope,
    mixed,
    unit,
    scale,
    tmix,
    first_d,
    second_d,
    tfirst,
    later,
    tlater,
    cot_later,
    cot_b,
    cot_pre,
    cot_first,
    cot_second,
    IP,
    RB,
    ACC,
    R1,
    T2,
    R2,
    T3,
    SC,
    g32,
    res32,
    RG,
    out_near,
    out_far,
    send_sem,
    recv_sem,
):
    lo = lax.axis_index("dp")
    f = lax.axis_index("fsdp")
    c = f % 2
    y = (f // 2) % 4
    z = (f // 8) % 4
    hi = f // 32
    x = hi * 2 + lo

    def dev(dx=None, dy=0, dz=0, core=None):
        xx = x if dx is None else (x + dx) % 4
        yy, zz = (y + dy) % 4, (z + dz) % 4
        cc = c if core is None else core
        return (xx % 2, (((xx // 2) * 4 + zz) * 4 + yy) * 2 + cc)

    def axis_dev(axis, d):
        return dev(**{"d" + axis: d})

    opp = ((3 - x) % 2, ((((3 - x) // 2) * 4 + z) * 4 + y) * 2 + c)
    partner = dev(core=1 - c)

    pending = []
    counter = [N_ITEM * ITEM_SEMS]

    def copy(src, dst, sem, to):
        op = pltpu.make_async_remote_copy(
            src_ref=src,
            dst_ref=dst,
            send_sem=send_sem.at[sem],
            recv_sem=recv_sem.at[sem],
            device_id=to,
            device_id_type=MESH,
        )
        op.start()
        pending.append(op)
        return op

    def fresh(n=1):
        base = counter[0]
        counter[0] += n
        return base

    barrier = pltpu.get_barrier_semaphore()
    peers = [partner] + [axis_dev(a, d) for a in ("x", "y", "z") for d in (1, 2, 3)]
    for peer in peers:
        pl.semaphore_signal(barrier, inc=1, device_id=peer, device_id_type=MESH)
    inner_wide[...] = inner_in[...].astype(F32)
    pl.semaphore_wait(barrier, len(peers))

    half = pl.ds(pl.multiple_of((1 - c) * 1536, 128), 1536)
    op_inner = copy(inner_wide.at[:, half], inner_far, fresh(), partner)
    half = pl.ds(pl.multiple_of((1 - c) * 384, 128), 384)
    op_pack = copy(pack.at[:, half], pack_far, fresh(), partner)

    def part(item, t, h, zz, yy, cut):
        if item == 0:
            rows = pl.ds(pl.multiple_of(lo * 32, 32), 32) if cut == 0 else ALL
            if cut == 1:
                rows = pl.ds(pl.multiple_of((1 - lo) * 32, 32), 32)
            return S.at[c, t, h, zz, yy, rows, :]
        cols = ALL
        if cut == 0:
            cols = pl.ds(pl.multiple_of(lo * 128, 128), 128)
        if cut == 1:
            cols = pl.ds(pl.multiple_of((1 - lo) * 128, 128), 128)
        if item < 3:
            return HI.at[c, (item - 1) * 3 + t, h, zz, yy, :, cols]
        return HO.at[(item - 3) * 3 + t, h, zz, yy, c, :, cols]

    one = lambda i: pl.ds(i, 1)
    ops = {}

    def send(item, key, sem, t, h, zz, yy, cut, to):
        ref = part(item, t, h, zz, yy, cut)
        ops[(item, key)] = copy(ref, ref, item * ITEM_SEMS + sem, to)

    def wait(item, *keys):
        for key in keys:
            ops[(item, key)].wait_recv()

    def stage_a(k):
        send(k, "0x", 0, 0, one(hi), one(z), one(y), None, opp)
        for d in (1, 2, 3):
            send(k, "1y%d" % d, 8 + d, 1, one(hi), one(z), one(y), 0, axis_dev("y", d))
            send(k, "2z%d" % d, 18 + d, 2, one(hi), one(z), one(y), None, axis_dev("z", d))

    def stage_b(k):
        wait(k, "0x")
        for d in (1, 2, 3):
            send(k, "0y%d" % d, d, 0, ALL, one(z), one(y), None, axis_dev("y", d))
        wait(k, "1y1", "1y2", "1y3")
        for d in (1, 2, 3):
            send(k, "1z%d" % d, 11 + d, 1, one(hi), one(z), ALL, 0, axis_dev("z", d))
        wait(k, "2z1", "2z2", "2z3")
        send(k, "2x", 22, 2, one(hi), ALL, one(y), None, opp)

    def hand(k, key, sem, t, h, zz, yy, cut):
        send(k, key, 26 + sem, t, h, zz, yy, cut, partner)

    low, high = pl.ds(0, 2), pl.ds(2, 2)
    h0, h1 = pl.ds(0, 1), pl.ds(1, 1)
    zb, zf, zo = (z + 3) % 4, (z + 1) % 4, (z + 2) % 4
    yb, yf, yo = (y + 3) % 4, (y + 1) % 4, (y + 2) % 4

    def x_part(k, d):
        xx = (x + d) % 4
        h = one(xx // 2)
        other = xx % 2
        if k == 0:
            return h, pl.ds(pl.multiple_of(other * 32, 32), 32), ALL
        return h, ALL, pl.ds(pl.multiple_of(other * 128, 128), 128)

    def x_ref(k, d, zz):
        h, rows, cols = x_part(k, d)
        if k == 0:
            return S.at[c, 1, h, zz, :, rows, :]
        if k < 3:
            return HI.at[c, (k - 1) * 3 + 1, h, zz, :, :, cols]
        return HO.at[(k - 3) * 3 + 1, h, zz, :, c, :, cols]

    def x_send(k, key, sem, d, zz, to):
        ref = x_ref(k, d, zz)
        ops[(k, key)] = copy(ref, ref, k * ITEM_SEMS + sem, to)

    def stage_c(k):
        wait(k, "0y1", "0y2", "0y3")
        send(k, "0f", 4, 0, ALL, one(z), ALL, None, axis_dev("z", 1))
        send(k, "0b", 5, 0, ALL, one(z), ALL, None, axis_dev("z", 3))
        wait(k, "1z1", "1z2", "1z3")
        x_send(k, "1f", 15, 0, ALL, axis_dev("x", 1))
        x_send(k, "1b", 16, 0, ALL, axis_dev("x", 3))
        wait(k, "2x")
        send(k, "2f", 23, 2, ALL, ALL, one(y), None, axis_dev("y", 1))
        send(k, "2b", 24, 2, ALL, ALL, one(y), None, axis_dev("y", 3))
        hand(k, "0p0", 0, 0, ALL, one(z), ALL, None)
        x_send(k, "1p0", 26 + 5, 0, ALL, partner)
        hand(k, "2p0", 10, 2, ALL, ALL, one(y), None)

    def stage_d(k):
        wait(k, "0f")
        send(k, "0ff", 6, 0, h0, one(zb), ALL, None, axis_dev("z", 1))
        wait(k, "0b")
        send(k, "0bb", 7, 0, h1, one(zf), ALL, None, axis_dev("z", 3))
        wait(k, "1f")
        x_send(k, "1ff", 17, 3, low, axis_dev("x", 1))
        wait(k, "1b")
        x_send(k, "1bb", 18, 1, high, axis_dev("x", 3))
        wait(k, "2f")
        send(k, "2ff", 25, 2, h0, ALL, one(yb), None, axis_dev("y", 1))
        wait(k, "2b")
        send(k, "2bb", 8, 2, h1, ALL, one(yf), None, axis_dev("y", 3))
        hand(k, "0p1", 1, 0, ALL, one(zb), ALL, None)
        hand(k, "0p2", 2, 0, ALL, one(zf), ALL, None)
        x_send(k, "1p1", 26 + 6, 3, ALL, partner)
        x_send(k, "1p2", 26 + 7, 1, ALL, partner)
        hand(k, "2p1", 11, 2, ALL, ALL, one(yb), None)
        hand(k, "2p2", 12, 2, ALL, ALL, one(yf), None)

    def stage_e(k):
        wait(k, "0ff")
        hand(k, "0p3", 3, 0, h0, one(zo), ALL, None)
        wait(k, "0bb")
        hand(k, "0p4", 4, 0, h1, one(zo), ALL, None)
        wait(k, "1ff")
        x_send(k, "1p3", 26 + 8, 2, low, partner)
        wait(k, "1bb")
        x_send(k, "1p4", 26 + 9, 2, high, partner)
        wait(k, "2ff")
        hand(k, "2p3", 13, 2, h0, ALL, one(yo), None)
        wait(k, "2bb")
        hand(k, "2p4", 14, 2, h1, ALL, one(yo), None)

    def stage_f(k):
        wait(k, *["%dp%d" % (t, i) for t in range(3) for i in range(5)])

    scalar_ops = {}
    scalar_base = fresh(30)
    places = (("core", c, 2), ("y", y, 4), ("z", z, 4), ("x", x, 4))

    def total_send(which, phase, value):
        axis, own, n = places[phase]
        SC[which, phase, own] = value
        ref = SC.at[which, phase, own]
        base = scalar_base + 10 * which + (0, 1, 4, 7)[phase]
        todo = []
        for d in range(1, n):
            to = partner if axis == "core" else axis_dev(axis, d)
            todo.append(copy(ref, ref, base + d - 1, to))
        scalar_ops[(which, phase)] = todo

    def total_take(which, phase):
        for op in scalar_ops[(which, phase)]:
            op.wait_recv()
        n = places[phase][2]
        value = SC[which, phase, 0]
        for i in range(1, n):
            value = value + SC[which, phase, i]
        return value

    def total_step(which, phase):
        value = total_take(which, phase)
        if phase < 3:
            total_send(which, phase + 1, value)
        return value

    def fold(value):
        value = value.reshape(-1, 8, value.shape[-1]).sum(axis=0)
        tile = value[:, 0:128]
        for i in range(1, value.shape[-1] // 128):
            tile = tile + value[:, 128 * i : 128 * i + 128]
        return tile

    def whole(tile):
        return jnp.sum(jnp.sum(tile, axis=1, keepdims=True), axis=0, keepdims=True)

    weigh_rows = outer_in
    for ct in range(6):
        if ct % 3 == 1:
            left = weigh_rows[:, 256 * ct : 256 * ct + 128]
            right = weigh_rows[:, 256 * ct + 128 : 256 * ct + 256]
            HO[ct, hi, z, y, c, :, pl.ds(pl.multiple_of(lo * 128, 128), 128)] = jnp.where(lo == 0, left, right)
        else:
            HO[ct, hi, z, y, c] = weigh_rows[:, 256 * ct : 256 * ct + 256]

    near = pack[:, pl.ds(pl.multiple_of(c * 384, 128), 384)]
    g_own = jnp.concatenate([pack[:, 128:256], pack[:, 512:640]], axis=1)
    total_send(0, 0, fold(g_own * g_own))
    op_pack.wait_recv()
    far = pack_far[...]
    pair = jnp.concatenate([jnp.where(c == 0, near, far), jnp.where(c == 0, far, near)], axis=0)
    g32[hi] = pair[:, 128:256]
    gains = pair[:, 256:384].astype(BF16)
    S[c, 0, hi, z, y, 0:48] = pair[:, 0:128].astype(BF16)
    S[c, 0, hi, z, y, 48:64] = gains[0:16]
    gb = pair[:, 128:256]
    both = jnp.concatenate([gb, pair[16:32, 256:384]], axis=0)
    S[c, 1, hi, z, y, pl.ds(pl.multiple_of(lo * 32, 32), 32)] = jnp.where(lo == 0, both[0:32], both[32:64]).astype(BF16)
    S[c, 2, hi, z, y, 0:48] = embed_in[...]
    S[c, 2, hi, z, y, 48:64] = gains[32:48]
    stage_a(0)
    op_g32 = copy(g32.at[one(hi)], g32.at[one(hi)], fresh(), opp)

    op_inner.wait_recv()
    near = inner_wide[:, pl.ds(pl.multiple_of(c * 1536, 128), 1536)]
    far = inner_far[...]
    pair = jnp.concatenate([jnp.where(c == 0, near, far), jnp.where(c == 0, far, near)], axis=0)
    for ct in range(6):
        if ct % 3 == 1:
            left = pair[:, 256 * ct : 256 * ct + 128]
            right = pair[:, 256 * ct + 128 : 256 * ct + 256]
            HI[c, ct, hi, z, y, :, pl.ds(pl.multiple_of(lo * 128, 128), 128)] = jnp.where(lo == 0, left, right).astype(BF16)
        else:
            HI[c, ct, hi, z, y] = pair[:, 256 * ct : 256 * ct + 256].astype(BF16)
    stage_a(1)
    stage_b(0)
    stage_a(2)
    stage_b(1)
    stage_c(0)
    total_step(0, 0)
    stage_a(3)
    stage_a(4)
    stage_c(1)
    stage_b(2)
    stage_d(0)
    total_step(0, 1)

    @pl.loop(0, 6)
    def _(i):
        s = pl.ds(pl.multiple_of(i * 256, 256), 256)
        start_t[s, :] = states[:, s].astype(F32).T.astype(BF16)

    stage_e(0)
    total_step(0, 2)
    stage_c(2)
    stage_f(0)
    rr = whole(total_step(0, 3)) * 0.5

    for t in range(3):
        for a in range(2):
            for b in range(4):
                gain_tall[a, b, :, 16 * t : 16 * t + 16] = S[0, t, a, b, :, 48:64]
    pick = (lax.broadcasted_iota(jnp.int32, (16, 128), 1) == 0).astype(BF16)
    gain[...] = nt(pick, gain_tall[...].reshape(D, 128))[0:8]
    for cc in range(2):
        for a in range(2):
            policy[768 * a : 768 * a + 768, 128 * cc : 128 * cc + 128] = S[cc, 0, a, :, :, 0:48].reshape(768, 128)
            going[768 * a : 768 * a + 768, 128 * cc : 128 * cc + 128] = S[cc, 1, a, :, :, 0:48].reshape(768, 128)
    for q in range(4):
        total = jnp.zeros((ACT, 384), F32)
        for cc in range(2):
            out_row = lax.broadcasted_iota(jnp.int32, (ACT, 512), 0)
            in_row = lax.broadcasted_iota(jnp.int32, (ACT, 512), 1)
            want = (lax.div(out_row, 8) * 16) + 4 * q + lax.rem(out_row, 4)
            mine = lax.rem(lax.div(out_row, 4), 2) == cc
            choose = jnp.where(mine & (in_row == want), 1.0, 0.0).astype(BF16)
            block = jnp.concatenate(
                [S[cc, 2, :, :, :, 16 * s : 16 * s + 16].reshape(512, 128) for s in range(3)], axis=1
            )
            total = total + nn(choose, block)
        embed[:, 384 * q : 384 * q + 384] = total.astype(BF16)

    def blocks(n):
        return pl.loop(0, ROWS // n)

    first = jnp.tanh(nn(states[...], policy[...]))
    first_d[...] = 1.0 - first * first
    mixed[...] = nn(first.astype(BF16), embed[...])
    tfirst[...] = first_d[...] * nn(states[...], going[...])
    tmix[...] = nn(tfirst[...].astype(BF16), embed[...])

    @blocks(32)
    def _(i):
        s = pl.ds(pl.multiple_of(i * 32, 32), 32)
        m = states[s, :].astype(F32) + mixed[s, :]
        mixed[s, :] = m
        r = lax.rsqrt(jnp.mean(m * m, axis=-1, keepdims=True) + EPS)
        scale[s, :] = jnp.broadcast_to(r, (32, 128))
        u = m * r
        unit[s, :] = u
        g = gain[0:1, :]
        NT[s, :] = (u * g).astype(BF16)

    def tangent_norm(offset):
        @blocks(32)
        def _(i):
            s = pl.ds(pl.multiple_of(i * 32, 32), 32)
            o = pl.ds(pl.multiple_of(i * 32 + offset, 32), 32)
            u, v, g = unit[s, :], tmix[s, :], gain[0:1, :]
            w = scale[s, 0:1] * (v - u * jnp.mean(u * v, axis=-1, keepdims=True))
            NT[o, :] = (w * g).astype(BF16)

    tangent_norm(256)

    stage_d(1)
    stage_b(3)
    stage_e(1)
    stage_d(2)
    stage_c(3)
    stage_b(4)
    stage_f(1)

    def take_inner(ch):
        for cc in range(2):
            @pl.loop(0, 3)
            def _(t):
                w = HI[cc, ch * 3 + t].reshape(D, 256)
                cols = pl.ds(pl.multiple_of(cc * 1536 + ch * 768 + t * 256, 256), 256)
                pre = nn(NT[0:256, :], w)
                sigma = jax.nn.sigmoid(pre)
                AA[0:256, cols] = (pre * sigma).astype(BF16)
                sl = swish_slope(pre, sigma)
                slope[:, cols] = sl
                AA[256:512, cols] = (sl * nn(NT[256:512, :], w)).astype(BF16)

    take_inner(0)
    stage_e(2)
    stage_d(3)
    stage_c(4)
    stage_f(2)
    take_inner(1)
    stage_e(3)
    stage_d(4)
    stage_f(3)

    def take_outer(ch):
        @pl.loop(0, 3)
        def _(t):
            w = HO[ch * 3 + t].reshape(FF, 256)
            cols = pl.ds(pl.multiple_of(ch * 768 + t * 256, 256), 256)
            l = (mixed[:, cols] + nn(AA[0:256, :], w)).astype(BF16)
            later[:, cols] = l
            later_t[cols, :] = l.astype(F32).T.astype(BF16)
            tlater[:, cols] = (tmix[:, cols] + nn(AA[256:512, :], w)).astype(BF16)

    take_outer(0)
    stage_e(4)
    stage_f(4)
    take_outer(1)
    op_g32.wait_recv()

    second = jnp.tanh(nn(later[...], policy[...]))
    second_d[...] = 1.0 - second * second
    weighting = precision[...] * (1.0 / TOTAL_ROWS)

    def finish_sweep(it):
        tsecond = second_d[...] * (nn(tlater[...], policy[...]) + nn(later[...], going[...]))
        tf = tfirst[...]
        total_send(1 + it, 0, fold(weighting * (tf * tf + tsecond * tsecond)))
        cs = (second_d[...] * (weighting * tsecond)).astype(BF16)
        cot_second[...] = cs
        cl = nt(cs, policy[...])
        cot_later[...] = cl
        cot_b[...] = cl.astype(BF16)

        @pl.loop(0, 4)
        def _(i):
            a, b = i // 2, i % 2
            acc = jnp.zeros((ROWS, 768), F32)
            for ct in range(6):
                w = HO[ct, a, pl.ds(b * 2, 2)].reshape(768, 256)
                acc = acc + nt(cot_b[:, 256 * ct : 256 * ct + 256], w)
            cols = pl.ds(pl.multiple_of(i * 768, 256), 768)
            cot_pre[:, cols] = (slope[:, cols] * acc).astype(BF16)

        total_step(1 + it, 0)

        @pl.loop(0, 2)
        def _(a):
            acc = jnp.zeros((ROWS, 768), F32)
            for n in range(12):
                w = HI[n // 6, n % 6, a].reshape(768, 256)
                acc = acc + nt(cot_pre[:, 256 * n : 256 * n + 256], w)
            cols = pl.ds(pl.multiple_of(a * 768, 256), 768)
            tmix[:, cols] = acc

        total_step(1 + it, 1)

        @blocks(32)
        def _(i):
            s = pl.ds(pl.multiple_of(i * 32, 32), 32)
            u, g = unit[s, :], gain[0:1, :]
            v = tmix[s, :] * g
            w = scale[s, 0:1] * (v - u * jnp.mean(u * v, axis=-1, keepdims=True))
            cot_b[s, :] = (cot_later[s, :] + w).astype(BF16)

        cf = (first_d[...] * (weighting * tfirst[...] + nt(cot_b[...], embed[...]))).astype(BF16)
        cot_first[...] = cf

    r_base = [fresh(16), fresh(16)]
    gather_base = fresh(13)

    def sum_image(it):
        base = r_base[it]

        @pl.loop(0, 6)
        def _(i):
            s = pl.ds(pl.multiple_of(i * 256, 256), 256)
            v = nn(start_t[s, :], cot_first[...]) + nn(later_t[s, :], cot_second[...])
            IP[it, 0, s, :] = v[:, 0:128]
            IP[it, 1, s, :] = v[:, 128:256]

        op = copy(IP.at[it, 1 - c], RB.at[it], base, partner)
        total_step(1 + it, 2)
        op.wait_recv()
        for a in range(2):
            rows = slice(768 * a, 768 * a + 768)
            ACC[it, a] = (IP[it, c, rows, :] + RB[it, rows, :]).reshape(4, 4, 48, 128)
        todo = []
        for d in (1, 2, 3):
            todo.append(copy(ACC.at[it, 0, :, (y + d) % 4], R1.at[it, 0, d - 1], base + d, axis_dev("y", d)))
            todo.append(copy(ACC.at[it, 1, (z + d) % 4], R1.at[it, 1, d - 1], base + 3 + d, axis_dev("z", d)))
        total = whole(total_step(1 + it, 3))
        for op in todo:
            op.wait_recv()
        T2[it, 0] = ACC[it, 0, :, y] + R1[it, 0, 0] + R1[it, 0, 1] + R1[it, 0, 2]
        T2[it, 1] = ACC[it, 1, z] + R1[it, 1, 0] + R1[it, 1, 1] + R1[it, 1, 2]
        todo = []
        for d in (1, 2, 3):
            todo.append(copy(T2.at[it, 0, (z + d) % 4], R2.at[it, 0, d - 1], base + 6 + d, axis_dev("z", d)))
            todo.append(copy(T2.at[it, 1, (y + d) % 4], R2.at[it, 1, d - 1], base + 9 + d, axis_dev("y", d)))
        for op in todo:
            op.wait_recv()
        T3[it, x, 0] = T2[it, 0, z] + R2[it, 0, 0] + R2[it, 0, 1] + R2[it, 0, 2]
        T3[it, x, 1] = T2[it, 1, y] + R2[it, 1, 0] + R2[it, 1, 1] + R2[it, 1, 2]
        todo = []
        for d in (1, 2, 3):
            todo.append(copy(T3.at[it, x], T3.at[it, x], base + 12 + d, axis_dev("x", d)))
        for op in todo:
            op.wait_recv()
        return total

    finish_sweep(0)
    bend = sum_image(0) + DAMPING * rr
    alpha1 = rr / bend
    image = T3[0, 0] + T3[0, 1] + T3[0, 2] + T3[0, 3]
    residual = g32[...] - alpha1 * (image + DAMPING * g32[...])
    res32[...] = residual
    RG[c, 0, z, y] = residual[0].astype(BF16)
    RG[c, 1, z, y] = residual[1].astype(BF16)
    todo = []
    for d in (1, 2, 3):
        ref = RG.at[c, 0, z, y]
        todo.append(copy(ref, ref, gather_base + d - 1, axis_dev("y", d)))
        ref = RG.at[c, 1, z, y]
        todo.append(copy(ref, ref, gather_base + d + 2, axis_dev("z", d)))
    for op in todo:
        op.wait_recv()
    todo = []
    for d in (1, 2, 3):
        ref = RG.at[c, 0, z]
        todo.append(copy(ref, ref, gather_base + d + 5, axis_dev("z", d)))
        ref = RG.at[c, 1, :, y]
        todo.append(copy(ref, ref, gather_base + d + 8, axis_dev("y", d)))
    for op in todo:
        op.wait_recv()
    op = copy(RG.at[c], RG.at[c], gather_base + 12, partner)
    op.wait_recv()

    tile = jnp.zeros((8, 128), F32)
    for cc in range(2):
        r = RG[cc].astype(F32).reshape(D, 128)
        tile = tile + fold(r * r)
    new = whole(tile)
    beta = new / rr
    tile = jnp.zeros((8, 128), F32)
    for cc in range(2):
        r = RG[cc].astype(F32).reshape(D, 128)
        cols = slice(128 * cc, 128 * cc + 128)
        v = r + beta * going[:, cols].astype(F32)
        tile = tile + fold(v * v)
        going[:, cols] = v.astype(BF16)
    dd = whole(tile)

    tfirst[...] = first_d[...] * nn(states[...], going[...])
    tmix[...] = nn(tfirst[...].astype(BF16), embed[...])
    tangent_norm(256)
    for cc in range(2):
        @pl.loop(0, 6)
        def _(t):
            cols = pl.ds(pl.multiple_of(cc * 1536 + t * 256, 256), 256)
            w = HI[cc, t].reshape(D, 256)
            AA[256:512, cols] = (slope[:, cols] * nn(NT[256:512, :], w)).astype(BF16)

    @pl.loop(0, 6)
    def _(t):
        cols = pl.ds(pl.multiple_of(t * 256, 256), 256)
        w = HO[t].reshape(FF, 256)
        tlater[:, cols] = (tmix[:, cols] + nn(AA[256:512, :], w)).astype(BF16)

    finish_sweep(1)
    bend = sum_image(1) + DAMPING * dd
    alpha2 = new / bend
    image = T3[1, 0, hi] + T3[1, 1, hi] + T3[1, 2, hi] + T3[1, 3, hi]
    g = g32[hi]
    res = res32[hi]
    direction = res + beta * g
    new_update = alpha1 * g + alpha2 * direction
    new_residual = res - alpha2 * (image + DAMPING * direction)
    out_near[0] = jnp.where(c == 0, new_update[24:48], new_update[0:24])
    out_near[1] = jnp.where(c == 0, new_residual[24:48], new_residual[0:24])
    op = copy(out_near, out_far, fresh(), partner)
    mine_u = jnp.where(c == 0, new_update[0:24], new_update[24:48])
    mine_r = jnp.where(c == 0, new_residual[0:24], new_residual[24:48])
    op.wait_recv()
    for mine, k, out in ((mine_u, 0, out_update), (mine_r, 1, out_residual)):
        other = out_far[k]
        out[:, 0:128] = jnp.where(c == 0, mine, other)
        out[:, 128:256] = jnp.where(c == 0, other, mine)
    for op in pending:
        op.wait_send()


def body(states, policy, action_embed, norm_gain, hidden_in, hidden_out, precision, gradient):
    wide = policy.astype(F32)
    gains = jnp.broadcast_to(norm_gain.astype(F32)[:, None], (norm_gain.shape[0], 128))
    pack = jnp.concatenate(
        [wide[:, 0:128], gradient[:, 0:128], gains, wide[:, 128:256], gradient[:, 128:256], gains], axis=1
    )
    embed = action_embed.reshape(4, 4, 3, 128).transpose(2, 1, 0, 3).reshape(48, 128)
    vmem = pl.BlockSpec(memory_space=pltpu.VMEM)
    shapes = [
        ((2, 3, 2, 4, 4, 64, 128), BF16),
        ((2, 6, 2, 4, 4, 48, 256), BF16),
        ((6, 2, 4, 4, 2, 48, 256), BF16),
        ((24, 384), F32),
        ((24, 3072), F32),
        ((24, 1536), F32),
        ((D, ACT), BF16),
        ((ACT, D), BF16),
        ((8, D), F32),
        ((2, 4, 4, 48, 128), BF16),
        ((D, ACT), BF16),
        ((D, ROWS), BF16),
        ((D, ROWS), BF16),
        ((512, D), BF16),
        ((512, FF), BF16),
        ((ROWS, FF), F32),
        ((ROWS, D), F32),
        ((ROWS, D), F32),
        ((ROWS, 128), F32),
        ((ROWS, D), F32),
        ((ROWS, ACT), F32),
        ((ROWS, ACT), F32),
        ((ROWS, ACT), F32),
        ((ROWS, D), BF16),
        ((ROWS, D), BF16),
        ((ROWS, D), F32),
        ((ROWS, D), BF16),
        ((ROWS, FF), BF16),
        ((ROWS, ACT), BF16),
        ((ROWS, ACT), BF16),
        ((2, 2, D, 128), F32),
        ((2, D, 128), F32),
        ((2, 2, 4, 4, 48, 128), F32),
        ((2, 2, 3, 4, 48, 128), F32),
        ((2, 2, 4, 48, 128), F32),
        ((2, 2, 3, 48, 128), F32),
        ((2, 4, 2, 48, 128), F32),
        ((3, 4, 4, 8, 128), F32),
        ((2, 48, 128), F32),
        ((2, 48, 128), F32),
        ((2, 2, 4, 4, 48, 128), BF16),
        ((2, 24, 128), F32),
        ((2, 24, 128), F32),
    ]
    n_sems = N_ITEM * ITEM_SEMS + OTHER_SEMS
    out = jax.ShapeDtypeStruct(gradient.shape, F32)
    return pl.pallas_call(
        kernel,
        out_shape=(out, out),
        in_specs=[vmem] * 6,
        out_specs=(vmem, vmem),
        scratch_shapes=[pltpu.VMEM(s, t) for s, t in shapes]
        + [pltpu.SemaphoreType.DMA((n_sems,)), pltpu.SemaphoreType.DMA((n_sems,))],
        compiler_params=pltpu.CompilerParams(
            collective_id=0, has_side_effects=True, vmem_limit_bytes=62 * 2**20
        ),
        name="natural_step",
    )(states, pack, embed, hidden_in, hidden_out, precision.reshape(1, ACT))


def solution(mesh):
    placed = (
        P(("dp", "fsdp"), None),
        P("fsdp", None),
        P("fsdp", None),
        P("fsdp"),
        P("fsdp", None),
        P("fsdp", None),
        P(),
        P("fsdp", None),
    )
    return jax.shard_map(
        body,
        mesh=mesh,
        in_specs=placed,
        out_specs=(P("fsdp", None), P("fsdp", None)),
        check_vma=False,
    )
```

```python
import functools

import jax
import jax.numpy as jnp
from jax import lax
from jax.experimental import pallas as pl
from jax.experimental.pallas import tpu as pltpu
from jax.sharding import PartitionSpec as P

MESH = pl.DeviceIdType.MESH
F32 = jnp.float32
BF16 = jnp.bfloat16
EPS = 1e-05
DAMPING = 0.1
ALL = slice(None)

ROWS = 256
D = 1536
FF = 3072
ACT = 256
TOTAL_ROWS = 32768
N_ITEM = 5
ITEM_SEMS = 41
OTHER_SEMS = 2 + 1 + 6 + 30 + 2 * 17 + 20 + 1


def nn(left, right):
    return jnp.dot(left, right, preferred_element_type=F32)


def nt(left, right):
    return lax.dot_general(left, right, (((1,), (1,)), ((), ())), preferred_element_type=F32)


def swish_slope(pre, sigma):
    return sigma * (1.0 + pre * (1.0 - sigma))


def kernel(
    states,
    policy_in,
    embed_in,
    gain_in,
    inner_in,
    outer_in,
    precision,
    gradient,
    out_update,
    out_residual,
    S,
    HI,
    HO,
    pack,
    pack_far,
    embed_near,
    inner_wide,
    inner_far,
    policy,
    embed,
    gain,
    gain_tall,
    going,
    start_t,
    later_t,
    NT,
    AA,
    slope,
    mixed,
    unit,
    scale,
    tmix,
    first_d,
    second_d,
    tfirst,
    later,
    tlater,
    cot_later,
    cot_b,
    cot_pre,
    cot_first,
    cot_second,
    IP,
    IPW,
    RB,
    ACC,
    ACCW,
    R1,
    T2,
    T2W,
    R2,
    T3,
    SC,
    g32,
    res32,
    RG,
    res_near,
    res_far,
    send_sem,
    recv_sem,
):
    lo = lax.axis_index("dp")
    f = lax.axis_index("fsdp")
    c = f % 2
    y = (f // 2) % 4
    z = (f // 8) % 4
    hi = f // 32
    x = hi * 2 + lo

    def dev(dx=None, dy=0, dz=0, core=None):
        xx = x if dx is None else (x + dx) % 4
        yy, zz = (y + dy) % 4, (z + dz) % 4
        cc = c if core is None else core
        return (xx % 2, (((xx // 2) * 4 + zz) * 4 + yy) * 2 + cc)

    def axis_dev(axis, d):
        return dev(**{"d" + axis: d})

    opp = ((3 - x) % 2, ((((3 - x) // 2) * 4 + z) * 4 + y) * 2 + c)
    partner = dev(core=1 - c)

    pending = []
    counter = [N_ITEM * ITEM_SEMS]

    def copy(src, dst, sem, to):
        op = pltpu.make_async_remote_copy(
            src_ref=src,
            dst_ref=dst,
            send_sem=send_sem.at[sem],
            recv_sem=recv_sem.at[sem],
            device_id=to,
            device_id_type=MESH,
        )
        op.start()
        pending.append(op)
        return op

    def fresh(n=1):
        base = counter[0]
        counter[0] += n
        return base

    barrier = pltpu.get_barrier_semaphore()
    peers = [partner] + [axis_dev(a, d) for a in ("x", "y", "z") for d in (1, 2, 3)]
    for peer in peers:
        pl.semaphore_signal(barrier, inc=1, device_id=peer, device_id_type=MESH)
    inner_wide[...] = inner_in[...].astype(F32)
    diagonal = lax.broadcasted_iota(jnp.int32, (24, 24), 0) == lax.broadcasted_iota(jnp.int32, (24, 24), 1)
    gain_row = jnp.broadcast_to(gain_in[...].astype(F32), (24, 24))
    gain_column = jnp.sum(jnp.where(diagonal, gain_row, 0.0), axis=1, keepdims=True)
    for core in range(2):
        pack[:, 384 * core : 384 * core + 128] = policy_in[:, 128 * core : 128 * core + 128].astype(F32)
        pack[:, 384 * core + 128 : 384 * core + 256] = gradient[:, 128 * core : 128 * core + 128]
        pack[:, 384 * core + 256 : 384 * core + 384] = jnp.broadcast_to(gain_column, (24, 128))
    wide = embed_in[...].astype(F32)
    for q in range(4):
        for s in range(3):
            column = 384 * q + 128 * s
            embed_near[16 * s + 4 * q : 16 * s + 4 * q + 4, :] = wide[:, column : column + 128]
    pl.semaphore_wait(barrier, len(peers))

    half = pl.ds(pl.multiple_of((1 - c) * 1536, 128), 1536)
    op_inner = copy(inner_wide.at[:, half], inner_far, fresh(), partner)
    half = pl.ds(pl.multiple_of((1 - c) * 384, 128), 384)
    op_pack = copy(pack.at[:, half], pack_far, fresh(), partner)

    def part(item, t, h, zz, yy, cut):
        if item == 0:
            rows = pl.ds(pl.multiple_of(lo * 32, 32), 32) if cut == 0 else ALL
            if cut == 1:
                rows = pl.ds(pl.multiple_of((1 - lo) * 32, 32), 32)
            return S.at[c, t, h, zz, yy, rows, :]
        cols = ALL
        if cut == 0:
            cols = pl.ds(pl.multiple_of(lo * 128, 128), 128)
        if cut == 1:
            cols = pl.ds(pl.multiple_of((1 - lo) * 128, 128), 128)
        if item < 3:
            return HI.at[c, (item - 1) * 3 + t, h, zz, yy, :, cols]
        return HO.at[(item - 3) * 3 + t, h, zz, yy, c, :, cols]

    one = lambda i: pl.ds(i, 1)
    ops = {}

    def send(item, key, sem, t, h, zz, yy, cut, to):
        ref = part(item, t, h, zz, yy, cut)
        ops[(item, key)] = copy(ref, ref, item * ITEM_SEMS + sem, to)

    def wait(item, *keys):
        for key in keys:
            ops[(item, key)].wait_recv()

    def stage_a(k):
        send(k, "0x", 0, 0, one(hi), one(z), one(y), None, opp)
        for d in (1, 2, 3):
            send(k, "1y%d" % d, 8 + d, 1, one(hi), one(z), one(y), 0, axis_dev("y", d))
            send(k, "2z%d" % d, 18 + d, 2, one(hi), one(z), one(y), None, axis_dev("z", d))

    def stage_b(k):
        wait(k, "0x")
        for d in (1, 2, 3):
            send(k, "0y%d" % d, d, 0, ALL, one(z), one(y), None, axis_dev("y", d))
        wait(k, "1y1", "1y2", "1y3")
        for d in (1, 2, 3):
            send(k, "1z%d" % d, 11 + d, 1, one(hi), one(z), ALL, 0, axis_dev("z", d))
        wait(k, "2z1", "2z2", "2z3")
        send(k, "2x", 22, 2, one(hi), ALL, one(y), None, opp)

    def hand(k, key, sem, t, h, zz, yy, cut):
        send(k, key, 26 + sem, t, h, zz, yy, cut, partner)

    low, high = pl.ds(0, 2), pl.ds(2, 2)
    h0, h1 = pl.ds(0, 1), pl.ds(1, 1)
    zb, zf, zo = (z + 3) % 4, (z + 1) % 4, (z + 2) % 4
    yb, yf, yo = (y + 3) % 4, (y + 1) % 4, (y + 2) % 4

    def x_part(k, d):
        xx = (x + d) % 4
        h = one(xx // 2)
        other = xx % 2
        if k == 0:
            return h, pl.ds(pl.multiple_of(other * 32, 32), 32), ALL
        return h, ALL, pl.ds(pl.multiple_of(other * 128, 128), 128)

    def x_ref(k, d, zz):
        h, rows, cols = x_part(k, d)
        if k == 0:
            return S.at[c, 1, h, zz, :, rows, :]
        if k < 3:
            return HI.at[c, (k - 1) * 3 + 1, h, zz, :, :, cols]
        return HO.at[(k - 3) * 3 + 1, h, zz, :, c, :, cols]

    def x_send(k, key, sem, d, zz, to):
        ref = x_ref(k, d, zz)
        ops[(k, key)] = copy(ref, ref, k * ITEM_SEMS + sem, to)

    fine_base = fresh(6)

    def stage_c(k):
        fine = k == N_ITEM - 1
        f0, b0, fl, bl = (h0, h1, low, high) if fine else (ALL, ALL, ALL, ALL)
        wait(k, "0y1", "0y2", "0y3")
        send(k, "0f", 4, 0, f0, one(z), ALL, None, axis_dev("z", 1))
        send(k, "0b", 5, 0, b0, one(z), ALL, None, axis_dev("z", 3))
        wait(k, "1z1", "1z2", "1z3")
        x_send(k, "1f", 15, 0, fl, axis_dev("x", 1))
        x_send(k, "1b", 16, 0, bl, axis_dev("x", 3))
        wait(k, "2x")
        send(k, "2f", 23, 2, f0, ALL, one(y), None, axis_dev("y", 1))
        send(k, "2b", 24, 2, b0, ALL, one(y), None, axis_dev("y", 3))
        if fine:
            sem = fine_base - k * ITEM_SEMS
            send(k, "0F", sem, 0, h1, one(z), ALL, None, axis_dev("z", 1))
            send(k, "0B", sem + 1, 0, h0, one(z), ALL, None, axis_dev("z", 3))
            x_send(k, "1F", sem + 2, 0, high, axis_dev("x", 1))
            x_send(k, "1B", sem + 3, 0, low, axis_dev("x", 3))
            send(k, "2F", sem + 4, 2, h1, ALL, one(y), None, axis_dev("y", 1))
            send(k, "2B", sem + 5, 2, h0, ALL, one(y), None, axis_dev("y", 3))
        hand(k, "0p0", 0, 0, ALL, one(z), ALL, None)
        x_send(k, "1p0", 26 + 5, 0, ALL, partner)
        hand(k, "2p0", 10, 2, ALL, ALL, one(y), None)

    def stage_d(k):
        fine = k == N_ITEM - 1
        wait(k, "0f")
        send(k, "0ff", 6, 0, h0, one(zb), ALL, None, axis_dev("z", 1))
        wait(k, "0b")
        send(k, "0bb", 7, 0, h1, one(zf), ALL, None, axis_dev("z", 3))
        wait(k, "1f")
        x_send(k, "1ff", 17, 3, low, axis_dev("x", 1))
        wait(k, "1b")
        x_send(k, "1bb", 18, 1, high, axis_dev("x", 3))
        wait(k, "2f")
        send(k, "2ff", 25, 2, h0, ALL, one(yb), None, axis_dev("y", 1))
        wait(k, "2b")
        send(k, "2bb", 8, 2, h1, ALL, one(yf), None, axis_dev("y", 3))
        if fine:
            wait(k, "0F", "0B")
        hand(k, "0p1", 1, 0, ALL, one(zb), ALL, None)
        hand(k, "0p2", 2, 0, ALL, one(zf), ALL, None)
        if fine:
            wait(k, "1F", "1B")
        x_send(k, "1p1", 26 + 6, 3, ALL, partner)
        x_send(k, "1p2", 26 + 7, 1, ALL, partner)
        if fine:
            wait(k, "2F", "2B")
        hand(k, "2p1", 11, 2, ALL, ALL, one(yb), None)
        hand(k, "2p2", 12, 2, ALL, ALL, one(yf), None)

    def stage_e(k):
        wait(k, "0ff")
        hand(k, "0p3", 3, 0, h0, one(zo), ALL, None)
        wait(k, "0bb")
        hand(k, "0p4", 4, 0, h1, one(zo), ALL, None)
        wait(k, "1ff")
        x_send(k, "1p3", 26 + 8, 2, low, partner)
        wait(k, "1bb")
        x_send(k, "1p4", 26 + 9, 2, high, partner)
        wait(k, "2ff")
        hand(k, "2p3", 13, 2, h0, ALL, one(yo), None)
        wait(k, "2bb")
        hand(k, "2p4", 14, 2, h1, ALL, one(yo), None)

    def stage_f(k):
        wait(k, *["%dp%d" % (t, i) for t in range(3) for i in range(5)])

    scalar_ops = {}
    scalar_base = fresh(30)
    places = (("core", c, 2), ("y", y, 4), ("z", z, 4), ("x", x, 4))

    def total_send(which, phase, value):
        axis, own, n = places[phase]
        SC[which, phase, own] = value
        ref = SC.at[which, phase, own]
        base = scalar_base + 10 * which + (0, 1, 4, 7)[phase]
        todo = []
        for d in range(1, n):
            to = partner if axis == "core" else axis_dev(axis, d)
            todo.append(copy(ref, ref, base + d - 1, to))
        scalar_ops[(which, phase)] = todo

    def total_take(which, phase):
        for op in scalar_ops[(which, phase)]:
            op.wait_recv()
        n = places[phase][2]
        value = SC[which, phase, 0]
        for i in range(1, n):
            value = value + SC[which, phase, i]
        return value

    def total_step(which, phase):
        value = total_take(which, phase)
        if phase < 3:
            total_send(which, phase + 1, value)
        return value

    def fold(value):
        value = value.reshape(-1, 8, value.shape[-1]).sum(axis=0)
        tile = value[:, 0:128]
        for i in range(1, value.shape[-1] // 128):
            tile = tile + value[:, 128 * i : 128 * i + 128]
        return tile

    def whole(tile):
        return jnp.sum(jnp.sum(tile, axis=1, keepdims=True), axis=0, keepdims=True)

    weigh_rows = outer_in
    for ct in range(6):
        if ct % 3 == 1:
            left = weigh_rows[:, 256 * ct : 256 * ct + 128]
            right = weigh_rows[:, 256 * ct + 128 : 256 * ct + 256]
            HO[ct, hi, z, y, c, :, pl.ds(pl.multiple_of(lo * 128, 128), 128)] = jnp.where(lo == 0, left, right)
        else:
            HO[ct, hi, z, y, c] = weigh_rows[:, 256 * ct : 256 * ct + 256]

    stage_a(3)
    stage_a(4)
    near = pack[:, pl.ds(pl.multiple_of(c * 384, 128), 384)]
    g_own = gradient[...]
    total_send(0, 0, fold(g_own * g_own))
    op_pack.wait_recv()
    far = pack_far[...]
    pair = jnp.concatenate([jnp.where(c == 0, near, far), jnp.where(c == 0, far, near)], axis=0)
    g32[hi] = pair[:, 128:256]
    gains = pair[:, 256:384].astype(BF16)
    S[c, 0, hi, z, y, 0:48] = pair[:, 0:128].astype(BF16)
    S[c, 0, hi, z, y, 48:64] = gains[0:16]
    gb = pair[:, 128:256]
    both = jnp.concatenate([gb, pair[16:32, 256:384]], axis=0)
    S[c, 1, hi, z, y, pl.ds(pl.multiple_of(lo * 32, 32), 32)] = jnp.where(lo == 0, both[0:32], both[32:64]).astype(BF16)
    S[c, 2, hi, z, y, 0:48] = embed_near[...].astype(BF16)
    S[c, 2, hi, z, y, 48:64] = gains[32:48]
    stage_a(0)
    op_g32 = copy(g32.at[one(hi)], g32.at[one(hi)], fresh(), opp)

    op_inner.wait_recv()
    near = inner_wide[:, pl.ds(pl.multiple_of(c * 1536, 128), 1536)]
    far = inner_far[...]
    pair = jnp.concatenate([jnp.where(c == 0, near, far), jnp.where(c == 0, far, near)], axis=0)
    for ct in range(6):
        if ct % 3 == 1:
            left = pair[:, 256 * ct : 256 * ct + 128]
            right = pair[:, 256 * ct + 128 : 256 * ct + 256]
            HI[c, ct, hi, z, y, :, pl.ds(pl.multiple_of(lo * 128, 128), 128)] = jnp.where(lo == 0, left, right).astype(BF16)
        else:
            HI[c, ct, hi, z, y] = pair[:, 256 * ct : 256 * ct + 256].astype(BF16)
    stage_a(1)
    stage_a(2)
    stage_b(3)
    stage_b(0)
    stage_b(1)
    stage_c(0)
    total_step(0, 0)
    stage_b(2)
    stage_c(1)
    stage_b(4)
    total_step(0, 1)
    stage_d(0)

    @pl.loop(0, 6)
    def _(i):
        s = pl.ds(pl.multiple_of(i * 256, 256), 256)
        start_t[s, :] = states[:, s].astype(F32).T.astype(BF16)

    stage_c(2)
    stage_e(0)
    total_step(0, 2)
    stage_f(0)
    rr = whole(total_step(0, 3)) * 0.5

    for t in range(3):
        for a in range(2):
            for b in range(4):
                gain_tall[a, b, :, 16 * t : 16 * t + 16] = S[0, t, a, b, :, 48:64]
    pick = (lax.broadcasted_iota(jnp.int32, (16, 128), 1) == 0).astype(BF16)
    gain[...] = nt(pick, gain_tall[...].reshape(D, 128))[0:8]
    for cc in range(2):
        for a in range(2):
            policy[768 * a : 768 * a + 768, 128 * cc : 128 * cc + 128] = S[cc, 0, a, :, :, 0:48].reshape(768, 128)
            going[768 * a : 768 * a + 768, 128 * cc : 128 * cc + 128] = S[cc, 1, a, :, :, 0:48].reshape(768, 128)
    for q in range(4):
        total = jnp.zeros((ACT, 384), F32)
        for cc in range(2):
            out_row = lax.broadcasted_iota(jnp.int32, (ACT, 512), 0)
            in_row = lax.broadcasted_iota(jnp.int32, (ACT, 512), 1)
            want = (lax.div(out_row, 8) * 16) + 4 * q + lax.rem(out_row, 4)
            mine = lax.rem(lax.div(out_row, 4), 2) == cc
            choose = jnp.where(mine & (in_row == want), 1.0, 0.0).astype(BF16)
            block = jnp.concatenate(
                [S[cc, 2, :, :, :, 16 * s : 16 * s + 16].reshape(512, 128) for s in range(3)], axis=1
            )
            total = total + nn(choose, block)
        embed[:, 384 * q : 384 * q + 384] = total.astype(BF16)

    def blocks(n):
        return pl.loop(0, ROWS // n)

    stage_d(1)
    stage_c(3)

    first = jnp.tanh(nn(states[...], policy[...]))
    first_d[...] = 1.0 - first * first
    mixed[...] = nn(first.astype(BF16), embed[...])
    tfirst[...] = first_d[...] * nn(states[...], going[...])
    tmix[...] = nn(tfirst[...].astype(BF16), embed[...])

    @blocks(32)
    def _(i):
        s = pl.ds(pl.multiple_of(i * 32, 32), 32)
        m = states[s, :].astype(F32) + mixed[s, :]
        mixed[s, :] = m
        r = lax.rsqrt(jnp.mean(m * m, axis=-1, keepdims=True) + EPS)
        scale[s, :] = jnp.broadcast_to(r, (32, 128))
        u = m * r
        unit[s, :] = u
        g = gain[0:1, :]
        NT[s, :] = (u * g).astype(BF16)

    def tangent_norm(offset):
        @blocks(32)
        def _(i):
            s = pl.ds(pl.multiple_of(i * 32, 32), 32)
            o = pl.ds(pl.multiple_of(i * 32 + offset, 32), 32)
            u, v, g = unit[s, :], tmix[s, :], gain[0:1, :]
            w = scale[s, 0:1] * (v - u * jnp.mean(u * v, axis=-1, keepdims=True))
            NT[o, :] = (w * g).astype(BF16)

    tangent_norm(256)

    stage_e(1)
    stage_d(2)
    stage_c(4)
    stage_f(1)

    def take_inner(ch):
        for cc in range(2):
            @pl.loop(0, 3, unroll=True)
            def _(t):
                w = HI[cc, ch * 3 + t].reshape(D, 256)
                cols = pl.ds(pl.multiple_of(cc * 1536 + ch * 768 + t * 256, 256), 256)
                pre = nn(NT[0:256, :], w)
                sigma = jax.nn.sigmoid(pre)
                AA[0:256, cols] = (pre * sigma).astype(BF16)
                sl = swish_slope(pre, sigma)
                slope[:, cols] = sl
                AA[256:512, cols] = (sl * nn(NT[256:512, :], w)).astype(BF16)

    take_inner(0)
    stage_e(2)
    stage_d(3)
    stage_f(2)
    take_inner(1)
    stage_e(3)
    stage_d(4)
    stage_f(3)

    def take_outer(ch):
        @pl.loop(0, 3, unroll=True)
        def _(t):
            w = HO[ch * 3 + t].reshape(FF, 256)
            cols = pl.ds(pl.multiple_of(ch * 768 + t * 256, 256), 256)
            l = (mixed[:, cols] + nn(AA[0:256, :], w)).astype(BF16)
            later[:, cols] = l
            later_t[cols, :] = l.astype(F32).T.astype(BF16)
            tlater[:, cols] = (tmix[:, cols] + nn(AA[256:512, :], w)).astype(BF16)

    take_outer(0)
    stage_e(4)
    stage_f(4)
    take_outer(1)
    op_g32.wait_recv()

    second = jnp.tanh(nn(later[...], policy[...]))
    second_d[...] = 1.0 - second * second
    weighting = precision[...] * (1.0 / TOTAL_ROWS)

    def finish_sweep(it):
        tsecond = second_d[...] * (nn(tlater[...], policy[...]) + nn(later[...], going[...]))
        tf = tfirst[...]
        total_send(1 + it, 0, fold(weighting * (tf * tf + tsecond * tsecond)))
        cs = (second_d[...] * (weighting * tsecond)).astype(BF16)
        cot_second[...] = cs
        cl = nt(cs, policy[...])
        cot_later[...] = cl
        cot_b[...] = cl.astype(BF16)

        @pl.loop(0, 4, unroll=True)
        def _(i):
            a, b = i // 2, i % 2
            acc = jnp.zeros((ROWS, 768), F32)
            for ct in range(6):
                w = HO[ct, a, pl.ds(b * 2, 2)].reshape(768, 256)
                acc = acc + nt(cot_b[:, 256 * ct : 256 * ct + 256], w)
            cols = pl.ds(pl.multiple_of(i * 768, 256), 768)
            cot_pre[:, cols] = (slope[:, cols] * acc).astype(BF16)

        total_step(1 + it, 0)

        @pl.loop(0, 2, unroll=True)
        def _(a):
            acc = jnp.zeros((ROWS, 768), F32)
            for n in range(12):
                w = HI[n // 6, n % 6, a].reshape(768, 256)
                acc = acc + nt(cot_pre[:, 256 * n : 256 * n + 256], w)
            cols = pl.ds(pl.multiple_of(a * 768, 256), 768)
            tmix[:, cols] = acc

        total_step(1 + it, 1)

        @blocks(32)
        def _(i):
            s = pl.ds(pl.multiple_of(i * 32, 32), 32)
            u, g = unit[s, :], gain[0:1, :]
            v = tmix[s, :] * g
            w = scale[s, 0:1] * (v - u * jnp.mean(u * v, axis=-1, keepdims=True))
            cot_b[s, :] = (cot_later[s, :] + w).astype(BF16)

        cf = (first_d[...] * (weighting * tfirst[...] + nt(cot_b[...], embed[...]))).astype(BF16)
        cot_first[...] = cf

    r_base = [fresh(17), fresh(17)]
    gather_base = fresh(20)

    def halves(v, it):
        if it == 0:
            low_half, high_half = v[:, 0:128], v[:, 128:256]
            low_half, high_half = low_half.reshape(16, 48, 128), high_half.reshape(16, 48, 128)
        else:
            v = v.reshape(16, 48, 256)
            low_half = jnp.concatenate([v[:, 0:24, 0:128], v[:, 0:24, 128:256]], axis=1)
            high_half = jnp.concatenate([v[:, 24:48, 0:128], v[:, 24:48, 128:256]], axis=1)
        return jnp.where(c == 0, low_half, high_half), jnp.where(c == 0, high_half, low_half)

    def sum_image(it):
        base = r_base[it]
        swap = []
        for a in range(2):
            rows = slice(768 * a, 768 * a + 768)
            v = nn(start_t[rows, :], cot_first[...]) + nn(later_t[rows, :], cot_second[...])
            keep, give = halves(v, it)
            IPW[it, a] = give.reshape(4, 4, 48, 128).astype(BF16)
            swap.append(copy(IPW.at[it, a], RB.at[it, a], base + a, partner))
            IP[it, a] = keep.reshape(4, 4, 48, 128)
        total_step(1 + it, 2)
        todo = []
        for a in range(2):
            swap[a].wait_recv()
            v = IP[it, a] + RB[it, a].astype(F32)
            ACC[it, a] = v
            ACCW[it, a] = v.astype(BF16)
            for d in (2, 1, 3):
                if a == 0:
                    todo.append(
                        copy(ACCW.at[it, 0, :, (y + d) % 4], R1.at[it, 0, d - 1], base + 1 + d, axis_dev("y", d))
                    )
                else:
                    todo.append(copy(ACCW.at[it, 1, (z + d) % 4], R1.at[it, 1, d - 1], base + 4 + d, axis_dev("z", d)))
        total = whole(total_step(1 + it, 3))
        second_todo = []
        for a in range(2):
            for op in todo[3 * a : 3 * a + 3]:
                op.wait_recv()
            v = ACC[it, 0, :, y] if a == 0 else ACC[it, 1, z]
            for d in range(3):
                v = v + R1[it, a, d].astype(F32)
            T2[it, a] = v
            T2W[it, a] = v.astype(BF16)
            for d in (2, 1, 3):
                axis, own = ("z", z) if a == 0 else ("y", y)
                second_todo.append(
                    copy(T2W.at[it, a, (own + d) % 4], R2.at[it, a, d - 1], base + 7 + 3 * a + d, axis_dev(axis, d))
                )
        for a in range(2):
            for op in second_todo[3 * a : 3 * a + 3]:
                op.wait_recv()
            v = T2[it, a, z if a == 0 else y]
            for d in range(3):
                v = v + R2[it, a, d].astype(F32)
            T3[it, x, a] = v.astype(BF16)
        todo = []
        for d in (2, 1, 3):
            todo.append(copy(T3.at[it, x], T3.at[it, x], base + 13 + d, axis_dev("x", d)))
        for op in todo:
            op.wait_recv()
        return total

    def summed(it, h):
        v = T3[it, 0, h].astype(F32)
        for i in range(1, 4):
            v = v + T3[it, i, h].astype(F32)
        return v

    finish_sweep(0)
    bend = sum_image(0) + DAMPING * rr
    alpha1 = rr / bend
    for a in range(2):
        g = g32[a]
        residual = g - alpha1 * (summed(0, a) + DAMPING * g)
        res32[a] = residual
        RG[c, a, z, y] = residual.astype(BF16)
    todo = []
    for d in (2, 1, 3):
        ref = RG.at[c, 0, z, y]
        todo.append((d, copy(ref, ref, gather_base + d - 1, axis_dev("y", d))))
        ref = RG.at[c, 1, z, y]
        todo.append((d, copy(ref, ref, gather_base + d + 2, axis_dev("z", d))))
    for d, op in todo:
        op.wait_recv()
    last = []
    for d in (2, 1, 3):
        ref = RG.at[c, 0, z]
        last.append((0, d, copy(ref, ref, gather_base + d + 5, axis_dev("z", d))))
        ref = RG.at[c, 1, :, y]
        last.append((1, d, copy(ref, ref, gather_base + d + 8, axis_dev("y", d))))
    swap = [
        copy(RG.at[c, 0, z], RG.at[c, 0, z], gather_base + 12, partner),
        copy(RG.at[c, 1, :, y], RG.at[c, 1, :, y], gather_base + 13, partner),
    ]
    mine = res32[hi]
    res_near[...] = jnp.where(c == 0, mine[24:48], mine[0:24])
    op_res = copy(res_near, res_far, fresh(), partner)
    for n, (a, d, op) in enumerate(last[2:] + last[:2]):
        op.wait_recv()
        ref = RG.at[c, 0, (z - d + 4) % 4] if a == 0 else RG.at[c, 1, :, (y - d + 4) % 4]
        swap.append(copy(ref, ref, gather_base + 14 + n, partner))
    for op in swap:
        op.wait_recv()

    tile = jnp.zeros((8, 128), F32)
    for cc in range(2):
        r = RG[cc].astype(F32).reshape(D, 128)
        tile = tile + fold(r * r)
    new = whole(tile)
    beta = new / rr
    tile = jnp.zeros((8, 128), F32)
    for cc in range(2):
        r = RG[cc].astype(F32).reshape(D, 128)
        cols = slice(128 * cc, 128 * cc + 128)
        v = r + beta * going[:, cols].astype(F32)
        tile = tile + fold(v * v)
        going[:, cols] = v.astype(BF16)
    dd = whole(tile)

    tfirst[...] = first_d[...] * nn(states[...], going[...])
    tmix[...] = nn(tfirst[...].astype(BF16), embed[...])
    tangent_norm(256)
    for cc in range(2):
        @pl.loop(0, 6, unroll=True)
        def _(t):
            cols = pl.ds(pl.multiple_of(cc * 1536 + t * 256, 256), 256)
            w = HI[cc, t].reshape(D, 256)
            AA[256:512, cols] = (slope[:, cols] * nn(NT[256:512, :], w)).astype(BF16)

    @pl.loop(0, 6, unroll=True)
    def _(t):
        cols = pl.ds(pl.multiple_of(t * 256, 256), 256)
        w = HO[t].reshape(FF, 256)
        tlater[:, cols] = (tmix[:, cols] + nn(AA[256:512, :], w)).astype(BF16)

    finish_sweep(1)
    bend = sum_image(1) + DAMPING * dd
    alpha2 = new / bend
    image = summed(1, hi)
    image = jnp.concatenate([image[0:24], image[24:48]], axis=1)
    g = gradient[...]
    op_res.wait_recv()
    mine = res32[hi]
    mine = jnp.where(c == 0, mine[0:24], mine[24:48])
    other = res_far[...]
    res = jnp.concatenate([jnp.where(c == 0, mine, other), jnp.where(c == 0, other, mine)], axis=1)
    direction = res + beta * g
    out_update[...] = alpha1 * g + alpha2 * direction
    out_residual[...] = res - alpha2 * (image + DAMPING * direction)
    for op in pending:
        op.wait_send()


def body(states, policy, action_embed, norm_gain, hidden_in, hidden_out, precision, gradient):
    vmem = pl.BlockSpec(memory_space=pltpu.VMEM)
    shapes = [
        ((2, 3, 2, 4, 4, 64, 128), BF16),
        ((2, 6, 2, 4, 4, 48, 256), BF16),
        ((6, 2, 4, 4, 2, 48, 256), BF16),
        ((24, 768), F32),
        ((24, 384), F32),
        ((48, 128), F32),
        ((24, 3072), F32),
        ((24, 1536), F32),
        ((D, ACT), BF16),
        ((ACT, D), BF16),
        ((8, D), F32),
        ((2, 4, 4, 48, 128), BF16),
        ((D, ACT), BF16),
        ((D, ROWS), BF16),
        ((D, ROWS), BF16),
        ((512, D), BF16),
        ((512, FF), BF16),
        ((ROWS, FF), F32),
        ((ROWS, D), F32),
        ((ROWS, D), F32),
        ((ROWS, 128), F32),
        ((ROWS, D), F32),
        ((ROWS, ACT), F32),
        ((ROWS, ACT), F32),
        ((ROWS, ACT), F32),
        ((ROWS, D), BF16),
        ((ROWS, D), BF16),
        ((ROWS, D), F32),
        ((ROWS, D), BF16),
        ((ROWS, FF), BF16),
        ((ROWS, ACT), BF16),
        ((ROWS, ACT), BF16),
        ((2, 2, 4, 4, 48, 128), F32),
        ((2, 2, 4, 4, 48, 128), BF16),
        ((2, 2, 4, 4, 48, 128), BF16),
        ((2, 2, 4, 4, 48, 128), F32),
        ((2, 2, 4, 4, 48, 128), BF16),
        ((2, 2, 3, 4, 48, 128), BF16),
        ((2, 2, 4, 48, 128), F32),
        ((2, 2, 4, 48, 128), BF16),
        ((2, 2, 3, 48, 128), BF16),
        ((2, 4, 2, 48, 128), BF16),
        ((3, 4, 4, 8, 128), F32),
        ((2, 48, 128), F32),
        ((2, 48, 128), F32),
        ((2, 2, 4, 4, 48, 128), BF16),
        ((24, 128), F32),
        ((24, 128), F32),
    ]
    n_sems = N_ITEM * ITEM_SEMS + OTHER_SEMS
    out = jax.ShapeDtypeStruct(gradient.shape, F32)
    return pl.pallas_call(
        kernel,
        out_shape=(out, out),
        in_specs=[vmem] * 8,
        out_specs=(vmem, vmem),
        scratch_shapes=[pltpu.VMEM(s, t) for s, t in shapes]
        + [pltpu.SemaphoreType.DMA((n_sems,)), pltpu.SemaphoreType.DMA((n_sems,))],
        compiler_params=pltpu.CompilerParams(
            collective_id=0, has_side_effects=True, vmem_limit_bytes=62 * 2**20
        ),
        name="natural_step",
    )(
        states,
        policy,
        action_embed,
        norm_gain.reshape(1, -1),
        hidden_in,
        hidden_out,
        precision.reshape(1, ACT),
        gradient,
    )


def solution(mesh):
    placed = (
        P(("dp", "fsdp"), None),
        P("fsdp", None),
        P("fsdp", None),
        P("fsdp"),
        P("fsdp", None),
        P("fsdp", None),
        P(),
        P("fsdp", None),
    )
    return jax.shard_map(
        body,
        mesh=mesh,
        in_specs=placed,
        out_specs=(P("fsdp", None), P("fsdp", None)),
        check_vma=False,
    )
```

```python
import functools

import jax
import jax.numpy as jnp
from jax import lax
from jax.experimental import pallas as pl
from jax.experimental.pallas import tpu as pltpu
from jax.sharding import PartitionSpec as P

MESH = pl.DeviceIdType.MESH
F32 = jnp.float32
BF16 = jnp.bfloat16
EPS = 1e-05
DAMPING = 0.1
ALL = slice(None)

ROWS = 256
D = 1536
FF = 3072
ACT = 256
TOTAL_ROWS = 32768
N_ITEM = 5
N_SEND = 90
N_RECV = 124


def nn(left, right):
    return jnp.dot(left, right, preferred_element_type=F32)


def nt(left, right):
    return lax.dot_general(left, right, (((1,), (1,)), ((), ())), preferred_element_type=F32)


def swish_slope(pre, sigma):
    return sigma * (1.0 + pre * (1.0 - sigma))


def kernel(
    states,
    policy_in,
    embed_in,
    gain_in,
    inner_in,
    outer_in,
    precision,
    gradient,
    out_update,
    out_residual,
    S,
    HI,
    HO,
    pack,
    pack_far,
    embed_near,
    inner_wide,
    inner_far,
    policy,
    embed,
    gain,
    gain_tall,
    going,
    start_t,
    later_t,
    NT,
    AA,
    slope,
    mixed,
    unit,
    scale,
    tmix,
    first_d,
    second_d,
    tfirst,
    later,
    tlater,
    cot_later,
    cot_b,
    cot_pre,
    cot_first,
    cot_second,
    IP,
    IPW,
    RB,
    ACC,
    ACCW,
    R1,
    T2,
    T2W,
    R2,
    T3,
    SC,
    g32,
    res32,
    RG,
    res_near,
    res_far,
    send_sem,
    recv_sem,
):
    lo = lax.axis_index("dp")
    f = lax.axis_index("fsdp")
    c = f % 2
    y = (f // 2) % 4
    z = (f // 8) % 4
    hi = f // 32
    x = hi * 2 + lo

    def dev(dx=None, dy=0, dz=0, core=None):
        xx = x if dx is None else (x + dx) % 4
        yy, zz = (y + dy) % 4, (z + dz) % 4
        cc = c if core is None else core
        return (xx % 2, (((xx // 2) * 4 + zz) * 4 + yy) * 2 + cc)

    def axis_dev(axis, d):
        return dev(**{"d" + axis: d})

    opp = ((3 - x) % 2, ((((3 - x) // 2) * 4 + z) * 4 + y) * 2 + c)
    partner = dev(core=1 - c)

    used = [0, 0]
    sent = []

    def fresh(which, n=1):
        used[which] += n
        assert used[which] <= (N_SEND, N_RECV)[which]
        return used[which] - n

    def describe(src, dst, s_sem, r_sem, to):
        return pltpu.make_async_remote_copy(
            src_ref=src,
            dst_ref=dst,
            send_sem=send_sem.at[s_sem],
            recv_sem=recv_sem.at[r_sem],
            device_id=to,
            device_id_type=MESH,
        )

    def copy(src, dst, s_sem, r_sem, to):
        describe(src, dst, s_sem, r_sem, to).start()

    def take(r_sem, ref):
        describe(ref, ref, 0, r_sem, partner).wait_recv()

    def sending(ref):
        s_sem = fresh(0)
        sent.append((s_sem, ref))
        return s_sem

    barrier = pltpu.get_barrier_semaphore()
    peers = [partner] + [axis_dev(a, d) for a in ("x", "y", "z") for d in (1, 2, 3)]
    for peer in peers:
        pl.semaphore_signal(barrier, inc=1, device_id=peer, device_id_type=MESH)
    inner_wide[...] = inner_in[...].astype(F32)
    diagonal = lax.broadcasted_iota(jnp.int32, (24, 24), 0) == lax.broadcasted_iota(jnp.int32, (24, 24), 1)
    gain_row = jnp.broadcast_to(gain_in[...].astype(F32), (24, 24))
    gain_column = jnp.sum(jnp.where(diagonal, gain_row, 0.0), axis=1, keepdims=True)
    for core in range(2):
        pack[:, 384 * core : 384 * core + 128] = policy_in[:, 128 * core : 128 * core + 128].astype(F32)
        pack[:, 384 * core + 128 : 384 * core + 256] = gradient[:, 128 * core : 128 * core + 128]
        pack[:, 384 * core + 256 : 384 * core + 384] = jnp.broadcast_to(gain_column, (24, 128))
    wide = embed_in[...].astype(F32)
    for q in range(4):
        for s in range(3):
            column = 384 * q + 128 * s
            embed_near[16 * s + 4 * q : 16 * s + 4 * q + 4, :] = wide[:, column : column + 128]
    pl.semaphore_wait(barrier, len(peers))

    near_half = pl.ds(pl.multiple_of(c * 384, 128), 384)
    far_half = pl.ds(pl.multiple_of((1 - c) * 384, 128), 384)
    pack_sem = fresh(1)
    copy(pack.at[:, far_half], pack_far, sending(pack_far), pack_sem, partner)
    half = pl.ds(pl.multiple_of((1 - c) * 1536, 128), 1536)
    inner_sem = fresh(1)
    copy(inner_wide.at[:, half], inner_far, sending(inner_far), inner_sem, partner)

    def part(item, t, place, core):
        h, zz, yy, side = place
        if item == 0:
            rows = ALL if side is None else pl.ds(pl.multiple_of(side * 32, 32), 32)
            return S.at[core, t, h, zz, yy, rows, :]
        cols = ALL if side is None else pl.ds(pl.multiple_of(side * 128, 128), 128)
        if item < 3:
            return HI.at[core, (item - 1) * 3 + t, h, zz, yy, :, cols]
        return HO.at[(item - 3) * 3 + t, h, zz, yy, core, :, cols]

    one = lambda i: pl.ds(i, 1)
    low, high = pl.ds(0, 2), pl.ds(2, 2)
    h0, h1 = pl.ds(0, 1), pl.ds(1, 1)
    first_two, first_three = pl.ds(0, 2), pl.ds(0, 3)
    here, zh, yh = one(hi), one(z), one(y)
    ring_axis = {(0, 2): "y", (0, 3): "z", (1, 2): "z", (1, 3): "x", (2, 2): "x", (2, 3): "y"}

    def piece(t, p, d, sub=None):
        xx, zd, yd = (x + d) % 4, one((z + d) % 4), one((y + d) % 4)
        hs = ALL if sub is None else (h0, h1)[sub]
        pair = ALL if sub is None else (low, high)[sub]
        return {
            (0, 2): (hs, zh, yd, None),
            (0, 3): (hs, zd, ALL, None),
            (1, 2): (here, zd, pair, lo),
            (1, 3): (one(xx // 2), pair, ALL, xx % 2),
            (2, 2): (one(xx // 2), pair, yh, xx % 2),
            (2, 3): (hs, ALL, yd, None),
        }[(t, p)]

    two_pieces = {
        (0, 2): (ALL, zh, first_two, None),
        (0, 3): (ALL, first_two, ALL, None),
        (1, 2): (here, first_two, ALL, lo),
        (1, 3): (here, ALL, ALL, None),
        (2, 2): (here, ALL, yh, None),
        (2, 3): (ALL, ALL, first_two, None),
    }
    three_pieces = {
        (0, 2): (ALL, zh, first_three, None),
        (0, 3): (ALL, first_three, ALL, None),
        (1, 2): (here, first_three, ALL, lo),
        (1, 3): (ALL, first_three, ALL, None),
        (2, 2): (ALL, first_three, yh, None),
        (2, 3): (ALL, ALL, first_three, None),
    }
    recv_of = {}
    send_of = {}

    def ship(k, t, place, s_sem, r_sem, to):
        ref = part(k, t, place, c)
        copy(ref, ref, s_sem, r_sem, to)

    def arrived(k, t, place, key):
        take(recv_of[key], part(k, t, place, c))

    first_places = (
        (here, zh, yh, None),
        (here, zh, first_three, lo),
        (here, first_three, yh, lo),
    )

    def stage_a(k):
        for t in range(3):
            s_sem = sending(part(k, t, first_places[t], c))
            recv_of[(k, t, 1)] = r_sem = fresh(1)
            if t == 0:
                ship(k, t, (here, zh, yh, None), s_sem, r_sem, opp)
            else:
                for d in (1, 3, 2):
                    ship(k, t, (here, zh, yh, lo), s_sem, r_sem, axis_dev("yz"[t - 1], d))

    def ring_start(k, t, p):
        axis = ring_axis[(t, p)]
        s_sem = sending(part(k, t, three_pieces[(t, p)], c))
        send_of[(k, t, p)] = s_sem
        base = fresh(1, 2)
        recv_of[(k, t, p, "near")], recv_of[(k, t, p, "far")] = base, base + 1
        if p == 3 and k == N_ITEM - 1:
            recv_of[(k, t, p, "rest")] = rest = fresh(1)
            for sub, sem in ((0, base), (1, rest)):
                ship(k, t, piece(t, p, 0, sub), s_sem, sem, axis_dev(axis, 1))
                ship(k, t, piece(t, p, 0, 1 - sub), s_sem, sem, axis_dev(axis, 3))
        else:
            ship(k, t, piece(t, p, 0), s_sem, base, axis_dev(axis, 1))
            ship(k, t, piece(t, p, 0), s_sem, base, axis_dev(axis, 3))

    def ring_pass(k, t, p):
        axis = ring_axis[(t, p)]
        s_sem, r_sem = send_of[(k, t, p)], recv_of[(k, t, p, "far")]
        place = piece(t, p, 2) if (k, t, p, "rest") in recv_of else two_pieces[(t, p)]
        arrived(k, t, place, (k, t, p, "near"))
        ship(k, t, piece(t, p, 3, 0), s_sem, r_sem, axis_dev(axis, 1))
        ship(k, t, piece(t, p, 1, 1), s_sem, r_sem, axis_dev(axis, 3))

    def item_whole(k, core):
        if k == 0:
            return S.at[core]
        if k < 3:
            return HI.at[core, pl.ds(3 * (k - 1), 3)]
        return HO.at[pl.ds(3 * (k - 3), 3), :, :, :, core]

    def hand(k, t, d):
        s_sem, r_sem = send_of[k], recv_of[k]
        ship(k, t, piece(t, 3, d), s_sem, r_sem, partner)

    def stage_b(k):
        for t in range(3):
            arrived(k, t, first_places[t], (k, t, 1))
            ring_start(k, t, 2)

    def stage_g(k):
        for t in range(3):
            ring_pass(k, t, 2)

    def stage_c(k):
        for t in range(3):
            arrived(k, t, piece(t, 2, 2), (k, t, 2, "far"))
            ring_start(k, t, 3)
        send_of[k] = sending(item_whole(k, c))
        recv_of[k] = fresh(1)
        for t in range(3):
            hand(k, t, 0)

    def stage_d(k):
        for t in range(3):
            ring_pass(k, t, 3)
        for t in range(3):
            if (k, t, 3, "rest") in recv_of:
                arrived(k, t, piece(t, 3, 2), (k, t, 3, "rest"))
            hand(k, t, 3)
            hand(k, t, 1)

    def stage_e(k):
        for t in range(3):
            arrived(k, t, piece(t, 3, 2), (k, t, 3, "far"))
            hand(k, t, 2)

    def stage_f(k):
        take(recv_of[k], item_whole(k, 1 - c))

    scalar_sems = {}
    places = (("core", c, 2), ("y", y, 4), ("z", z, 4), ("x", x, 4))

    def total_send(which, phase, value):
        axis, own, n = places[phase]
        SC[which, phase, own] = value
        ref = SC.at[which, phase, own]
        others = SC.at[which, phase, pl.ds(0, n - 1)]
        s_sem = sending(others)
        scalar_sems[(which, phase)] = r_sem = fresh(1)
        for d in range(1, n):
            to = partner if axis == "core" else axis_dev(axis, d)
            copy(ref, ref, s_sem, r_sem, to)

    def total_take(which, phase):
        n = places[phase][2]
        take(scalar_sems[(which, phase)], SC.at[which, phase, pl.ds(0, n - 1)])
        value = SC[which, phase, 0]
        for i in range(1, n):
            value = value + SC[which, phase, i]
        return value

    def total_step(which, phase):
        value = total_take(which, phase)
        if phase < 3:
            total_send(which, phase + 1, value)
        return value

    def fold(value):
        value = value.reshape(-1, 8, value.shape[-1]).sum(axis=0)
        tile = value[:, 0:128]
        for i in range(1, value.shape[-1] // 128):
            tile = tile + value[:, 128 * i : 128 * i + 128]
        return tile

    def whole(tile):
        return jnp.sum(jnp.sum(tile, axis=1, keepdims=True), axis=0, keepdims=True)

    weigh_rows = outer_in
    for ct in range(6):
        if ct % 3:
            left = weigh_rows[:, 256 * ct : 256 * ct + 128]
            right = weigh_rows[:, 256 * ct + 128 : 256 * ct + 256]
            HO[ct, hi, z, y, c, :, pl.ds(pl.multiple_of(lo * 128, 128), 128)] = jnp.where(lo == 0, left, right)
        else:
            HO[ct, hi, z, y, c] = weigh_rows[:, 256 * ct : 256 * ct + 256]

    stage_a(3)
    stage_a(4)
    near = pack[:, near_half]
    g_own = gradient[...]
    total_send(0, 0, fold(g_own * g_own))
    take(pack_sem, pack_far)
    far = pack_far[...]
    pair = jnp.concatenate([jnp.where(c == 0, near, far), jnp.where(c == 0, far, near)], axis=0)
    g32[hi] = pair[:, 128:256]
    gains = pair[:, 256:384].astype(BF16)
    S[c, 0, hi, z, y, 0:48] = pair[:, 0:128].astype(BF16)
    S[c, 0, hi, z, y, 48:64] = gains[0:16]
    gb = pair[:, 128:256]
    both = jnp.concatenate([gb, pair[16:32, 256:384]], axis=0)
    S[c, 1, hi, z, y, pl.ds(pl.multiple_of(lo * 32, 32), 32)] = jnp.where(lo == 0, both[0:32], both[32:64]).astype(BF16)
    both = jnp.concatenate([embed_near[...], pair[32:48, 256:384]], axis=0)
    S[c, 2, hi, z, y, pl.ds(pl.multiple_of(lo * 32, 32), 32)] = jnp.where(lo == 0, both[0:32], both[32:64]).astype(BF16)
    stage_a(0)
    g_sem = fresh(1)
    copy(g32.at[hi], g32.at[hi], sending(g32.at[hi]), g_sem, opp)

    take(inner_sem, inner_far)
    near = inner_wide[:, pl.ds(pl.multiple_of(c * 1536, 128), 1536)]
    far = inner_far[...]
    pair = jnp.concatenate([jnp.where(c == 0, near, far), jnp.where(c == 0, far, near)], axis=0)
    for ct in range(6):
        if ct % 3:
            left = pair[:, 256 * ct : 256 * ct + 128]
            right = pair[:, 256 * ct + 128 : 256 * ct + 256]
            HI[c, ct, hi, z, y, :, pl.ds(pl.multiple_of(lo * 128, 128), 128)] = jnp.where(lo == 0, left, right).astype(BF16)
        else:
            HI[c, ct, hi, z, y] = pair[:, 256 * ct : 256 * ct + 256].astype(BF16)
    stage_a(1)
    stage_a(2)
    stage_b(3)
    stage_b(4)
    stage_b(0)
    stage_b(1)
    stage_b(2)
    stage_g(3)
    stage_g(4)
    stage_g(0)
    stage_g(1)
    stage_c(0)
    stage_g(2)
    total_step(0, 0)
    stage_c(1)
    total_step(0, 1)
    stage_d(0)

    @pl.loop(0, 6)
    def _(i):
        s = pl.ds(pl.multiple_of(i * 256, 256), 256)
        start_t[s, :] = states[:, s].astype(F32).T.astype(BF16)

    stage_c(2)
    stage_e(0)
    total_step(0, 2)
    stage_f(0)
    rr = whole(total_step(0, 3)) * 0.5

    for t in range(3):
        for a in range(2):
            for b in range(4):
                gain_tall[a, b, :, 16 * t : 16 * t + 16] = S[0, t, a, b, :, 48:64]
    pick = (lax.broadcasted_iota(jnp.int32, (16, 128), 1) == 0).astype(BF16)
    gain[...] = nt(pick, gain_tall[...].reshape(D, 128))[0:8]
    for cc in range(2):
        for a in range(2):
            policy[768 * a : 768 * a + 768, 128 * cc : 128 * cc + 128] = S[cc, 0, a, :, :, 0:48].reshape(768, 128)
            going[768 * a : 768 * a + 768, 128 * cc : 128 * cc + 128] = S[cc, 1, a, :, :, 0:48].reshape(768, 128)
    for q in range(4):
        total = jnp.zeros((ACT, 384), F32)
        for cc in range(2):
            out_row = lax.broadcasted_iota(jnp.int32, (ACT, 512), 0)
            in_row = lax.broadcasted_iota(jnp.int32, (ACT, 512), 1)
            want = (lax.div(out_row, 8) * 16) + 4 * q + lax.rem(out_row, 4)
            mine = lax.rem(lax.div(out_row, 4), 2) == cc
            choose = jnp.where(mine & (in_row == want), 1.0, 0.0).astype(BF16)
            block = jnp.concatenate(
                [S[cc, 2, :, :, :, 16 * s : 16 * s + 16].reshape(512, 128) for s in range(3)], axis=1
            )
            total = total + nn(choose, block)
        embed[:, 384 * q : 384 * q + 384] = total.astype(BF16)

    def blocks(n):
        return pl.loop(0, ROWS // n)

    stage_d(1)
    stage_c(3)

    first = jnp.tanh(nn(states[...], policy[...]))
    first_d[...] = 1.0 - first * first
    mixed[...] = nn(first.astype(BF16), embed[...])
    tfirst[...] = first_d[...] * nn(states[...], going[...])
    tmix[...] = nn(tfirst[...].astype(BF16), embed[...])

    @blocks(32)
    def _(i):
        s = pl.ds(pl.multiple_of(i * 32, 32), 32)
        m = states[s, :].astype(F32) + mixed[s, :]
        mixed[s, :] = m
        r = lax.rsqrt(jnp.mean(m * m, axis=-1, keepdims=True) + EPS)
        scale[s, :] = jnp.broadcast_to(r, (32, 128))
        u = m * r
        unit[s, :] = u
        g = gain[0:1, :]
        NT[s, :] = (u * g).astype(BF16)

    def tangent_norm(offset):
        @blocks(32)
        def _(i):
            s = pl.ds(pl.multiple_of(i * 32, 32), 32)
            o = pl.ds(pl.multiple_of(i * 32 + offset, 32), 32)
            u, v, g = unit[s, :], tmix[s, :], gain[0:1, :]
            w = scale[s, 0:1] * (v - u * jnp.mean(u * v, axis=-1, keepdims=True))
            NT[o, :] = (w * g).astype(BF16)

    tangent_norm(256)

    stage_e(1)
    stage_d(2)
    stage_c(4)
    stage_f(1)

    def take_inner(ch):
        for cc in range(2):
            @pl.loop(0, 3, unroll=True)
            def _(t):
                w = HI[cc, ch * 3 + t].reshape(D, 256)
                cols = pl.ds(pl.multiple_of(cc * 1536 + ch * 768 + t * 256, 256), 256)
                pre = nn(NT[0:256, :], w)
                sigma = jax.nn.sigmoid(pre)
                AA[0:256, cols] = (pre * sigma).astype(BF16)
                sl = swish_slope(pre, sigma)
                slope[:, cols] = sl
                AA[256:512, cols] = (sl * nn(NT[256:512, :], w)).astype(BF16)

    take_inner(0)
    stage_e(2)
    stage_d(3)
    stage_f(2)
    take_inner(1)
    stage_e(3)
    stage_d(4)
    stage_f(3)

    def take_outer(ch):
        @pl.loop(0, 3, unroll=True)
        def _(t):
            w = HO[ch * 3 + t].reshape(FF, 256)
            cols = pl.ds(pl.multiple_of(ch * 768 + t * 256, 256), 256)
            l = (mixed[:, cols] + nn(AA[0:256, :], w)).astype(BF16)
            later[:, cols] = l
            later_t[cols, :] = l.astype(F32).T.astype(BF16)
            tlater[:, cols] = (tmix[:, cols] + nn(AA[256:512, :], w)).astype(BF16)

    take_outer(0)
    stage_e(4)
    stage_f(4)
    take_outer(1)
    take(g_sem, g32.at[1 - hi])

    second = jnp.tanh(nn(later[...], policy[...]))
    second_d[...] = 1.0 - second * second
    weighting = precision[...] * (1.0 / TOTAL_ROWS)

    def finish_sweep(it):
        tsecond = second_d[...] * (nn(tlater[...], policy[...]) + nn(later[...], going[...]))
        tf = tfirst[...]
        total_send(1 + it, 0, fold(weighting * (tf * tf + tsecond * tsecond)))
        cs = (second_d[...] * (weighting * tsecond)).astype(BF16)
        cot_second[...] = cs
        cl = nt(cs, policy[...])
        cot_later[...] = cl
        cot_b[...] = cl.astype(BF16)

        @pl.loop(0, 4, unroll=True)
        def _(i):
            a, b = i // 2, i % 2
            acc = jnp.zeros((ROWS, 768), F32)
            for ct in range(6):
                w = HO[ct, a, pl.ds(b * 2, 2)].reshape(768, 256)
                acc = acc + nt(cot_b[:, 256 * ct : 256 * ct + 256], w)
            cols = pl.ds(pl.multiple_of(i * 768, 256), 768)
            cot_pre[:, cols] = (slope[:, cols] * acc).astype(BF16)

        total_step(1 + it, 0)

        @pl.loop(0, 2, unroll=True)
        def _(a):
            acc = jnp.zeros((ROWS, 768), F32)
            for n in range(12):
                w = HI[n // 6, n % 6, a].reshape(768, 256)
                acc = acc + nt(cot_pre[:, 256 * n : 256 * n + 256], w)
            cols = pl.ds(pl.multiple_of(a * 768, 256), 768)
            tmix[:, cols] = acc

        total_step(1 + it, 1)

        @blocks(32)
        def _(i):
            s = pl.ds(pl.multiple_of(i * 32, 32), 32)
            u, g = unit[s, :], gain[0:1, :]
            v = tmix[s, :] * g
            w = scale[s, 0:1] * (v - u * jnp.mean(u * v, axis=-1, keepdims=True))
            cot_b[s, :] = (cot_later[s, :] + w).astype(BF16)

        cf = (first_d[...] * (weighting * tfirst[...] + nt(cot_b[...], embed[...]))).astype(BF16)
        cot_first[...] = cf

    def halves(v, it):
        if it == 0:
            low_half, high_half = v[:, 0:128], v[:, 128:256]
            low_half, high_half = low_half.reshape(16, 48, 128), high_half.reshape(16, 48, 128)
        else:
            v = v.reshape(16, 48, 256)
            low_half = jnp.concatenate([v[:, 0:24, 0:128], v[:, 0:24, 128:256]], axis=1)
            high_half = jnp.concatenate([v[:, 24:48, 0:128], v[:, 24:48, 128:256]], axis=1)
        return jnp.where(c == 0, low_half, high_half), jnp.where(c == 0, high_half, low_half)

    def sum_image(it):
        swap = []
        for a in range(2):
            rows = slice(768 * a, 768 * a + 768)
            v = nn(start_t[rows, :], cot_first[...]) + nn(later_t[rows, :], cot_second[...])
            keep, give = halves(v, it)
            IPW[it, a] = give.reshape(4, 4, 48, 128).astype(BF16)
            swap.append(fresh(1))
            copy(IPW.at[it, a], RB.at[it, a], sending(IPW.at[it, a]), swap[a], partner)
            IP[it, a] = keep.reshape(4, 4, 48, 128)
        total_step(1 + it, 2)
        sems = []
        for a in range(2):
            take(swap[a], RB.at[it, a])
            v = IP[it, a] + RB[it, a].astype(F32)
            ACC[it, a] = v
            ACCW[it, a] = v.astype(BF16)
            s_sem = sending(R1.at[it, a])
            sems.append(fresh(1))
            for d in (2, 1, 3):
                if a == 0:
                    copy(ACCW.at[it, 0, :, (y + d) % 4], R1.at[it, 0, d - 1], s_sem, sems[a], axis_dev("y", d))
                else:
                    copy(ACCW.at[it, 1, (z + d) % 4], R1.at[it, 1, d - 1], s_sem, sems[a], axis_dev("z", d))
        total = whole(total_step(1 + it, 3))
        second_sems = []
        for a in range(2):
            take(sems[a], R1.at[it, a])
            v = ACC[it, 0, :, y] if a == 0 else ACC[it, 1, z]
            for d in range(3):
                v = v + R1[it, a, d].astype(F32)
            T2[it, a] = v
            T2W[it, a] = v.astype(BF16)
            s_sem = sending(R2.at[it, a])
            second_sems.append(fresh(1))
            axis, own = ("z", z) if a == 0 else ("y", y)
            for d in (2, 1, 3):
                copy(T2W.at[it, a, (own + d) % 4], R2.at[it, a, d - 1], s_sem, second_sems[a], axis_dev(axis, d))
        for a in range(2):
            take(second_sems[a], R2.at[it, a])
            v = T2[it, a, z if a == 0 else y]
            for d in range(3):
                v = v + R2[it, a, d].astype(F32)
            T3[it, x, a] = v.astype(BF16)
        three = T3.at[it, pl.ds(0, 3)]
        s_sem, r_sem = sending(three), fresh(1)
        for d in (2, 1, 3):
            copy(T3.at[it, x], T3.at[it, x], s_sem, r_sem, axis_dev("x", d))
        take(r_sem, three)
        return total

    def summed(it, h):
        v = T3[it, 0, h].astype(F32)
        for i in range(1, 4):
            v = v + T3[it, i, h].astype(F32)
        return v

    finish_sweep(0)
    bend = sum_image(0) + DAMPING * rr
    alpha1 = rr / bend
    for a in range(2):
        g = g32[a]
        residual = g - alpha1 * (summed(0, a) + DAMPING * g)
        res32[a] = residual
        RG[c, a, z, y] = residual.astype(BF16)
    three = (RG.at[c, 0, z, first_three], RG.at[c, 1, first_three, y])
    sems = (fresh(1), fresh(1))
    s_sems = (sending(three[0]), sending(three[1]))
    for d in (2, 1, 3):
        ref = RG.at[c, 0, z, y]
        copy(ref, ref, s_sems[0], sems[0], axis_dev("y", d))
        ref = RG.at[c, 1, z, y]
        copy(ref, ref, s_sems[1], sems[1], axis_dev("z", d))
    swap_send, swap_recv = sending(RG.at[c]), fresh(1)
    s_sems = (sending(RG.at[c, 0, first_three]), sending(RG.at[c, 1, :, first_three]))
    last = {}
    for a in range(2):
        take(sems[a], three[a])
        ref = RG.at[c, 0, z] if a == 0 else RG.at[c, 1, :, y]
        for d in (2, 1, 3):
            last[(a, d)] = fresh(1)
            copy(ref, ref, s_sems[a], last[(a, d)], axis_dev("zy"[a], d))
        copy(ref, ref, swap_send, swap_recv, partner)
    mine = res32[hi]
    res_near[...] = jnp.where(c == 0, mine[24:48], mine[0:24])
    res_sem = fresh(1)
    copy(res_near, res_far, sending(res_near), res_sem, partner)
    for d in (1, 3, 2):
        for a in range(2):
            ref = RG.at[c, 0, (z - d + 4) % 4] if a == 0 else RG.at[c, 1, :, (y - d + 4) % 4]
            take(last[(a, d)], ref)
            copy(ref, ref, swap_send, swap_recv, partner)
    take(swap_recv, RG.at[1 - c])

    tile = jnp.zeros((8, 128), F32)
    for cc in range(2):
        r = RG[cc].astype(F32).reshape(D, 128)
        tile = tile + fold(r * r)
    new = whole(tile)
    beta = new / rr
    tile = jnp.zeros((8, 128), F32)
    for cc in range(2):
        r = RG[cc].astype(F32).reshape(D, 128)
        cols = slice(128 * cc, 128 * cc + 128)
        v = r + beta * going[:, cols].astype(F32)
        tile = tile + fold(v * v)
        going[:, cols] = v.astype(BF16)
    dd = whole(tile)

    tfirst[...] = first_d[...] * nn(states[...], going[...])
    tmix[...] = nn(tfirst[...].astype(BF16), embed[...])
    tangent_norm(256)
    for cc in range(2):
        @pl.loop(0, 6, unroll=True)
        def _(t):
            cols = pl.ds(pl.multiple_of(cc * 1536 + t * 256, 256), 256)
            w = HI[cc, t].reshape(D, 256)
            AA[256:512, cols] = (slope[:, cols] * nn(NT[256:512, :], w)).astype(BF16)

    @pl.loop(0, 6, unroll=True)
    def _(t):
        cols = pl.ds(pl.multiple_of(t * 256, 256), 256)
        w = HO[t].reshape(FF, 256)
        tlater[:, cols] = (tmix[:, cols] + nn(AA[256:512, :], w)).astype(BF16)

    finish_sweep(1)
    bend = sum_image(1) + DAMPING * dd
    alpha2 = new / bend
    image = summed(1, hi)
    image = jnp.concatenate([image[0:24], image[24:48]], axis=1)
    g = gradient[...]
    take(res_sem, res_far)
    mine = res32[hi]
    mine = jnp.where(c == 0, mine[0:24], mine[24:48])
    other = res_far[...]
    res = jnp.concatenate([jnp.where(c == 0, mine, other), jnp.where(c == 0, other, mine)], axis=1)
    direction = res + beta * g
    out_update[...] = alpha1 * g + alpha2 * direction
    out_residual[...] = res - alpha2 * (image + DAMPING * direction)
    for s_sem, ref in sent:
        describe(ref, ref, s_sem, 0, partner).wait_send()


def body(states, policy, action_embed, norm_gain, hidden_in, hidden_out, precision, gradient):
    vmem = pl.BlockSpec(memory_space=pltpu.VMEM)
    shapes = [
        ((2, 3, 2, 4, 4, 64, 128), BF16),
        ((2, 6, 2, 4, 4, 48, 256), BF16),
        ((6, 2, 4, 4, 2, 48, 256), BF16),
        ((24, 768), F32),
        ((24, 384), F32),
        ((48, 128), F32),
        ((24, 3072), F32),
        ((24, 1536), F32),
        ((D, ACT), BF16),
        ((ACT, D), BF16),
        ((8, D), F32),
        ((2, 4, 4, 48, 128), BF16),
        ((D, ACT), BF16),
        ((D, ROWS), BF16),
        ((D, ROWS), BF16),
        ((512, D), BF16),
        ((512, FF), BF16),
        ((ROWS, FF), F32),
        ((ROWS, D), F32),
        ((ROWS, D), F32),
        ((ROWS, 128), F32),
        ((ROWS, D), F32),
        ((ROWS, ACT), F32),
        ((ROWS, ACT), F32),
        ((ROWS, ACT), F32),
        ((ROWS, D), BF16),
        ((ROWS, D), BF16),
        ((ROWS, D), F32),
        ((ROWS, D), BF16),
        ((ROWS, FF), BF16),
        ((ROWS, ACT), BF16),
        ((ROWS, ACT), BF16),
        ((2, 2, 4, 4, 48, 128), F32),
        ((2, 2, 4, 4, 48, 128), BF16),
        ((2, 2, 4, 4, 48, 128), BF16),
        ((2, 2, 4, 4, 48, 128), F32),
        ((2, 2, 4, 4, 48, 128), BF16),
        ((2, 2, 3, 4, 48, 128), BF16),
        ((2, 2, 4, 48, 128), F32),
        ((2, 2, 4, 48, 128), BF16),
        ((2, 2, 3, 48, 128), BF16),
        ((2, 4, 2, 48, 128), BF16),
        ((3, 4, 4, 8, 128), F32),
        ((2, 48, 128), F32),
        ((2, 48, 128), F32),
        ((2, 2, 4, 4, 48, 128), BF16),
        ((24, 128), F32),
        ((24, 128), F32),
    ]
    out = jax.ShapeDtypeStruct(gradient.shape, F32)
    return pl.pallas_call(
        kernel,
        out_shape=(out, out),
        in_specs=[vmem] * 8,
        out_specs=(vmem, vmem),
        scratch_shapes=[pltpu.VMEM(s, t) for s, t in shapes]
        + [pltpu.SemaphoreType.DMA((N_SEND,)), pltpu.SemaphoreType.DMA((N_RECV,))],
        compiler_params=pltpu.CompilerParams(
            collective_id=0, has_side_effects=True, vmem_limit_bytes=62 * 2**20
        ),
        name="natural_step",
    )(
        states,
        policy,
        action_embed,
        norm_gain.reshape(1, -1),
        hidden_in,
        hidden_out,
        precision.reshape(1, ACT),
        gradient,
    )


def solution(mesh):
    placed = (
        P(("dp", "fsdp"), None),
        P("fsdp", None),
        P("fsdp", None),
        P("fsdp"),
        P("fsdp", None),
        P("fsdp", None),
        P(),
        P("fsdp", None),
    )
    return jax.shard_map(
        body,
        mesh=mesh,
        in_specs=placed,
        out_specs=(P("fsdp", None), P("fsdp", None)),
        check_vma=False,
    )
```

```python
import functools

import jax
import jax.numpy as jnp
from jax import lax
from jax.experimental import pallas as pl
from jax.experimental.pallas import tpu as pltpu
from jax.sharding import PartitionSpec as P

MESH = pl.DeviceIdType.MESH
F32 = jnp.float32
BF16 = jnp.bfloat16
EPS = 1e-05
DAMPING = 0.1
ALL = slice(None)

ROWS = 256
D = 1536
FF = 3072
ACT = 256
TOTAL_ROWS = 32768
N_ITEM = 5
N_SEND = 90
N_RECV = 124


def nn(left, right):
    return jnp.dot(left, right, preferred_element_type=F32)


def nt(left, right):
    return lax.dot_general(left, right, (((1,), (1,)), ((), ())), preferred_element_type=F32)


def swish_slope(pre, sigma):
    return sigma * (1.0 + pre * (1.0 - sigma))


def kernel(
    states,
    policy_in,
    embed_in,
    gain_in,
    inner_in,
    outer_in,
    precision,
    gradient,
    out,
    S,
    HI,
    HO,
    pack,
    pack_far,
    embed_near,
    inner_wide,
    inner_far,
    policy,
    embed,
    gain,
    gain_tall,
    going,
    start_t,
    later_t,
    NT,
    AA,
    slope,
    mixed,
    unit,
    scale,
    tmix,
    first_d,
    second_d,
    tfirst,
    later,
    tlater,
    cot_later,
    cot_b,
    cot_pre,
    cot_first,
    cot_second,
    IP,
    IPW,
    RB,
    ACC,
    ACCW,
    R1,
    T2,
    T2W,
    R2,
    T3,
    SC,
    g32,
    res32,
    RG,
    res_near,
    res_far,
    send_sem,
    recv_sem,
):
    lo = lax.axis_index("dp")
    f = lax.axis_index("fsdp")
    c = f % 2
    y = (f // 2) % 4
    z = (f // 8) % 4
    hi = f // 32
    x = hi * 2 + lo

    def dev(dx=None, dy=0, dz=0, core=None):
        xx = x if dx is None else (x + dx) % 4
        yy, zz = (y + dy) % 4, (z + dz) % 4
        cc = c if core is None else core
        return (xx % 2, (((xx // 2) * 4 + zz) * 4 + yy) * 2 + cc)

    def axis_dev(axis, d):
        return dev(**{"d" + axis: d})

    opp = ((3 - x) % 2, ((((3 - x) // 2) * 4 + z) * 4 + y) * 2 + c)
    partner = dev(core=1 - c)

    used = [0, 0]
    sent = []

    def fresh(which, n=1):
        used[which] += n
        assert used[which] <= (N_SEND, N_RECV)[which]
        return used[which] - n

    def describe(src, dst, s_sem, r_sem, to):
        return pltpu.make_async_remote_copy(
            src_ref=src,
            dst_ref=dst,
            send_sem=send_sem.at[s_sem],
            recv_sem=recv_sem.at[r_sem],
            device_id=to,
            device_id_type=MESH,
        )

    def copy(src, dst, s_sem, r_sem, to):
        describe(src, dst, s_sem, r_sem, to).start()

    def take(r_sem, ref):
        describe(ref, ref, 0, r_sem, partner).wait_recv()

    def sending(ref):
        s_sem = fresh(0)
        sent.append((s_sem, ref))
        return s_sem

    barrier = pltpu.get_barrier_semaphore()
    peers = [partner] + [axis_dev(a, d) for a in ("x", "y", "z") for d in (1, 2, 3)]
    for peer in peers:
        pl.semaphore_signal(barrier, inc=1, device_id=peer, device_id_type=MESH)
    inner_wide[...] = inner_in[...].astype(F32)
    diagonal = lax.broadcasted_iota(jnp.int32, (24, 24), 0) == lax.broadcasted_iota(jnp.int32, (24, 24), 1)
    gain_row = jnp.broadcast_to(gain_in[...].astype(F32), (24, 24))
    gain_column = jnp.sum(jnp.where(diagonal, gain_row, 0.0), axis=1, keepdims=True)
    for core in range(2):
        pack[:, 384 * core : 384 * core + 128] = policy_in[:, 128 * core : 128 * core + 128].astype(F32)
        pack[:, 384 * core + 128 : 384 * core + 256] = gradient[:, 128 * core : 128 * core + 128]
        pack[:, 384 * core + 256 : 384 * core + 384] = jnp.broadcast_to(gain_column, (24, 128))
    wide = embed_in[...].astype(F32)
    for q in range(4):
        for s in range(3):
            column = 384 * q + 128 * s
            embed_near[16 * s + 4 * q : 16 * s + 4 * q + 4, :] = wide[:, column : column + 128]
    pl.semaphore_wait(barrier, len(peers))

    near_half = pl.ds(pl.multiple_of(c * 384, 128), 384)
    far_half = pl.ds(pl.multiple_of((1 - c) * 384, 128), 384)
    pack_sem = fresh(1)
    copy(pack.at[:, far_half], pack_far, sending(pack_far), pack_sem, partner)
    half = pl.ds(pl.multiple_of((1 - c) * 1536, 128), 1536)
    inner_sem = fresh(1)
    copy(inner_wide.at[:, half], inner_far, sending(inner_far), inner_sem, partner)

    def part(item, t, place, core):
        h, zz, yy, side = place
        if item == 0:
            rows = ALL if side is None else pl.ds(pl.multiple_of(side * 32, 32), 32)
            return S.at[core, t, h, zz, yy, rows, :]
        cols = ALL if side is None else pl.ds(pl.multiple_of(side * 128, 128), 128)
        if item < 3:
            return HI.at[core, (item - 1) * 3 + t, h, zz, yy, :, cols]
        return HO.at[(item - 3) * 3 + t, h, zz, yy, core, :, cols]

    one = lambda i: pl.ds(i, 1)
    low, high = pl.ds(0, 2), pl.ds(2, 2)
    h0, h1 = pl.ds(0, 1), pl.ds(1, 1)
    first_two, first_three = pl.ds(0, 2), pl.ds(0, 3)
    here, zh, yh = one(hi), one(z), one(y)
    ring_axis = {(0, 2): "y", (0, 3): "z", (1, 2): "z", (1, 3): "x", (2, 2): "x", (2, 3): "y"}

    def piece(t, p, d, sub=None):
        xx, zd, yd = (x + d) % 4, one((z + d) % 4), one((y + d) % 4)
        hs = ALL if sub is None else (h0, h1)[sub]
        pair = ALL if sub is None else (low, high)[sub]
        return {
            (0, 2): (hs, zh, yd, None),
            (0, 3): (hs, zd, ALL, None),
            (1, 2): (here, zd, pair, lo),
            (1, 3): (one(xx // 2), pair, ALL, xx % 2),
            (2, 2): (one(xx // 2), pair, yh, xx % 2),
            (2, 3): (hs, ALL, yd, None),
        }[(t, p)]

    two_pieces = {
        (0, 2): (ALL, zh, first_two, None),
        (0, 3): (ALL, first_two, ALL, None),
        (1, 2): (here, first_two, ALL, lo),
        (1, 3): (here, ALL, ALL, None),
        (2, 2): (here, ALL, yh, None),
        (2, 3): (ALL, ALL, first_two, None),
    }
    three_pieces = {
        (0, 2): (ALL, zh, first_three, None),
        (0, 3): (ALL, first_three, ALL, None),
        (1, 2): (here, first_three, ALL, lo),
        (1, 3): (ALL, first_three, ALL, None),
        (2, 2): (ALL, first_three, yh, None),
        (2, 3): (ALL, ALL, first_three, None),
    }
    recv_of = {}
    send_of = {}

    def ship(k, t, place, s_sem, r_sem, to):
        ref = part(k, t, place, c)
        copy(ref, ref, s_sem, r_sem, to)

    def arrived(k, t, place, key):
        take(recv_of[key], part(k, t, place, c))

    first_places = (
        (here, zh, yh, None),
        (here, zh, first_three, lo),
        (here, first_three, yh, lo),
    )

    def stage_a(k):
        for t in range(3):
            s_sem = sending(part(k, t, first_places[t], c))
            recv_of[(k, t, 1)] = r_sem = fresh(1)
            if t == 0:
                ship(k, t, (here, zh, yh, None), s_sem, r_sem, opp)
            else:
                for d in (1, 3, 2):
                    ship(k, t, (here, zh, yh, lo), s_sem, r_sem, axis_dev("yz"[t - 1], d))

    def ring_start(k, t, p):
        axis = ring_axis[(t, p)]
        s_sem = sending(part(k, t, three_pieces[(t, p)], c))
        send_of[(k, t, p)] = s_sem
        base = fresh(1, 2)
        recv_of[(k, t, p, "near")], recv_of[(k, t, p, "far")] = base, base + 1
        if p == 3 and k == N_ITEM - 1:
            recv_of[(k, t, p, "rest")] = rest = fresh(1)
            for sub, sem in ((0, base), (1, rest)):
                ship(k, t, piece(t, p, 0, sub), s_sem, sem, axis_dev(axis, 1))
                ship(k, t, piece(t, p, 0, 1 - sub), s_sem, sem, axis_dev(axis, 3))
        else:
            ship(k, t, piece(t, p, 0), s_sem, base, axis_dev(axis, 1))
            ship(k, t, piece(t, p, 0), s_sem, base, axis_dev(axis, 3))

    def ring_pass(k, t, p):
        axis = ring_axis[(t, p)]
        s_sem, r_sem = send_of[(k, t, p)], recv_of[(k, t, p, "far")]
        place = piece(t, p, 2) if (k, t, p, "rest") in recv_of else two_pieces[(t, p)]
        arrived(k, t, place, (k, t, p, "near"))
        ship(k, t, piece(t, p, 3, 0), s_sem, r_sem, axis_dev(axis, 1))
        ship(k, t, piece(t, p, 1, 1), s_sem, r_sem, axis_dev(axis, 3))

    def item_whole(k, core):
        if k == 0:
            return S.at[core]
        if k < 3:
            return HI.at[core, pl.ds(3 * (k - 1), 3)]
        return HO.at[pl.ds(3 * (k - 3), 3), :, :, :, core]

    def hand(k, t, d):
        s_sem, r_sem = send_of[k], recv_of[k]
        ship(k, t, piece(t, 3, d), s_sem, r_sem, partner)

    def stage_b(k):
        for t in range(3):
            arrived(k, t, first_places[t], (k, t, 1))
            ring_start(k, t, 2)

    def stage_g(k):
        for t in range(3):
            ring_pass(k, t, 2)

    def stage_c(k):
        for t in range(3):
            arrived(k, t, piece(t, 2, 2), (k, t, 2, "far"))
            ring_start(k, t, 3)
        send_of[k] = sending(item_whole(k, c))
        recv_of[k] = fresh(1)
        for t in range(3):
            hand(k, t, 0)

    def stage_pass(k):
        for t in range(3):
            ring_pass(k, t, 3)

    def stage_d(k):
        if k < N_ITEM - 1:
            stage_pass(k)
        for t in range(3):
            if (k, t, 3, "rest") in recv_of:
                arrived(k, t, piece(t, 3, 2), (k, t, 3, "rest"))
            hand(k, t, 3)
            hand(k, t, 1)

    def stage_e(k):
        for t in range(3):
            arrived(k, t, piece(t, 3, 2), (k, t, 3, "far"))
            hand(k, t, 2)

    def stage_f(k):
        take(recv_of[k], item_whole(k, 1 - c))

    scalar_sems = {}
    places = (("core", c, 2), ("y", y, 4), ("z", z, 4), ("x", x, 4))

    def total_send(which, phase, value):
        axis, own, n = places[phase]
        SC[which, phase, own] = value
        ref = SC.at[which, phase, own]
        others = SC.at[which, phase, pl.ds(0, n - 1)]
        s_sem = sending(others)
        scalar_sems[(which, phase)] = r_sem = fresh(1)
        for d in range(1, n):
            to = partner if axis == "core" else axis_dev(axis, d)
            copy(ref, ref, s_sem, r_sem, to)

    def total_take(which, phase):
        n = places[phase][2]
        take(scalar_sems[(which, phase)], SC.at[which, phase, pl.ds(0, n - 1)])
        value = SC[which, phase, 0]
        for i in range(1, n):
            value = value + SC[which, phase, i]
        return value

    def total_step(which, phase):
        value = total_take(which, phase)
        if phase < 3:
            total_send(which, phase + 1, value)
        return value

    def fold(value):
        value = value.reshape(-1, 8, value.shape[-1]).sum(axis=0)
        tile = value[:, 0:128]
        for i in range(1, value.shape[-1] // 128):
            tile = tile + value[:, 128 * i : 128 * i + 128]
        return tile

    def whole(tile):
        return jnp.sum(jnp.sum(tile, axis=1, keepdims=True), axis=0, keepdims=True)

    weigh_rows = outer_in
    for ct in range(6):
        if ct % 3:
            left = weigh_rows[:, 256 * ct : 256 * ct + 128]
            right = weigh_rows[:, 256 * ct + 128 : 256 * ct + 256]
            HO[ct, hi, z, y, c, :, pl.ds(pl.multiple_of(lo * 128, 128), 128)] = jnp.where(lo == 0, left, right)
        else:
            HO[ct, hi, z, y, c] = weigh_rows[:, 256 * ct : 256 * ct + 256]

    stage_a(3)
    stage_a(4)
    near = pack[:, near_half]
    g_own = gradient[...]
    total_send(0, 0, fold(g_own * g_own))
    take(pack_sem, pack_far)
    far = pack_far[...]
    pair = jnp.concatenate([jnp.where(c == 0, near, far), jnp.where(c == 0, far, near)], axis=0)
    g32[hi] = pair[:, 128:256]
    gains = pair[:, 256:384].astype(BF16)
    S[c, 0, hi, z, y, 0:48] = pair[:, 0:128].astype(BF16)
    S[c, 0, hi, z, y, 48:64] = gains[0:16]
    gb = pair[:, 128:256]
    both = jnp.concatenate([gb, pair[16:32, 256:384]], axis=0)
    S[c, 1, hi, z, y, pl.ds(pl.multiple_of(lo * 32, 32), 32)] = jnp.where(lo == 0, both[0:32], both[32:64]).astype(BF16)
    both = jnp.concatenate([embed_near[...], pair[32:48, 256:384]], axis=0)
    S[c, 2, hi, z, y, pl.ds(pl.multiple_of(lo * 32, 32), 32)] = jnp.where(lo == 0, both[0:32], both[32:64]).astype(BF16)
    stage_a(0)
    stage_b(3)
    g_sem = fresh(1)
    copy(g32.at[hi], g32.at[hi], sending(g32.at[hi]), g_sem, opp)

    take(inner_sem, inner_far)
    near = inner_wide[:, pl.ds(pl.multiple_of(c * 1536, 128), 1536)]
    far = inner_far[...]
    pair = jnp.concatenate([jnp.where(c == 0, near, far), jnp.where(c == 0, far, near)], axis=0)
    for ct in range(6):
        if ct % 3:
            left = pair[:, 256 * ct : 256 * ct + 128]
            right = pair[:, 256 * ct + 128 : 256 * ct + 256]
            HI[c, ct, hi, z, y, :, pl.ds(pl.multiple_of(lo * 128, 128), 128)] = jnp.where(lo == 0, left, right).astype(BF16)
        else:
            HI[c, ct, hi, z, y] = pair[:, 256 * ct : 256 * ct + 256].astype(BF16)
    stage_a(1)
    stage_a(2)
    stage_g(3)
    stage_b(0)
    stage_c(3)
    stage_b(1)
    stage_b(4)
    stage_g(0)
    stage_b(2)
    stage_c(0)
    stage_g(1)
    total_step(0, 0)
    stage_c(1)
    stage_d(3)
    stage_g(2)
    stage_g(4)
    total_step(0, 1)
    stage_d(0)
    stage_c(2)

    @pl.loop(0, 6)
    def _(i):
        s = pl.ds(pl.multiple_of(i * 256, 256), 256)
        start_t[s, :] = states[:, s].astype(F32).T.astype(BF16)

    stage_e(3)
    stage_e(0)
    total_step(0, 2)
    stage_f(0)
    rr = whole(total_step(0, 3)) * 0.5

    for t in range(3):
        for a in range(2):
            for b in range(4):
                gain_tall[a, b, :, 16 * t : 16 * t + 16] = S[0, t, a, b, :, 48:64]
    pick = (lax.broadcasted_iota(jnp.int32, (16, 128), 1) == 0).astype(BF16)
    gain[...] = nt(pick, gain_tall[...].reshape(D, 128))[0:8]
    for cc in range(2):
        for a in range(2):
            policy[768 * a : 768 * a + 768, 128 * cc : 128 * cc + 128] = S[cc, 0, a, :, :, 0:48].reshape(768, 128)
            going[768 * a : 768 * a + 768, 128 * cc : 128 * cc + 128] = S[cc, 1, a, :, :, 0:48].reshape(768, 128)
    for q in range(4):
        total = jnp.zeros((ACT, 384), F32)
        for cc in range(2):
            out_row = lax.broadcasted_iota(jnp.int32, (ACT, 512), 0)
            in_row = lax.broadcasted_iota(jnp.int32, (ACT, 512), 1)
            want = (lax.div(out_row, 8) * 16) + 4 * q + lax.rem(out_row, 4)
            mine = lax.rem(lax.div(out_row, 4), 2) == cc
            choose = jnp.where(mine & (in_row == want), 1.0, 0.0).astype(BF16)
            block = jnp.concatenate(
                [S[cc, 2, :, :, :, 16 * s : 16 * s + 16].reshape(512, 128) for s in range(3)], axis=1
            )
            total = total + nn(choose, block)
        embed[:, 384 * q : 384 * q + 384] = total.astype(BF16)

    def blocks(n):
        return pl.loop(0, ROWS // n)

    stage_d(1)
    stage_c(4)

    first = jnp.tanh(nn(states[...], policy[...]))
    first_d[...] = 1.0 - first * first
    mixed[...] = nn(first.astype(BF16), embed[...])
    tfirst[...] = first_d[...] * nn(states[...], going[...])
    tmix[...] = nn(tfirst[...].astype(BF16), embed[...])

    @blocks(32)
    def _(i):
        s = pl.ds(pl.multiple_of(i * 32, 32), 32)
        m = states[s, :].astype(F32) + mixed[s, :]
        mixed[s, :] = m
        r = lax.rsqrt(jnp.mean(m * m, axis=-1, keepdims=True) + EPS)
        scale[s, :] = jnp.broadcast_to(r, (32, 128))
        u = m * r
        unit[s, :] = u
        g = gain[0:1, :]
        NT[s, :] = (u * g).astype(BF16)

    def tangent_norm(offset):
        @blocks(32)
        def _(i):
            s = pl.ds(pl.multiple_of(i * 32, 32), 32)
            o = pl.ds(pl.multiple_of(i * 32 + offset, 32), 32)
            u, v, g = unit[s, :], tmix[s, :], gain[0:1, :]
            w = scale[s, 0:1] * (v - u * jnp.mean(u * v, axis=-1, keepdims=True))
            NT[o, :] = (w * g).astype(BF16)

    tangent_norm(256)

    stage_e(1)
    stage_f(1)

    def take_inner(ch, cc):
        @pl.loop(0, 3, unroll=True)
        def _(t):
            w = HI[cc, ch * 3 + t].reshape(D, 256)
            cols = pl.ds(pl.multiple_of(cc * 1536 + ch * 768 + t * 256, 256), 256)
            pre = nn(NT[0:256, :], w)
            sigma = jax.nn.sigmoid(pre)
            AA[0:256, cols] = (pre * sigma).astype(BF16)
            sl = swish_slope(pre, sigma)
            slope[:, cols] = sl
            AA[256:512, cols] = (sl * nn(NT[256:512, :], w)).astype(BF16)

    take_inner(0, 0)
    stage_d(2)
    take_inner(0, 1)
    stage_e(2)
    stage_f(2)
    take_inner(1, 0)
    stage_pass(4)
    take_inner(1, 1)
    stage_d(4)
    stage_f(3)

    def take_outer(ch):
        @pl.loop(0, 3, unroll=True)
        def _(t):
            w = HO[ch * 3 + t].reshape(FF, 256)
            cols = pl.ds(pl.multiple_of(ch * 768 + t * 256, 256), 256)
            l = (mixed[:, cols] + nn(AA[0:256, :], w)).astype(BF16)
            later[:, cols] = l
            later_t[cols, :] = l.astype(F32).T.astype(BF16)
            tlater[:, cols] = (tmix[:, cols] + nn(AA[256:512, :], w)).astype(BF16)

    take_outer(0)
    stage_e(4)
    stage_f(4)
    take_outer(1)
    take(g_sem, g32.at[1 - hi])

    second = jnp.tanh(nn(later[...], policy[...]))
    second_d[...] = 1.0 - second * second
    weighting = precision[...] * (1.0 / TOTAL_ROWS)

    def finish_sweep(it):
        tsecond = second_d[...] * (nn(tlater[...], policy[...]) + nn(later[...], going[...]))
        tf = tfirst[...]
        total_send(1 + it, 0, fold(weighting * (tf * tf + tsecond * tsecond)))
        cs = (second_d[...] * (weighting * tsecond)).astype(BF16)
        cot_second[...] = cs
        cl = nt(cs, policy[...])
        cot_later[...] = cl
        cot_b[...] = cl.astype(BF16)

        @pl.loop(0, 4, unroll=True)
        def _(i):
            a, b = i // 2, i % 2
            acc = jnp.zeros((ROWS, 768), F32)
            for ct in range(6):
                w = HO[ct, a, pl.ds(b * 2, 2)].reshape(768, 256)
                acc = acc + nt(cot_b[:, 256 * ct : 256 * ct + 256], w)
            cols = pl.ds(pl.multiple_of(i * 768, 256), 768)
            cot_pre[:, cols] = (slope[:, cols] * acc).astype(BF16)

        total_step(1 + it, 0)

        @pl.loop(0, 2, unroll=True)
        def _(a):
            acc = jnp.zeros((ROWS, 768), F32)
            for n in range(12):
                w = HI[n // 6, n % 6, a].reshape(768, 256)
                acc = acc + nt(cot_pre[:, 256 * n : 256 * n + 256], w)
            cols = pl.ds(pl.multiple_of(a * 768, 256), 768)
            tmix[:, cols] = acc

        total_step(1 + it, 1)

        @blocks(32)
        def _(i):
            s = pl.ds(pl.multiple_of(i * 32, 32), 32)
            u, g = unit[s, :], gain[0:1, :]
            v = tmix[s, :] * g
            w = scale[s, 0:1] * (v - u * jnp.mean(u * v, axis=-1, keepdims=True))
            cot_b[s, :] = (cot_later[s, :] + w).astype(BF16)

        cf = (first_d[...] * (weighting * tfirst[...] + nt(cot_b[...], embed[...]))).astype(BF16)
        cot_first[...] = cf

    def halves(v, it):
        if it == 0:
            low_half, high_half = v[:, 0:128], v[:, 128:256]
            low_half, high_half = low_half.reshape(16, 48, 128), high_half.reshape(16, 48, 128)
        else:
            v = v.reshape(16, 48, 256)
            low_half = jnp.concatenate([v[:, 0:24, 0:128], v[:, 0:24, 128:256]], axis=1)
            high_half = jnp.concatenate([v[:, 24:48, 0:128], v[:, 24:48, 128:256]], axis=1)
        return jnp.where(c == 0, low_half, high_half), jnp.where(c == 0, high_half, low_half)

    def sum_image(it):
        swap = []
        for a in range(2):
            rows = slice(768 * a, 768 * a + 768)
            v = nn(start_t[rows, :], cot_first[...]) + nn(later_t[rows, :], cot_second[...])
            keep, give = halves(v, it)
            IPW[it, a] = give.reshape(4, 4, 48, 128).astype(BF16)
            swap.append(fresh(1))
            copy(IPW.at[it, a], RB.at[it, a], sending(IPW.at[it, a]), swap[a], partner)
            IP[it, a] = keep.reshape(4, 4, 48, 128)
        total_step(1 + it, 2)
        sems = []
        for a in range(2):
            take(swap[a], RB.at[it, a])
            v = IP[it, a] + RB[it, a].astype(F32)
            ACC[it, a] = v
            ACCW[it, a] = v.astype(BF16)
            s_sem = sending(R1.at[it, a])
            sems.append(fresh(1))
            for d in (2, 1, 3):
                if a == 0:
                    copy(ACCW.at[it, 0, :, (y + d) % 4], R1.at[it, 0, d - 1], s_sem, sems[a], axis_dev("y", d))
                else:
                    copy(ACCW.at[it, 1, (z + d) % 4], R1.at[it, 1, d - 1], s_sem, sems[a], axis_dev("z", d))
        total = whole(total_step(1 + it, 3))
        second_sems = []
        for a in range(2):
            take(sems[a], R1.at[it, a])
            v = ACC[it, 0, :, y] if a == 0 else ACC[it, 1, z]
            for d in range(3):
                v = v + R1[it, a, d].astype(F32)
            T2[it, a] = v
            T2W[it, a] = v.astype(BF16)
            s_sem = sending(R2.at[it, a])
            second_sems.append(fresh(1))
            axis, own = ("z", z) if a == 0 else ("y", y)
            for d in (2, 1, 3):
                copy(T2W.at[it, a, (own + d) % 4], R2.at[it, a, d - 1], s_sem, second_sems[a], axis_dev(axis, d))
        for a in range(2):
            take(second_sems[a], R2.at[it, a])
            v = T2[it, a, z if a == 0 else y]
            for d in range(3):
                v = v + R2[it, a, d].astype(F32)
            T3[it, x, a] = v.astype(BF16)
        three = T3.at[it, pl.ds(0, 3)]
        s_sem, r_sem = sending(three), fresh(1)
        for d in (2, 1, 3):
            copy(T3.at[it, x], T3.at[it, x], s_sem, r_sem, axis_dev("x", d))
        take(r_sem, three)
        return total

    def summed(it, h):
        v = T3[it, 0, h].astype(F32)
        for i in range(1, 4):
            v = v + T3[it, i, h].astype(F32)
        return v

    finish_sweep(0)
    bend = sum_image(0) + DAMPING * rr
    alpha1 = rr / bend
    for a in range(2):
        g = g32[a]
        residual = g - alpha1 * (summed(0, a) + DAMPING * g)
        res32[a] = residual
        RG[c, a, z, y] = residual.astype(BF16)
    three = (RG.at[c, 0, z, first_three], RG.at[c, 1, first_three, y])
    sems = (fresh(1), fresh(1))
    s_sems = (sending(three[0]), sending(three[1]))
    for d in (2, 1, 3):
        ref = RG.at[c, 0, z, y]
        copy(ref, ref, s_sems[0], sems[0], axis_dev("y", d))
        ref = RG.at[c, 1, z, y]
        copy(ref, ref, s_sems[1], sems[1], axis_dev("z", d))
    swap_send, swap_recv = sending(RG.at[c]), fresh(1)
    s_sems = (sending(RG.at[c, 0, first_three]), sending(RG.at[c, 1, :, first_three]))
    last = {}
    for a in range(2):
        take(sems[a], three[a])
        ref = RG.at[c, 0, z] if a == 0 else RG.at[c, 1, :, y]
        for d in (2, 1, 3):
            last[(a, d)] = fresh(1)
            copy(ref, ref, s_sems[a], last[(a, d)], axis_dev("zy"[a], d))
        copy(ref, ref, swap_send, swap_recv, partner)
    mine = res32[hi]
    res_near[...] = jnp.where(c == 0, mine[24:48], mine[0:24])
    res_sem = fresh(1)
    copy(res_near, res_far, sending(res_near), res_sem, partner)
    for d in (1, 3, 2):
        for a in range(2):
            ref = RG.at[c, 0, (z - d + 4) % 4] if a == 0 else RG.at[c, 1, :, (y - d + 4) % 4]
            take(last[(a, d)], ref)
            copy(ref, ref, swap_send, swap_recv, partner)
    take(swap_recv, RG.at[1 - c])

    tile = jnp.zeros((8, 128), F32)
    for cc in range(2):
        r = RG[cc].astype(F32).reshape(D, 128)
        tile = tile + fold(r * r)
    new = whole(tile)
    beta = new / rr
    tile = jnp.zeros((8, 128), F32)
    for cc in range(2):
        r = RG[cc].astype(F32).reshape(D, 128)
        cols = slice(128 * cc, 128 * cc + 128)
        v = r + beta * going[:, cols].astype(F32)
        tile = tile + fold(v * v)
        going[:, cols] = v.astype(BF16)
    dd = whole(tile)

    tfirst[...] = first_d[...] * nn(states[...], going[...])
    tmix[...] = nn(tfirst[...].astype(BF16), embed[...])
    tangent_norm(256)
    for cc in range(2):
        @pl.loop(0, 6, unroll=True)
        def _(t):
            cols = pl.ds(pl.multiple_of(cc * 1536 + t * 256, 256), 256)
            w = HI[cc, t].reshape(D, 256)
            AA[256:512, cols] = (slope[:, cols] * nn(NT[256:512, :], w)).astype(BF16)

    @pl.loop(0, 6, unroll=True)
    def _(t):
        cols = pl.ds(pl.multiple_of(t * 256, 256), 256)
        w = HO[t].reshape(FF, 256)
        tlater[:, cols] = (tmix[:, cols] + nn(AA[256:512, :], w)).astype(BF16)

    finish_sweep(1)
    bend = sum_image(1) + DAMPING * dd
    alpha2 = new / bend
    image = summed(1, hi)
    image = jnp.concatenate([image[0:24], image[24:48]], axis=1)
    g = gradient[...]
    take(res_sem, res_far)
    mine = res32[hi]
    mine = jnp.where(c == 0, mine[0:24], mine[24:48])
    other = res_far[...]
    res = jnp.concatenate([jnp.where(c == 0, mine, other), jnp.where(c == 0, other, mine)], axis=1)
    direction = res + beta * g
    out[0:24, :] = alpha1 * g + alpha2 * direction
    out[24:48, :] = res - alpha2 * (image + DAMPING * direction)
    for s_sem, ref in sent:
        describe(ref, ref, s_sem, 0, partner).wait_send()


def body(states, policy, action_embed, norm_gain, hidden_in, hidden_out, precision, gradient):
    vmem = pl.BlockSpec(memory_space=pltpu.VMEM)
    shapes = [
        ((2, 3, 2, 4, 4, 64, 128), BF16),
        ((2, 6, 2, 4, 4, 48, 256), BF16),
        ((6, 2, 4, 4, 2, 48, 256), BF16),
        ((24, 768), F32),
        ((24, 384), F32),
        ((48, 128), F32),
        ((24, 3072), F32),
        ((24, 1536), F32),
        ((D, ACT), BF16),
        ((ACT, D), BF16),
        ((8, D), F32),
        ((2, 4, 4, 48, 128), BF16),
        ((D, ACT), BF16),
        ((D, ROWS), BF16),
        ((D, ROWS), BF16),
        ((512, D), BF16),
        ((512, FF), BF16),
        ((ROWS, FF), F32),
        ((ROWS, D), F32),
        ((ROWS, D), F32),
        ((ROWS, 128), F32),
        ((ROWS, D), F32),
        ((ROWS, ACT), F32),
        ((ROWS, ACT), F32),
        ((ROWS, ACT), F32),
        ((ROWS, D), BF16),
        ((ROWS, D), BF16),
        ((ROWS, D), F32),
        ((ROWS, D), BF16),
        ((ROWS, FF), BF16),
        ((ROWS, ACT), BF16),
        ((ROWS, ACT), BF16),
        ((2, 2, 4, 4, 48, 128), F32),
        ((2, 2, 4, 4, 48, 128), BF16),
        ((2, 2, 4, 4, 48, 128), BF16),
        ((2, 2, 4, 4, 48, 128), F32),
        ((2, 2, 4, 4, 48, 128), BF16),
        ((2, 2, 3, 4, 48, 128), BF16),
        ((2, 2, 4, 48, 128), F32),
        ((2, 2, 4, 48, 128), BF16),
        ((2, 2, 3, 48, 128), BF16),
        ((2, 4, 2, 48, 128), BF16),
        ((3, 4, 4, 8, 128), F32),
        ((2, 48, 128), F32),
        ((2, 48, 128), F32),
        ((2, 2, 4, 4, 48, 128), BF16),
        ((24, 128), F32),
        ((24, 128), F32),
    ]
    both = pl.pallas_call(
        kernel,
        out_shape=jax.ShapeDtypeStruct((48, ACT), F32),
        in_specs=[vmem] * 8,
        out_specs=vmem,
        scratch_shapes=[pltpu.VMEM(s, t) for s, t in shapes]
        + [pltpu.SemaphoreType.DMA((N_SEND,)), pltpu.SemaphoreType.DMA((N_RECV,))],
        compiler_params=pltpu.CompilerParams(
            collective_id=0, has_side_effects=True, vmem_limit_bytes=62 * 2**20
        ),
        name="natural_step",
    )(
        states,
        policy,
        action_embed,
        norm_gain.reshape(1, -1),
        hidden_in,
        hidden_out,
        precision.reshape(1, ACT),
        gradient,
    )
    return both[0:24], both[24:48]


def solution(mesh):
    placed = (
        P(("dp", "fsdp"), None),
        P("fsdp", None),
        P("fsdp", None),
        P("fsdp"),
        P("fsdp", None),
        P("fsdp", None),
        P(),
        P("fsdp", None),
    )
    return jax.shard_map(
        body,
        mesh=mesh,
        in_specs=placed,
        out_specs=(P("fsdp", None), P("fsdp", None)),
        check_vma=False,
    )
```

```python
import functools

import jax
import jax.numpy as jnp
from jax import lax
from jax.experimental import pallas as pl
from jax.experimental.pallas import tpu as pltpu
from jax.sharding import PartitionSpec as P

MESH = pl.DeviceIdType.MESH
F32 = jnp.float32
BF16 = jnp.bfloat16
EPS = 1e-05
DAMPING = 0.1
ALL = slice(None)

ROWS = 256
D = 1536
FF = 3072
ACT = 256
TOTAL_ROWS = 32768
LAST = 4
N_SEND = 90
N_RECV = 124


def nn(left, right):
    return jnp.dot(left, right, preferred_element_type=F32)


def nt(left, right):
    return lax.dot_general(left, right, (((1,), (1,)), ((), ())), preferred_element_type=F32)


def swish_slope(pre, sigma):
    return sigma * (1.0 + pre * (1.0 - sigma))


def kernel(
    states,
    policy_in,
    embed_in,
    gain_in,
    inner_in,
    outer_in,
    precision,
    gradient,
    out,
    S,
    HI,
    HO,
    pack,
    pack_far,
    embed_near,
    inner_wide,
    inner_far,
    policy,
    embed,
    gain,
    gain_tall,
    going,
    start_t,
    later_t,
    NT,
    AA,
    slope,
    mixed,
    unit,
    scale,
    tmix,
    first_d,
    second_d,
    tfirst,
    later,
    tlater,
    cot_later,
    cot_b,
    cot_pre,
    cot_first,
    cot_second,
    IP,
    IPW,
    RB,
    ACC,
    ACCW,
    R1,
    T2,
    T2W,
    R2,
    T3,
    SC,
    g32,
    res32,
    RG,
    res_near,
    res_far,
    send_sem,
    recv_sem,
):
    lo = lax.axis_index("dp")
    f = lax.axis_index("fsdp")
    c = f % 2
    y = (f // 2) % 4
    z = (f // 8) % 4
    hi = f // 32
    x = hi * 2 + lo

    def dev(dx=None, dy=0, dz=0, core=None):
        xx = x if dx is None else (x + dx) % 4
        yy, zz = (y + dy) % 4, (z + dz) % 4
        cc = c if core is None else core
        return (xx % 2, (((xx // 2) * 4 + zz) * 4 + yy) * 2 + cc)

    def axis_dev(axis, d):
        return dev(**{"d" + axis: d})

    opp = ((3 - x) % 2, ((((3 - x) // 2) * 4 + z) * 4 + y) * 2 + c)
    partner = dev(core=1 - c)

    used = [0, 0]
    sent = []

    def fresh(which, n=1):
        used[which] += n
        assert used[which] <= (N_SEND, N_RECV)[which]
        return used[which] - n

    def describe(src, dst, s_sem, r_sem, to):
        return pltpu.make_async_remote_copy(
            src_ref=src,
            dst_ref=dst,
            send_sem=send_sem.at[s_sem],
            recv_sem=recv_sem.at[r_sem],
            device_id=to,
            device_id_type=MESH,
        )

    def copy(src, dst, s_sem, r_sem, to):
        describe(src, dst, s_sem, r_sem, to).start()

    def take(r_sem, ref):
        describe(ref, ref, 0, r_sem, partner).wait_recv()

    def sending(ref):
        s_sem = fresh(0)
        sent.append((s_sem, ref))
        return s_sem

    barrier = pltpu.get_barrier_semaphore()
    peers = [partner] + [axis_dev(a, d) for a in ("x", "y", "z") for d in (1, 2, 3)]
    for peer in peers:
        pl.semaphore_signal(barrier, inc=1, device_id=peer, device_id_type=MESH)
    inner_wide[...] = inner_in[...].astype(F32)
    diagonal = lax.broadcasted_iota(jnp.int32, (24, 24), 0) == lax.broadcasted_iota(jnp.int32, (24, 24), 1)
    gain_row = jnp.broadcast_to(gain_in[...].astype(F32), (24, 24))
    gain_column = jnp.sum(jnp.where(diagonal, gain_row, 0.0), axis=1, keepdims=True)
    for core in range(2):
        pack[:, 384 * core : 384 * core + 128] = policy_in[:, 128 * core : 128 * core + 128].astype(F32)
        pack[:, 384 * core + 128 : 384 * core + 256] = gradient[:, 128 * core : 128 * core + 128]
        pack[:, 384 * core + 256 : 384 * core + 384] = jnp.broadcast_to(gain_column, (24, 128))
    wide = embed_in[...].astype(F32)
    for q in range(4):
        for s in range(3):
            column = 384 * q + 128 * s
            embed_near[16 * s + 4 * q : 16 * s + 4 * q + 4, :] = wide[:, column : column + 128]
    pl.semaphore_wait(barrier, len(peers))

    near_half = pl.ds(pl.multiple_of(c * 384, 128), 384)
    far_half = pl.ds(pl.multiple_of((1 - c) * 384, 128), 384)
    pack_sem = fresh(1)
    copy(pack.at[:, far_half], pack_far, sending(pack_far), pack_sem, partner)
    half = pl.ds(pl.multiple_of((1 - c) * 1536, 128), 1536)
    inner_sem = fresh(1)
    copy(inner_wide.at[:, half], inner_far, sending(inner_far), inner_sem, partner)

    def part(item, t, place, core):
        h, zz, yy, side = place
        if item == 0:
            rows = ALL if side is None else pl.ds(pl.multiple_of(side * 32, 32), 32)
            return S.at[core, t, h, zz, yy, rows, :]
        cols = ALL if side is None else pl.ds(pl.multiple_of(side * 128, 128), 128)
        if item == 1:
            return HI.at[core, :, t, h, zz, yy, :, cols]
        return HO.at[ALL if item == 2 else item - 3, t, h, zz, yy, core, :, cols]

    one = lambda i: pl.ds(i, 1)
    low, high = pl.ds(0, 2), pl.ds(2, 2)
    h0, h1 = pl.ds(0, 1), pl.ds(1, 1)
    first_two, first_three = pl.ds(0, 2), pl.ds(0, 3)
    here, zh, yh = one(hi), one(z), one(y)
    ring_axis = {(0, 2): "y", (0, 3): "z", (1, 2): "z", (1, 3): "x", (2, 2): "x", (2, 3): "y"}

    def piece(t, p, d, sub=None):
        xx, zd, yd = (x + d) % 4, one((z + d) % 4), one((y + d) % 4)
        hs = ALL if sub is None else (h0, h1)[sub]
        pair = ALL if sub is None else (low, high)[sub]
        return {
            (0, 2): (hs, zh, yd, None),
            (0, 3): (hs, zd, ALL, None),
            (1, 2): (here, zd, pair, lo),
            (1, 3): (one(xx // 2), pair, ALL, xx % 2),
            (2, 2): (one(xx // 2), pair, yh, xx % 2),
            (2, 3): (hs, ALL, yd, None),
        }[(t, p)]

    two_pieces = {
        (0, 2): (ALL, zh, first_two, None),
        (0, 3): (ALL, first_two, ALL, None),
        (1, 2): (here, first_two, ALL, lo),
        (1, 3): (here, ALL, ALL, None),
        (2, 2): (here, ALL, yh, None),
        (2, 3): (ALL, ALL, first_two, None),
    }
    three_pieces = {
        (0, 2): (ALL, zh, first_three, None),
        (0, 3): (ALL, first_three, ALL, None),
        (1, 2): (here, first_three, ALL, lo),
        (1, 3): (ALL, first_three, ALL, None),
        (2, 2): (ALL, first_three, yh, None),
        (2, 3): (ALL, ALL, first_three, None),
    }
    recv_of = {}
    send_of = {}

    def ship(k, t, place, s_sem, r_sem, to):
        ref = part(k, t, place, c)
        copy(ref, ref, s_sem, r_sem, to)

    def arrived(k, t, place, key):
        take(recv_of[key], part(k, t, place, c))

    first_places = (
        (here, zh, yh, None),
        (here, zh, first_three, lo),
        (here, first_three, yh, lo),
    )

    def stage_a(k):
        for t in range(3):
            s_sem = sending(part(k, t, first_places[t], c))
            recv_of[(k, t, 1)] = r_sem = fresh(1)
            if t == 0:
                ship(k, t, (here, zh, yh, None), s_sem, r_sem, opp)
            else:
                for d in (1, 3, 2):
                    ship(k, t, (here, zh, yh, lo), s_sem, r_sem, axis_dev("yz"[t - 1], d))

    def ring_start(k, t, p):
        axis = ring_axis[(t, p)]
        s_sem = sending(part(k, t, three_pieces[(t, p)], c))
        send_of[(k, t, p)] = s_sem
        base = fresh(1, 2)
        recv_of[(k, t, p, "near")], recv_of[(k, t, p, "far")] = base, base + 1
        if p == 3 and k == LAST:
            recv_of[(k, t, p, "rest")] = rest = fresh(1)
            for sub, sem in ((0, base), (1, rest)):
                ship(k, t, piece(t, p, 0, sub), s_sem, sem, axis_dev(axis, 1))
                ship(k, t, piece(t, p, 0, 1 - sub), s_sem, sem, axis_dev(axis, 3))
        else:
            ship(k, t, piece(t, p, 0), s_sem, base, axis_dev(axis, 1))
            ship(k, t, piece(t, p, 0), s_sem, base, axis_dev(axis, 3))

    def ring_pass(k, t, p):
        axis = ring_axis[(t, p)]
        s_sem, r_sem = send_of[(k, t, p)], recv_of[(k, t, p, "far")]
        place = piece(t, p, 2) if (k, t, p, "rest") in recv_of else two_pieces[(t, p)]
        arrived(k, t, place, (k, t, p, "near"))
        ship(k, t, piece(t, p, 3, 0), s_sem, r_sem, axis_dev(axis, 1))
        ship(k, t, piece(t, p, 1, 1), s_sem, r_sem, axis_dev(axis, 3))

    def item_whole(k, core):
        if k == 0:
            return S.at[core]
        if k == 1:
            return HI.at[core]
        return HO.at[k - 3, :, :, :, :, core]

    def hand(k, t, d):
        if k == 1 or k == LAST:
            ship(k, t, piece(t, 3, d), send_of[k], recv_of[k], partner)

    def stage_b(k):
        for t in range(3):
            arrived(k, t, first_places[t], (k, t, 1))
            ring_start(k, t, 2)

    def stage_g(k):
        for t in range(3):
            ring_pass(k, t, 2)

    def stage_c(k):
        for t in range(3):
            if k < LAST:
                first_two_phases = min(k, 2)
                arrived(first_two_phases, t, piece(t, 2, 2), (first_two_phases, t, 2, "far"))
            ring_start(k, t, 3)
        send_of[k] = sending(item_whole(k, c))
        recv_of[k] = fresh(1)
        for t in range(3):
            hand(k, t, 0)

    def stage_pass(k):
        for t in range(3):
            ring_pass(k, t, 3)

    def stage_d(k):
        for t in range(3):
            if (k, t, 3, "rest") in recv_of:
                arrived(k, t, piece(t, 3, 2), (k, t, 3, "rest"))
            hand(k, t, 3)
            hand(k, t, 1)

    def stage_e(k):
        for t in range(3):
            arrived(k, t, piece(t, 3, 2), (k, t, 3, "far"))
            hand(k, t, 2)
        if k == 0:
            copy(S.at[c], S.at[c], send_of[k], recv_of[k], partner)
        if k == 3:
            copy(item_whole(k, c), item_whole(k, c), send_of[k], recv_of[k], partner)

    def stage_f(k):
        take(recv_of[k], item_whole(k, 1 - c))

    scalar_sems = {}
    places = (("core", c, 2), ("y", y, 4), ("z", z, 4), ("x", x, 4))

    def total_send(which, phase, value):
        axis, own, n = places[phase]
        SC[which, phase, own] = value
        ref = SC.at[which, phase, own]
        others = SC.at[which, phase, pl.ds(0, n - 1)]
        s_sem = sending(others)
        scalar_sems[(which, phase)] = r_sem = fresh(1)
        for d in range(1, n):
            to = partner if axis == "core" else axis_dev(axis, d)
            copy(ref, ref, s_sem, r_sem, to)

    def total_take(which, phase):
        n = places[phase][2]
        take(scalar_sems[(which, phase)], SC.at[which, phase, pl.ds(0, n - 1)])
        value = SC[which, phase, 0]
        for i in range(1, n):
            value = value + SC[which, phase, i]
        return value

    def total_step(which, phase):
        value = total_take(which, phase)
        if phase < 3:
            total_send(which, phase + 1, value)
        return value

    def fold(value):
        value = value.reshape(-1, 8, value.shape[-1]).sum(axis=0)
        tile = value[:, 0:128]
        for i in range(1, value.shape[-1] // 128):
            tile = tile + value[:, 128 * i : 128 * i + 128]
        return tile

    def whole(tile):
        return jnp.sum(jnp.sum(tile, axis=1, keepdims=True), axis=0, keepdims=True)

    weigh_rows = outer_in
    for ct in range(6):
        if ct % 3:
            left = weigh_rows[:, 256 * ct : 256 * ct + 128]
            right = weigh_rows[:, 256 * ct + 128 : 256 * ct + 256]
            HO[ct // 3, ct % 3, hi, z, y, c, :, pl.ds(pl.multiple_of(lo * 128, 128), 128)] = jnp.where(lo == 0, left, right)
        else:
            HO[ct // 3, ct % 3, hi, z, y, c] = weigh_rows[:, 256 * ct : 256 * ct + 256]

    stage_a(2)
    near = pack[:, near_half]
    g_own = gradient[...]
    total_send(0, 0, fold(g_own * g_own))
    take(pack_sem, pack_far)
    far = pack_far[...]
    pair = jnp.concatenate([jnp.where(c == 0, near, far), jnp.where(c == 0, far, near)], axis=0)
    g32[hi] = pair[:, 128:256]
    gains = pair[:, 256:384].astype(BF16)
    S[c, 0, hi, z, y, 0:48] = pair[:, 0:128].astype(BF16)
    S[c, 0, hi, z, y, 48:64] = gains[0:16]
    gb = pair[:, 128:256]
    both = jnp.concatenate([gb, pair[16:32, 256:384]], axis=0)
    S[c, 1, hi, z, y, pl.ds(pl.multiple_of(lo * 32, 32), 32)] = jnp.where(lo == 0, both[0:32], both[32:64]).astype(BF16)
    both = jnp.concatenate([embed_near[...], pair[32:48, 256:384]], axis=0)
    S[c, 2, hi, z, y, pl.ds(pl.multiple_of(lo * 32, 32), 32)] = jnp.where(lo == 0, both[0:32], both[32:64]).astype(BF16)
    stage_a(0)
    g_sem = fresh(1)
    copy(g32.at[hi], g32.at[hi], sending(g32.at[hi]), g_sem, opp)

    take(inner_sem, inner_far)
    near = inner_wide[:, pl.ds(pl.multiple_of(c * 1536, 128), 1536)]
    far = inner_far[...]
    pair = jnp.concatenate([jnp.where(c == 0, near, far), jnp.where(c == 0, far, near)], axis=0)
    for ct in range(6):
        if ct % 3:
            left = pair[:, 256 * ct : 256 * ct + 128]
            right = pair[:, 256 * ct + 128 : 256 * ct + 256]
            HI[c, ct // 3, ct % 3, hi, z, y, :, pl.ds(pl.multiple_of(lo * 128, 128), 128)] = jnp.where(lo == 0, left, right).astype(BF16)
        else:
            HI[c, ct // 3, ct % 3, hi, z, y] = pair[:, 256 * ct : 256 * ct + 256].astype(BF16)
    stage_a(1)
    stage_b(2)
    stage_b(0)
    stage_b(1)
    stage_g(2)
    stage_g(0)
    stage_g(1)
    stage_c(0)
    stage_c(1)
    total_step(0, 0)
    stage_pass(0)
    total_step(0, 1)

    @pl.loop(0, 6)
    def _(i):
        s = pl.ds(pl.multiple_of(i * 256, 256), 256)
        start_t[s, :] = states[:, s].astype(F32).T.astype(BF16)

    stage_c(3)
    stage_e(0)
    total_step(0, 2)
    stage_f(0)
    rr = whole(total_step(0, 3)) * 0.5

    for t in range(3):
        for a in range(2):
            for b in range(4):
                gain_tall[a, b, :, 16 * t : 16 * t + 16] = S[0, t, a, b, :, 48:64]
    pick = (lax.broadcasted_iota(jnp.int32, (16, 128), 1) == 0).astype(BF16)
    gain[...] = nt(pick, gain_tall[...].reshape(D, 128))[0:8]
    for cc in range(2):
        for a in range(2):
            policy[768 * a : 768 * a + 768, 128 * cc : 128 * cc + 128] = S[cc, 0, a, :, :, 0:48].reshape(768, 128)
            going[768 * a : 768 * a + 768, 128 * cc : 128 * cc + 128] = S[cc, 1, a, :, :, 0:48].reshape(768, 128)
    for q in range(4):
        total = jnp.zeros((ACT, 384), F32)
        for cc in range(2):
            out_row = lax.broadcasted_iota(jnp.int32, (ACT, 512), 0)
            in_row = lax.broadcasted_iota(jnp.int32, (ACT, 512), 1)
            want = (lax.div(out_row, 8) * 16) + 4 * q + lax.rem(out_row, 4)
            mine = lax.rem(lax.div(out_row, 4), 2) == cc
            choose = jnp.where(mine & (in_row == want), 1.0, 0.0).astype(BF16)
            block = jnp.concatenate(
                [S[cc, 2, :, :, :, 16 * s : 16 * s + 16].reshape(512, 128) for s in range(3)], axis=1
            )
            total = total + nn(choose, block)
        embed[:, 384 * q : 384 * q + 384] = total.astype(BF16)

    def blocks(n):
        return pl.loop(0, ROWS // n)

    stage_pass(1)
    stage_d(1)
    stage_c(4)

    first = jnp.tanh(nn(states[...], policy[...]))
    first_d[...] = 1.0 - first * first
    mixed[...] = nn(first.astype(BF16), embed[...])
    tfirst[...] = first_d[...] * nn(states[...], going[...])
    tmix[...] = nn(tfirst[...].astype(BF16), embed[...])

    @blocks(32)
    def _(i):
        s = pl.ds(pl.multiple_of(i * 32, 32), 32)
        m = states[s, :].astype(F32) + mixed[s, :]
        mixed[s, :] = m
        r = lax.rsqrt(jnp.mean(m * m, axis=-1, keepdims=True) + EPS)
        scale[s, :] = jnp.broadcast_to(r, (32, 128))
        u = m * r
        unit[s, :] = u
        g = gain[0:1, :]
        NT[s, :] = (u * g).astype(BF16)

    def tangent_norm(offset):
        @blocks(32)
        def _(i):
            s = pl.ds(pl.multiple_of(i * 32, 32), 32)
            o = pl.ds(pl.multiple_of(i * 32 + offset, 32), 32)
            u, v, g = unit[s, :], tmix[s, :], gain[0:1, :]
            w = scale[s, 0:1] * (v - u * jnp.mean(u * v, axis=-1, keepdims=True))
            NT[o, :] = (w * g).astype(BF16)

    tangent_norm(256)

    stage_e(1)
    stage_pass(3)
    stage_f(1)

    def take_inner(ch, cc):
        @pl.loop(0, 3, unroll=True)
        def _(t):
            w = HI[cc, ch, t].reshape(D, 256)
            cols = pl.ds(pl.multiple_of(cc * 1536 + ch * 768 + t * 256, 256), 256)
            pre = nn(NT[0:256, :], w)
            sigma = jax.nn.sigmoid(pre)
            AA[0:256, cols] = (pre * sigma).astype(BF16)
            sl = swish_slope(pre, sigma)
            slope[:, cols] = sl
            AA[256:512, cols] = (sl * nn(NT[256:512, :], w)).astype(BF16)

    take_inner(0, 0)
    take_inner(0, 1)
    stage_e(3)
    take_inner(1, 0)
    stage_pass(4)
    take_inner(1, 1)
    stage_d(4)
    stage_f(3)

    def take_outer(ch):
        @pl.loop(0, 3, unroll=True)
        def _(t):
            w = HO[ch, t].reshape(FF, 256)
            cols = pl.ds(pl.multiple_of(ch * 768 + t * 256, 256), 256)
            l = (mixed[:, cols] + nn(AA[0:256, :], w)).astype(BF16)
            later[:, cols] = l
            later_t[cols, :] = l.astype(F32).T.astype(BF16)
            tlater[:, cols] = (tmix[:, cols] + nn(AA[256:512, :], w)).astype(BF16)

    take_outer(0)
    stage_e(4)
    stage_f(4)
    take_outer(1)
    take(g_sem, g32.at[1 - hi])

    second = jnp.tanh(nn(later[...], policy[...]))
    second_d[...] = 1.0 - second * second
    weighting = precision[...] * (1.0 / TOTAL_ROWS)

    def finish_sweep(it):
        tsecond = second_d[...] * (nn(tlater[...], policy[...]) + nn(later[...], going[...]))
        tf = tfirst[...]
        total_send(1 + it, 0, fold(weighting * (tf * tf + tsecond * tsecond)))
        cs = (second_d[...] * (weighting * tsecond)).astype(BF16)
        cot_second[...] = cs
        cl = nt(cs, policy[...])
        cot_later[...] = cl
        cot_b[...] = cl.astype(BF16)

        @pl.loop(0, 4, unroll=True)
        def _(i):
            a, b = i // 2, i % 2
            acc = jnp.zeros((ROWS, 768), F32)
            for ct in range(6):
                w = HO[ct // 3, ct % 3, a, pl.ds(b * 2, 2)].reshape(768, 256)
                acc = acc + nt(cot_b[:, 256 * ct : 256 * ct + 256], w)
            cols = pl.ds(pl.multiple_of(i * 768, 256), 768)
            cot_pre[:, cols] = (slope[:, cols] * acc).astype(BF16)

        total_step(1 + it, 0)

        @pl.loop(0, 2, unroll=True)
        def _(a):
            acc = jnp.zeros((ROWS, 768), F32)
            for n in range(12):
                w = HI[n // 6, n // 3 % 2, n % 3, a].reshape(768, 256)
                acc = acc + nt(cot_pre[:, 256 * n : 256 * n + 256], w)
            cols = pl.ds(pl.multiple_of(a * 768, 256), 768)
            tmix[:, cols] = acc

        total_step(1 + it, 1)

        @blocks(32)
        def _(i):
            s = pl.ds(pl.multiple_of(i * 32, 32), 32)
            u, g = unit[s, :], gain[0:1, :]
            v = tmix[s, :] * g
            w = scale[s, 0:1] * (v - u * jnp.mean(u * v, axis=-1, keepdims=True))
            cot_b[s, :] = (cot_later[s, :] + w).astype(BF16)

        cf = (first_d[...] * (weighting * tfirst[...] + nt(cot_b[...], embed[...]))).astype(BF16)
        cot_first[...] = cf

    def halves(v, it):
        if it == 0:
            low_half, high_half = v[:, 0:128], v[:, 128:256]
            low_half, high_half = low_half.reshape(16, 48, 128), high_half.reshape(16, 48, 128)
        else:
            v = v.reshape(16, 48, 256)
            low_half = jnp.concatenate([v[:, 0:24, 0:128], v[:, 0:24, 128:256]], axis=1)
            high_half = jnp.concatenate([v[:, 24:48, 0:128], v[:, 24:48, 128:256]], axis=1)
        return jnp.where(c == 0, low_half, high_half), jnp.where(c == 0, high_half, low_half)

    def sum_image(it):
        swap = []
        for a in range(2):
            rows = slice(768 * a, 768 * a + 768)
            v = nn(start_t[rows, :], cot_first[...]) + nn(later_t[rows, :], cot_second[...])
            keep, give = halves(v, it)
            IPW[it, a] = give.reshape(4, 4, 48, 128).astype(BF16)
            swap.append(fresh(1))
            copy(IPW.at[it, a], RB.at[it, a], sending(IPW.at[it, a]), swap[a], partner)
            IP[it, a] = keep.reshape(4, 4, 48, 128)
        total_step(1 + it, 2)
        sems = []
        for a in range(2):
            take(swap[a], RB.at[it, a])
            v = IP[it, a] + RB[it, a].astype(F32)
            ACC[it, a] = v
            ACCW[it, a] = v.astype(BF16)
            s_sem = sending(R1.at[it, a])
            sems.append(fresh(1))
            for d in (2, 1, 3):
                if a == 0:
                    copy(ACCW.at[it, 0, :, (y + d) % 4], R1.at[it, 0, d - 1], s_sem, sems[a], axis_dev("y", d))
                else:
                    copy(ACCW.at[it, 1, (z + d) % 4], R1.at[it, 1, d - 1], s_sem, sems[a], axis_dev("z", d))
        total = whole(total_step(1 + it, 3))
        second_sems = []
        for a in range(2):
            take(sems[a], R1.at[it, a])
            v = ACC[it, 0, :, y] if a == 0 else ACC[it, 1, z]
            for d in range(3):
                v = v + R1[it, a, d].astype(F32)
            T2[it, a] = v
            T2W[it, a] = v.astype(BF16)
            s_sem = sending(R2.at[it, a])
            second_sems.append(fresh(1))
            axis, own = ("z", z) if a == 0 else ("y", y)
            for d in (2, 1, 3):
                copy(T2W.at[it, a, (own + d) % 4], R2.at[it, a, d - 1], s_sem, second_sems[a], axis_dev(axis, d))
        for a in range(2):
            take(second_sems[a], R2.at[it, a])
            v = T2[it, a, z if a == 0 else y]
            for d in range(3):
                v = v + R2[it, a, d].astype(F32)
            T3[it, x, a] = v.astype(BF16)
        three = T3.at[it, pl.ds(0, 3)]
        s_sem, r_sem = sending(three), fresh(1)
        for d in (2, 1, 3):
            copy(T3.at[it, x], T3.at[it, x], s_sem, r_sem, axis_dev("x", d))
        take(r_sem, three)
        return total

    def summed(it, h):
        v = T3[it, 0, h].astype(F32)
        for i in range(1, 4):
            v = v + T3[it, i, h].astype(F32)
        return v

    finish_sweep(0)
    bend = sum_image(0) + DAMPING * rr
    alpha1 = rr / bend
    for a in range(2):
        g = g32[a]
        residual = g - alpha1 * (summed(0, a) + DAMPING * g)
        res32[a] = residual
        RG[c, a, z, y] = residual.astype(BF16)
    three = (RG.at[c, 0, z, first_three], RG.at[c, 1, first_three, y])
    sems = (fresh(1), fresh(1))
    s_sems = (sending(three[0]), sending(three[1]))
    for d in (2, 1, 3):
        ref = RG.at[c, 0, z, y]
        copy(ref, ref, s_sems[0], sems[0], axis_dev("y", d))
        ref = RG.at[c, 1, z, y]
        copy(ref, ref, s_sems[1], sems[1], axis_dev("z", d))
    swap_send, swap_recv = sending(RG.at[c]), fresh(1)
    s_sems = (sending(RG.at[c, 0, first_three]), sending(RG.at[c, 1, :, first_three]))
    last = {}
    for a in range(2):
        take(sems[a], three[a])
        ref = RG.at[c, 0, z] if a == 0 else RG.at[c, 1, :, y]
        for d in (2, 1, 3):
            last[(a, d)] = fresh(1)
            copy(ref, ref, s_sems[a], last[(a, d)], axis_dev("zy"[a], d))
        copy(ref, ref, swap_send, swap_recv, partner)
    mine = res32[hi]
    res_near[...] = jnp.where(c == 0, mine[24:48], mine[0:24])
    res_sem = fresh(1)
    copy(res_near, res_far, sending(res_near), res_sem, partner)
    for d in (1, 3, 2):
        for a in range(2):
            ref = RG.at[c, 0, (z - d + 4) % 4] if a == 0 else RG.at[c, 1, :, (y - d + 4) % 4]
            take(last[(a, d)], ref)
            copy(ref, ref, swap_send, swap_recv, partner)
    take(swap_recv, RG.at[1 - c])

    tile = jnp.zeros((8, 128), F32)
    for cc in range(2):
        r = RG[cc].astype(F32).reshape(D, 128)
        tile = tile + fold(r * r)
    new = whole(tile)
    beta = new / rr
    tile = jnp.zeros((8, 128), F32)
    for cc in range(2):
        r = RG[cc].astype(F32).reshape(D, 128)
        cols = slice(128 * cc, 128 * cc + 128)
        v = r + beta * going[:, cols].astype(F32)
        tile = tile + fold(v * v)
        going[:, cols] = v.astype(BF16)
    dd = whole(tile)

    tfirst[...] = first_d[...] * nn(states[...], going[...])
    tmix[...] = nn(tfirst[...].astype(BF16), embed[...])
    tangent_norm(256)
    for cc in range(2):
        @pl.loop(0, 6, unroll=True)
        def _(t):
            cols = pl.ds(pl.multiple_of(cc * 1536 + t * 256, 256), 256)
            w = HI[cc, t // 3, t % 3].reshape(D, 256)
            AA[256:512, cols] = (slope[:, cols] * nn(NT[256:512, :], w)).astype(BF16)

    @pl.loop(0, 6, unroll=True)
    def _(t):
        cols = pl.ds(pl.multiple_of(t * 256, 256), 256)
        w = HO[t // 3, t % 3].reshape(FF, 256)
        tlater[:, cols] = (tmix[:, cols] + nn(AA[256:512, :], w)).astype(BF16)

    finish_sweep(1)
    bend = sum_image(1) + DAMPING * dd
    alpha2 = new / bend
    image = summed(1, hi)
    image = jnp.concatenate([image[0:24], image[24:48]], axis=1)
    g = gradient[...]
    take(res_sem, res_far)
    mine = res32[hi]
    mine = jnp.where(c == 0, mine[0:24], mine[24:48])
    other = res_far[...]
    res = jnp.concatenate([jnp.where(c == 0, mine, other), jnp.where(c == 0, other, mine)], axis=1)
    direction = res + beta * g
    out[0:24, :] = alpha1 * g + alpha2 * direction
    out[24:48, :] = res - alpha2 * (image + DAMPING * direction)
    for s_sem, ref in sent:
        describe(ref, ref, s_sem, 0, partner).wait_send()


def body(states, policy, action_embed, norm_gain, hidden_in, hidden_out, precision, gradient):
    vmem = pl.BlockSpec(memory_space=pltpu.VMEM)
    shapes = [
        ((2, 3, 2, 4, 4, 64, 128), BF16),
        ((2, 2, 3, 2, 4, 4, 48, 256), BF16),
        ((2, 3, 2, 4, 4, 2, 48, 256), BF16),
        ((24, 768), F32),
        ((24, 384), F32),
        ((48, 128), F32),
        ((24, 3072), F32),
        ((24, 1536), F32),
        ((D, ACT), BF16),
        ((ACT, D), BF16),
        ((8, D), F32),
        ((2, 4, 4, 48, 128), BF16),
        ((D, ACT), BF16),
        ((D, ROWS), BF16),
        ((D, ROWS), BF16),
        ((512, D), BF16),
        ((512, FF), BF16),
        ((ROWS, FF), F32),
        ((ROWS, D), F32),
        ((ROWS, D), F32),
        ((ROWS, 128), F32),
        ((ROWS, D), F32),
        ((ROWS, ACT), F32),
        ((ROWS, ACT), F32),
        ((ROWS, ACT), F32),
        ((ROWS, D), BF16),
        ((ROWS, D), BF16),
        ((ROWS, D), F32),
        ((ROWS, D), BF16),
        ((ROWS, FF), BF16),
        ((ROWS, ACT), BF16),
        ((ROWS, ACT), BF16),
        ((2, 2, 4, 4, 48, 128), F32),
        ((2, 2, 4, 4, 48, 128), BF16),
        ((2, 2, 4, 4, 48, 128), BF16),
        ((2, 2, 4, 4, 48, 128), F32),
        ((2, 2, 4, 4, 48, 128), BF16),
        ((2, 2, 3, 4, 48, 128), BF16),
        ((2, 2, 4, 48, 128), F32),
        ((2, 2, 4, 48, 128), BF16),
        ((2, 2, 3, 48, 128), BF16),
        ((2, 4, 2, 48, 128), BF16),
        ((3, 4, 4, 8, 128), F32),
        ((2, 48, 128), F32),
        ((2, 48, 128), F32),
        ((2, 2, 4, 4, 48, 128), BF16),
        ((24, 128), F32),
        ((24, 128), F32),
    ]
    both = pl.pallas_call(
        kernel,
        out_shape=jax.ShapeDtypeStruct((48, ACT), F32),
        in_specs=[vmem] * 8,
        out_specs=vmem,
        scratch_shapes=[pltpu.VMEM(s, t) for s, t in shapes]
        + [pltpu.SemaphoreType.DMA((N_SEND,)), pltpu.SemaphoreType.DMA((N_RECV,))],
        compiler_params=pltpu.CompilerParams(
            collective_id=0, has_side_effects=True, vmem_limit_bytes=62 * 2**20
        ),
        name="natural_step",
    )(
        states,
        policy,
        action_embed,
        norm_gain.reshape(1, -1),
        hidden_in,
        hidden_out,
        precision.reshape(1, ACT),
        gradient,
    )
    return both[0:24], both[24:48]


def solution(mesh):
    placed = (
        P(("dp", "fsdp"), None),
        P("fsdp", None),
        P("fsdp", None),
        P("fsdp"),
        P("fsdp", None),
        P("fsdp", None),
        P(),
        P("fsdp", None),
    )
    return jax.shard_map(
        body,
        mesh=mesh,
        in_specs=placed,
        out_specs=(P("fsdp", None), P("fsdp", None)),
        check_vma=False,
    )
```

```python
import functools

import jax
import jax.numpy as jnp
from jax import lax
from jax.experimental import pallas as pl
from jax.experimental.pallas import tpu as pltpu
from jax.sharding import PartitionSpec as P

MESH = pl.DeviceIdType.MESH
F32 = jnp.float32
BF16 = jnp.bfloat16
EPS = 1e-05
DAMPING = 0.1
ALL = slice(None)

ROWS = 256
D = 1536
FF = 3072
ACT = 256
TOTAL_ROWS = 32768
LAST = 4
N_SEND = 90
N_RECV = 124


def nn(left, right):
    return jnp.dot(left, right, preferred_element_type=F32)


def nt(left, right):
    return lax.dot_general(left, right, (((1,), (1,)), ((), ())), preferred_element_type=F32)


def swish_slope(pre, sigma):
    return sigma * (1.0 + pre * (1.0 - sigma))


def kernel(
    states,
    policy_in,
    embed_in,
    gain_in,
    inner_in,
    outer_in,
    precision,
    gradient,
    out,
    S,
    HI,
    HO,
    pack,
    pack_far,
    embed_near,
    inner_wide,
    inner_far,
    policy,
    embed,
    gain,
    gain_tall,
    going,
    start_t,
    later_t,
    NT,
    AA,
    slope,
    mixed,
    unit,
    scale,
    tmix,
    first_d,
    second_d,
    tfirst,
    later,
    tlater,
    cot_later,
    cot_b,
    cot_pre,
    cot_first,
    cot_second,
    IP,
    IPW,
    RB,
    ACC,
    ACCW,
    R1,
    T2,
    T2W,
    R2,
    T3,
    SC,
    g32,
    res32,
    RG,
    res_near,
    res_far,
    send_sem,
    recv_sem,
):
    lo = lax.axis_index("dp")
    f = lax.axis_index("fsdp")
    c = f % 2
    y = (f // 2) % 4
    z = (f // 8) % 4
    hi = f // 32
    x = hi * 2 + lo

    def dev(dx=None, dy=0, dz=0, core=None):
        xx = x if dx is None else (x + dx) % 4
        yy, zz = (y + dy) % 4, (z + dz) % 4
        cc = c if core is None else core
        return (xx % 2, (((xx // 2) * 4 + zz) * 4 + yy) * 2 + cc)

    def axis_dev(axis, d):
        return dev(**{"d" + axis: d})

    opp = ((3 - x) % 2, ((((3 - x) // 2) * 4 + z) * 4 + y) * 2 + c)
    partner = dev(core=1 - c)

    used = [0, 0]
    sent = []

    def fresh(which, n=1):
        used[which] += n
        assert used[which] <= (N_SEND, N_RECV)[which]
        return used[which] - n

    def describe(src, dst, s_sem, r_sem, to):
        return pltpu.make_async_remote_copy(
            src_ref=src,
            dst_ref=dst,
            send_sem=send_sem.at[s_sem],
            recv_sem=recv_sem.at[r_sem],
            device_id=to,
            device_id_type=MESH,
        )

    def copy(src, dst, s_sem, r_sem, to):
        describe(src, dst, s_sem, r_sem, to).start()

    def take(r_sem, ref):
        describe(ref, ref, 0, r_sem, partner).wait_recv()

    def sending(ref):
        s_sem = fresh(0)
        sent.append((s_sem, ref))
        return s_sem

    barrier = pltpu.get_barrier_semaphore()
    peers = [partner] + [axis_dev(a, d) for a in ("x", "y", "z") for d in (1, 2, 3)]
    for peer in peers:
        pl.semaphore_signal(barrier, inc=1, device_id=peer, device_id_type=MESH)
    inner_wide[...] = inner_in[...].astype(F32)
    diagonal = lax.broadcasted_iota(jnp.int32, (24, 24), 0) == lax.broadcasted_iota(jnp.int32, (24, 24), 1)
    gain_row = jnp.broadcast_to(gain_in[...].astype(F32), (24, 24))
    gain_column = jnp.sum(jnp.where(diagonal, gain_row, 0.0), axis=1, keepdims=True)
    for core in range(2):
        pack[:, 384 * core : 384 * core + 128] = policy_in[:, 128 * core : 128 * core + 128].astype(F32)
        pack[:, 384 * core + 128 : 384 * core + 256] = gradient[:, 128 * core : 128 * core + 128]
        pack[:, 384 * core + 256 : 384 * core + 384] = jnp.broadcast_to(gain_column, (24, 128))
    wide = embed_in[...].astype(F32)
    for q in range(4):
        for s in range(3):
            column = 384 * q + 128 * s
            embed_near[16 * s + 4 * q : 16 * s + 4 * q + 4, :] = wide[:, column : column + 128]
    pl.semaphore_wait(barrier, len(peers))

    near_half = pl.ds(pl.multiple_of(c * 384, 128), 384)
    far_half = pl.ds(pl.multiple_of((1 - c) * 384, 128), 384)
    pack_sem = fresh(1)
    copy(pack.at[:, far_half], pack_far, sending(pack_far), pack_sem, partner)
    half = pl.ds(pl.multiple_of((1 - c) * 1536, 128), 1536)
    inner_sem = fresh(1)
    copy(inner_wide.at[:, half], inner_far, sending(inner_far), inner_sem, partner)

    def part(item, t, place, core):
        h, zz, yy, side = place
        if item == 0:
            rows = ALL if side is None else pl.ds(pl.multiple_of(side * 32, 32), 32)
            return S.at[core, t, h, zz, yy, rows, :]
        cols = ALL if side is None else pl.ds(pl.multiple_of(side * 128, 128), 128)
        if item == 1:
            return HI.at[core, :, t, h, zz, yy, :, cols]
        if item >= 5:
            return HI.at[core, item - 5, t, h, zz, yy, :, cols]
        return HO.at[ALL if item == 2 else item - 3, t, h, zz, yy, core, :, cols]

    one = lambda i: pl.ds(i, 1)
    low, high = pl.ds(0, 2), pl.ds(2, 2)
    h0, h1 = pl.ds(0, 1), pl.ds(1, 1)
    first_two, first_three = pl.ds(0, 2), pl.ds(0, 3)
    here, zh, yh = one(hi), one(z), one(y)
    ring_axis = {(0, 2): "y", (0, 3): "z", (1, 2): "z", (1, 3): "x", (2, 2): "x", (2, 3): "y"}

    def piece(t, p, d, sub=None):
        xx, zd, yd = (x + d) % 4, one((z + d) % 4), one((y + d) % 4)
        hs = ALL if sub is None else (h0, h1)[sub]
        pair = ALL if sub is None else (low, high)[sub]
        return {
            (0, 2): (hs, zh, yd, None),
            (0, 3): (hs, zd, ALL, None),
            (1, 2): (here, zd, pair, lo),
            (1, 3): (one(xx // 2), pair, ALL, xx % 2),
            (2, 2): (one(xx // 2), pair, yh, xx % 2),
            (2, 3): (hs, ALL, yd, None),
        }[(t, p)]

    two_pieces = {
        (0, 2): (ALL, zh, first_two, None),
        (0, 3): (ALL, first_two, ALL, None),
        (1, 2): (here, first_two, ALL, lo),
        (1, 3): (here, ALL, ALL, None),
        (2, 2): (here, ALL, yh, None),
        (2, 3): (ALL, ALL, first_two, None),
    }
    three_pieces = {
        (0, 2): (ALL, zh, first_three, None),
        (0, 3): (ALL, first_three, ALL, None),
        (1, 2): (here, first_three, ALL, lo),
        (1, 3): (ALL, first_three, ALL, None),
        (2, 2): (ALL, first_three, yh, None),
        (2, 3): (ALL, ALL, first_three, None),
    }
    recv_of = {}
    send_of = {}

    def ship(k, t, place, s_sem, r_sem, to):
        ref = part(k, t, place, c)
        copy(ref, ref, s_sem, r_sem, to)

    def arrived(k, t, place, key):
        take(recv_of[key], part(k, t, place, c))

    first_places = (
        (here, zh, yh, None),
        (here, zh, first_three, lo),
        (here, first_three, yh, lo),
    )

    def stage_a(k):
        for t in range(3):
            s_sem = sending(part(k, t, first_places[t], c))
            recv_of[(k, t, 1)] = r_sem = fresh(1)
            if t == 0:
                ship(k, t, (here, zh, yh, None), s_sem, r_sem, opp)
            else:
                for d in (1, 3, 2):
                    ship(k, t, (here, zh, yh, lo), s_sem, r_sem, axis_dev("yz"[t - 1], d))

    def ring_start(k, t, p):
        axis = ring_axis[(t, p)]
        s_sem = sending(part(k, t, three_pieces[(t, p)], c))
        send_of[(k, t, p)] = s_sem
        base = fresh(1, 2)
        recv_of[(k, t, p, "near")], recv_of[(k, t, p, "far")] = base, base + 1
        if p == 3 and k == LAST:
            recv_of[(k, t, p, "rest")] = rest = fresh(1)
            for sub, sem in ((0, base), (1, rest)):
                ship(k, t, piece(t, p, 0, sub), s_sem, sem, axis_dev(axis, 1))
                ship(k, t, piece(t, p, 0, 1 - sub), s_sem, sem, axis_dev(axis, 3))
        else:
            ship(k, t, piece(t, p, 0), s_sem, base, axis_dev(axis, 1))
            ship(k, t, piece(t, p, 0), s_sem, base, axis_dev(axis, 3))

    def ring_pass(k, t, p):
        axis = ring_axis[(t, p)]
        s_sem, r_sem = send_of[(k, t, p)], recv_of[(k, t, p, "far")]
        place = piece(t, p, 2) if (k, t, p, "rest") in recv_of else two_pieces[(t, p)]
        arrived(k, t, place, (k, t, p, "near"))
        ship(k, t, piece(t, p, 3, 0), s_sem, r_sem, axis_dev(axis, 1))
        ship(k, t, piece(t, p, 1, 1), s_sem, r_sem, axis_dev(axis, 3))

    def item_whole(k, core):
        if k == 0:
            return S.at[core]
        if k >= 5:
            return HI.at[core, k - 5]
        return HO.at[k - 3, :, :, :, :, core]

    def hand(k, t, d):
        ship(k, t, piece(t, 3, d), send_of[k], recv_of[(k, t, "hand")], partner)

    def stage_b(k):
        for t in range(3):
            arrived(k, t, first_places[t], (k, t, 1))
            ring_start(k, t, 2)

    def stage_g(k):
        for t in range(3):
            ring_pass(k, t, 2)

    before = {0: 0, 5: 1, 3: 2}

    def stage_c(k):
        for t in range(3):
            if k in before:
                arrived(before[k], t, piece(t, 2, 2), (before[k], t, 2, "far"))
            ring_start(k, t, 3)
        send_of[k] = sending(item_whole(k, c))
        shared = None if k == LAST else fresh(1)
        for t in range(3):
            recv_of[(k, t, "hand")] = fresh(1) if k == LAST else shared
            hand(k, t, 0)

    def stage_pass(k):
        for t in range(3):
            ring_pass(k, t, 3)

    def stage_d(k):
        for t in range(3):
            if (k, t, 3, "rest") in recv_of:
                arrived(k, t, piece(t, 3, 2), (k, t, 3, "rest"))
            hand(k, t, 3)
            hand(k, t, 1)

    def stage_e(k):
        for t in range(3):
            arrived(k, t, piece(t, 3, 2), (k, t, 3, "far"))
            hand(k, t, 2)

    def stage_f(k):
        take(recv_of[(k, 0, "hand")], item_whole(k, 1 - c))

    scalar_sems = {}
    places = (("core", c, 2), ("y", y, 4), ("z", z, 4), ("x", x, 4))

    def total_send(which, phase, value):
        axis, own, n = places[phase]
        SC[which, phase, own] = value
        ref = SC.at[which, phase, own]
        others = SC.at[which, phase, pl.ds(0, n - 1)]
        s_sem = sending(others)
        scalar_sems[(which, phase)] = r_sem = fresh(1)
        for d in range(1, n):
            to = partner if axis == "core" else axis_dev(axis, d)
            copy(ref, ref, s_sem, r_sem, to)

    def total_take(which, phase):
        n = places[phase][2]
        take(scalar_sems[(which, phase)], SC.at[which, phase, pl.ds(0, n - 1)])
        value = SC[which, phase, 0]
        for i in range(1, n):
            value = value + SC[which, phase, i]
        return value

    def total_step(which, phase):
        value = total_take(which, phase)
        if phase < 3:
            total_send(which, phase + 1, value)
        return value

    def fold(value):
        value = value.reshape(-1, 8, value.shape[-1]).sum(axis=0)
        tile = value[:, 0:128]
        for i in range(1, value.shape[-1] // 128):
            tile = tile + value[:, 128 * i : 128 * i + 128]
        return tile

    def whole(tile):
        return jnp.sum(jnp.sum(tile, axis=1, keepdims=True), axis=0, keepdims=True)

    weigh_rows = outer_in
    for ct in range(6):
        if ct % 3:
            left = weigh_rows[:, 256 * ct : 256 * ct + 128]
            right = weigh_rows[:, 256 * ct + 128 : 256 * ct + 256]
            HO[ct // 3, ct % 3, hi, z, y, c, :, pl.ds(pl.multiple_of(lo * 128, 128), 128)] = jnp.where(lo == 0, left, right)
        else:
            HO[ct // 3, ct % 3, hi, z, y, c] = weigh_rows[:, 256 * ct : 256 * ct + 256]

    stage_a(2)
    near = pack[:, near_half]
    g_own = gradient[...]
    total_send(0, 0, fold(g_own * g_own))
    take(pack_sem, pack_far)
    far = pack_far[...]
    pair = jnp.concatenate([jnp.where(c == 0, near, far), jnp.where(c == 0, far, near)], axis=0)
    g32[hi] = pair[:, 128:256]
    gains = pair[:, 256:384].astype(BF16)
    S[c, 0, hi, z, y, 0:48] = pair[:, 0:128].astype(BF16)
    S[c, 0, hi, z, y, 48:64] = gains[0:16]
    gb = pair[:, 128:256]
    both = jnp.concatenate([gb, pair[16:32, 256:384]], axis=0)
    S[c, 1, hi, z, y, pl.ds(pl.multiple_of(lo * 32, 32), 32)] = jnp.where(lo == 0, both[0:32], both[32:64]).astype(BF16)
    both = jnp.concatenate([embed_near[...], pair[32:48, 256:384]], axis=0)
    S[c, 2, hi, z, y, pl.ds(pl.multiple_of(lo * 32, 32), 32)] = jnp.where(lo == 0, both[0:32], both[32:64]).astype(BF16)
    stage_a(0)
    g_sem = fresh(1)
    copy(g32.at[hi], g32.at[hi], sending(g32.at[hi]), g_sem, opp)

    take(inner_sem, inner_far)
    near = inner_wide[:, pl.ds(pl.multiple_of(c * 1536, 128), 1536)]
    far = inner_far[...]
    pair = jnp.concatenate([jnp.where(c == 0, near, far), jnp.where(c == 0, far, near)], axis=0)
    for ct in range(6):
        if ct % 3:
            left = pair[:, 256 * ct : 256 * ct + 128]
            right = pair[:, 256 * ct + 128 : 256 * ct + 256]
            HI[c, ct // 3, ct % 3, hi, z, y, :, pl.ds(pl.multiple_of(lo * 128, 128), 128)] = jnp.where(lo == 0, left, right).astype(BF16)
        else:
            HI[c, ct // 3, ct % 3, hi, z, y] = pair[:, 256 * ct : 256 * ct + 256].astype(BF16)
    stage_a(1)
    stage_b(2)
    stage_b(0)
    stage_b(1)
    stage_g(2)
    stage_g(0)
    stage_g(1)
    stage_c(0)
    total_step(0, 0)
    stage_c(5)
    total_step(0, 1)
    stage_pass(0)
    stage_d(0)

    @pl.loop(0, 6)
    def _(i):
        s = pl.ds(pl.multiple_of(i * 256, 256), 256)
        start_t[s, :] = states[:, s].astype(F32).T.astype(BF16)

    stage_c(6)
    stage_e(0)
    total_step(0, 2)
    stage_f(0)
    rr = whole(total_step(0, 3)) * 0.5

    for t in range(3):
        for a in range(2):
            for b in range(4):
                gain_tall[a, b, :, 16 * t : 16 * t + 16] = S[0, t, a, b, :, 48:64]
    pick = (lax.broadcasted_iota(jnp.int32, (16, 128), 1) == 0).astype(BF16)
    gain[...] = nt(pick, gain_tall[...].reshape(D, 128))[0:8]
    for cc in range(2):
        for a in range(2):
            policy[768 * a : 768 * a + 768, 128 * cc : 128 * cc + 128] = S[cc, 0, a, :, :, 0:48].reshape(768, 128)
            going[768 * a : 768 * a + 768, 128 * cc : 128 * cc + 128] = S[cc, 1, a, :, :, 0:48].reshape(768, 128)
    for q in range(4):
        total = jnp.zeros((ACT, 384), F32)
        for cc in range(2):
            out_row = lax.broadcasted_iota(jnp.int32, (ACT, 512), 0)
            in_row = lax.broadcasted_iota(jnp.int32, (ACT, 512), 1)
            want = (lax.div(out_row, 8) * 16) + 4 * q + lax.rem(out_row, 4)
            mine = lax.rem(lax.div(out_row, 4), 2) == cc
            choose = jnp.where(mine & (in_row == want), 1.0, 0.0).astype(BF16)
            block = jnp.concatenate(
                [S[cc, 2, :, :, :, 16 * s : 16 * s + 16].reshape(512, 128) for s in range(3)], axis=1
            )
            total = total + nn(choose, block)
        embed[:, 384 * q : 384 * q + 384] = total.astype(BF16)

    def blocks(n):
        return pl.loop(0, ROWS // n)

    stage_pass(5)
    stage_d(5)
    stage_c(3)

    first = jnp.tanh(nn(states[...], policy[...]))
    first_d[...] = 1.0 - first * first
    mixed[...] = nn(first.astype(BF16), embed[...])
    tfirst[...] = first_d[...] * nn(states[...], going[...])
    tmix[...] = nn(tfirst[...].astype(BF16), embed[...])

    @blocks(32)
    def _(i):
        s = pl.ds(pl.multiple_of(i * 32, 32), 32)
        m = states[s, :].astype(F32) + mixed[s, :]
        mixed[s, :] = m
        r = lax.rsqrt(jnp.mean(m * m, axis=-1, keepdims=True) + EPS)
        scale[s, :] = jnp.broadcast_to(r, (32, 128))
        u = m * r
        unit[s, :] = u
        g = gain[0:1, :]
        NT[s, :] = (u * g).astype(BF16)

    def tangent_norm(offset):
        @blocks(32)
        def _(i):
            s = pl.ds(pl.multiple_of(i * 32, 32), 32)
            o = pl.ds(pl.multiple_of(i * 32 + offset, 32), 32)
            u, v, g = unit[s, :], tmix[s, :], gain[0:1, :]
            w = scale[s, 0:1] * (v - u * jnp.mean(u * v, axis=-1, keepdims=True))
            NT[o, :] = (w * g).astype(BF16)

    tangent_norm(256)

    stage_e(5)
    stage_pass(6)
    stage_d(6)
    stage_c(4)
    stage_f(5)

    def take_inner(ch, cc):
        @pl.loop(0, 3, unroll=True)
        def _(t):
            w = HI[cc, ch, t].reshape(D, 256)
            cols = pl.ds(pl.multiple_of(cc * 1536 + ch * 768 + t * 256, 256), 256)
            pre = nn(NT[0:256, :], w)
            sigma = jax.nn.sigmoid(pre)
            AA[0:256, cols] = (pre * sigma).astype(BF16)
            sl = swish_slope(pre, sigma)
            slope[:, cols] = sl
            AA[256:512, cols] = (sl * nn(NT[256:512, :], w)).astype(BF16)

    take_inner(0, 0)
    take_inner(0, 1)
    stage_e(6)
    stage_pass(3)
    stage_d(3)
    stage_f(6)
    take_inner(1, 0)
    stage_e(3)
    stage_pass(4)
    take_inner(1, 1)
    stage_d(4)
    stage_f(3)

    def take_outer(ch, t):
        w = HO[ch, t].reshape(FF, 256)
        cols = pl.ds(pl.multiple_of(ch * 768 + t * 256, 256), 256)
        l = (mixed[:, cols] + nn(AA[0:256, :], w)).astype(BF16)
        later[:, cols] = l
        later_t[cols, :] = l.astype(F32).T.astype(BF16)
        tlater[:, cols] = (tmix[:, cols] + nn(AA[256:512, :], w)).astype(BF16)

    @pl.loop(0, 3, unroll=True)
    def _(t):
        take_outer(0, t)

    stage_e(4)
    for t in range(3):
        take(recv_of[(LAST, t, "hand")], part(LAST, t, (ALL, ALL, ALL, None), 1 - c))
        take_outer(1, t)
    take(g_sem, g32.at[1 - hi])

    second = jnp.tanh(nn(later[...], policy[...]))
    second_d[...] = 1.0 - second * second
    weighting = precision[...] * (1.0 / TOTAL_ROWS)

    def finish_sweep(it):
        tsecond = second_d[...] * (nn(tlater[...], policy[...]) + nn(later[...], going[...]))
        tf = tfirst[...]
        total_send(1 + it, 0, fold(weighting * (tf * tf + tsecond * tsecond)))
        cs = (second_d[...] * (weighting * tsecond)).astype(BF16)
        cot_second[...] = cs
        cl = nt(cs, policy[...])
        cot_later[...] = cl
        cot_b[...] = cl.astype(BF16)

        @pl.loop(0, 4, unroll=True)
        def _(i):
            a, b = i // 2, i % 2
            acc = jnp.zeros((ROWS, 768), F32)
            for ct in range(6):
                w = HO[ct // 3, ct % 3, a, pl.ds(b * 2, 2)].reshape(768, 256)
                acc = acc + nt(cot_b[:, 256 * ct : 256 * ct + 256], w)
            cols = pl.ds(pl.multiple_of(i * 768, 256), 768)
            cot_pre[:, cols] = (slope[:, cols] * acc).astype(BF16)

        total_step(1 + it, 0)

        @pl.loop(0, 2, unroll=True)
        def _(a):
            acc = jnp.zeros((ROWS, 768), F32)
            for n in range(12):
                w = HI[n // 6, n // 3 % 2, n % 3, a].reshape(768, 256)
                acc = acc + nt(cot_pre[:, 256 * n : 256 * n + 256], w)
            cols = pl.ds(pl.multiple_of(a * 768, 256), 768)
            tmix[:, cols] = acc

        total_step(1 + it, 1)

        @blocks(32)
        def _(i):
            s = pl.ds(pl.multiple_of(i * 32, 32), 32)
            u, g = unit[s, :], gain[0:1, :]
            v = tmix[s, :] * g
            w = scale[s, 0:1] * (v - u * jnp.mean(u * v, axis=-1, keepdims=True))
            cot_b[s, :] = (cot_later[s, :] + w).astype(BF16)

        cf = (first_d[...] * (weighting * tfirst[...] + nt(cot_b[...], embed[...]))).astype(BF16)
        cot_first[...] = cf

    def halves(v, it):
        if it == 0:
            low_half, high_half = v[:, 0:128], v[:, 128:256]
            low_half, high_half = low_half.reshape(16, 48, 128), high_half.reshape(16, 48, 128)
        else:
            v = v.reshape(16, 48, 256)
            low_half = jnp.concatenate([v[:, 0:24, 0:128], v[:, 0:24, 128:256]], axis=1)
            high_half = jnp.concatenate([v[:, 24:48, 0:128], v[:, 24:48, 128:256]], axis=1)
        return jnp.where(c == 0, low_half, high_half), jnp.where(c == 0, high_half, low_half)

    def sum_image(it):
        swap = []
        for a in range(2):
            rows = slice(768 * a, 768 * a + 768)
            v = nn(start_t[rows, :], cot_first[...]) + nn(later_t[rows, :], cot_second[...])
            keep, give = halves(v, it)
            IPW[it, a] = give.reshape(4, 4, 48, 128).astype(BF16)
            swap.append(fresh(1))
            copy(IPW.at[it, a], RB.at[it, a], sending(IPW.at[it, a]), swap[a], partner)
            IP[it, a] = keep.reshape(4, 4, 48, 128)
        total_step(1 + it, 2)
        sems = []
        for a in range(2):
            take(swap[a], RB.at[it, a])
            v = IP[it, a] + RB[it, a].astype(F32)
            ACC[it, a] = v
            ACCW[it, a] = v.astype(BF16)
            s_sem = sending(R1.at[it, a])
            sems.append(fresh(1))
            for d in (2, 1, 3):
                if a == 0:
                    copy(ACCW.at[it, 0, :, (y + d) % 4], R1.at[it, 0, d - 1], s_sem, sems[a], axis_dev("y", d))
                else:
                    copy(ACCW.at[it, 1, (z + d) % 4], R1.at[it, 1, d - 1], s_sem, sems[a], axis_dev("z", d))
        total = whole(total_step(1 + it, 3))
        second_sems = []
        for a in range(2):
            take(sems[a], R1.at[it, a])
            v = ACC[it, 0, :, y] if a == 0 else ACC[it, 1, z]
            for d in range(3):
                v = v + R1[it, a, d].astype(F32)
            T2[it, a] = v
            T2W[it, a] = v.astype(BF16)
            s_sem = sending(R2.at[it, a])
            second_sems.append(fresh(1))
            axis, own = ("z", z) if a == 0 else ("y", y)
            for d in (2, 1, 3):
                copy(T2W.at[it, a, (own + d) % 4], R2.at[it, a, d - 1], s_sem, second_sems[a], axis_dev(axis, d))
        for a in range(2):
            take(second_sems[a], R2.at[it, a])
            v = T2[it, a, z if a == 0 else y]
            for d in range(3):
                v = v + R2[it, a, d].astype(F32)
            T3[it, x, a] = v.astype(BF16)
        three = T3.at[it, pl.ds(0, 3)]
        s_sem, r_sem = sending(three), fresh(1)
        for d in (2, 1, 3):
            copy(T3.at[it, x], T3.at[it, x], s_sem, r_sem, axis_dev("x", d))
        take(r_sem, three)
        return total

    def summed(it, h):
        v = T3[it, 0, h].astype(F32)
        for i in range(1, 4):
            v = v + T3[it, i, h].astype(F32)
        return v

    finish_sweep(0)
    bend = sum_image(0) + DAMPING * rr
    alpha1 = rr / bend
    for a in range(2):
        g = g32[a]
        residual = g - alpha1 * (summed(0, a) + DAMPING * g)
        res32[a] = residual
        RG[c, a, z, y] = residual.astype(BF16)
    three = (RG.at[c, 0, z, first_three], RG.at[c, 1, first_three, y])
    sems = (fresh(1), fresh(1))
    s_sems = (sending(three[0]), sending(three[1]))
    for d in (2, 1, 3):
        ref = RG.at[c, 0, z, y]
        copy(ref, ref, s_sems[0], sems[0], axis_dev("y", d))
        ref = RG.at[c, 1, z, y]
        copy(ref, ref, s_sems[1], sems[1], axis_dev("z", d))
    swap_send, swap_recv = sending(RG.at[c]), fresh(1)
    s_sems = (sending(RG.at[c, 0, first_three]), sending(RG.at[c, 1, :, first_three]))
    last = {}
    for a in range(2):
        take(sems[a], three[a])
        ref = RG.at[c, 0, z] if a == 0 else RG.at[c, 1, :, y]
        for d in (2, 1, 3):
            last[(a, d)] = fresh(1)
            copy(ref, ref, s_sems[a], last[(a, d)], axis_dev("zy"[a], d))
        copy(ref, ref, swap_send, swap_recv, partner)
    mine = res32[hi]
    res_near[...] = jnp.where(c == 0, mine[24:48], mine[0:24])
    res_sem = fresh(1)
    copy(res_near, res_far, sending(res_near), res_sem, partner)
    for d in (1, 3, 2):
        for a in range(2):
            ref = RG.at[c, 0, (z - d + 4) % 4] if a == 0 else RG.at[c, 1, :, (y - d + 4) % 4]
            take(last[(a, d)], ref)
            copy(ref, ref, swap_send, swap_recv, partner)
    take(swap_recv, RG.at[1 - c])

    tile = jnp.zeros((8, 128), F32)
    for cc in range(2):
        r = RG[cc].astype(F32).reshape(D, 128)
        tile = tile + fold(r * r)
    new = whole(tile)
    beta = new / rr
    tile = jnp.zeros((8, 128), F32)
    for cc in range(2):
        r = RG[cc].astype(F32).reshape(D, 128)
        cols = slice(128 * cc, 128 * cc + 128)
        v = r + beta * going[:, cols].astype(F32)
        tile = tile + fold(v * v)
        going[:, cols] = v.astype(BF16)
    dd = whole(tile)

    tfirst[...] = first_d[...] * nn(states[...], going[...])
    tmix[...] = nn(tfirst[...].astype(BF16), embed[...])
    tangent_norm(256)
    for cc in range(2):
        @pl.loop(0, 6, unroll=True)
        def _(t):
            cols = pl.ds(pl.multiple_of(cc * 1536 + t * 256, 256), 256)
            w = HI[cc, t // 3, t % 3].reshape(D, 256)
            AA[256:512, cols] = (slope[:, cols] * nn(NT[256:512, :], w)).astype(BF16)

    @pl.loop(0, 6, unroll=True)
    def _(t):
        cols = pl.ds(pl.multiple_of(t * 256, 256), 256)
        w = HO[t // 3, t % 3].reshape(FF, 256)
        tlater[:, cols] = (tmix[:, cols] + nn(AA[256:512, :], w)).astype(BF16)

    finish_sweep(1)
    bend = sum_image(1) + DAMPING * dd
    alpha2 = new / bend
    image = summed(1, hi)
    image = jnp.concatenate([image[0:24], image[24:48]], axis=1)
    g = gradient[...]
    take(res_sem, res_far)
    mine = res32[hi]
    mine = jnp.where(c == 0, mine[0:24], mine[24:48])
    other = res_far[...]
    res = jnp.concatenate([jnp.where(c == 0, mine, other), jnp.where(c == 0, other, mine)], axis=1)
    direction = res + beta * g
    out[0:24, :] = alpha1 * g + alpha2 * direction
    out[24:48, :] = res - alpha2 * (image + DAMPING * direction)
    for s_sem, ref in sent:
        describe(ref, ref, s_sem, 0, partner).wait_send()


def body(states, policy, action_embed, norm_gain, hidden_in, hidden_out, precision, gradient):
    vmem = pl.BlockSpec(memory_space=pltpu.VMEM)
    shapes = [
        ((2, 3, 2, 4, 4, 64, 128), BF16),
        ((2, 2, 3, 2, 4, 4, 48, 256), BF16),
        ((2, 3, 2, 4, 4, 2, 48, 256), BF16),
        ((24, 768), F32),
        ((24, 384), F32),
        ((48, 128), F32),
        ((24, 3072), F32),
        ((24, 1536), F32),
        ((D, ACT), BF16),
        ((ACT, D), BF16),
        ((8, D), F32),
        ((2, 4, 4, 48, 128), BF16),
        ((D, ACT), BF16),
        ((D, ROWS), BF16),
        ((D, ROWS), BF16),
        ((512, D), BF16),
        ((512, FF), BF16),
        ((ROWS, FF), F32),
        ((ROWS, D), F32),
        ((ROWS, D), F32),
        ((ROWS, 128), F32),
        ((ROWS, D), F32),
        ((ROWS, ACT), F32),
        ((ROWS, ACT), F32),
        ((ROWS, ACT), F32),
        ((ROWS, D), BF16),
        ((ROWS, D), BF16),
        ((ROWS, D), F32),
        ((ROWS, D), BF16),
        ((ROWS, FF), BF16),
        ((ROWS, ACT), BF16),
        ((ROWS, ACT), BF16),
        ((2, 2, 4, 4, 48, 128), F32),
        ((2, 2, 4, 4, 48, 128), BF16),
        ((2, 2, 4, 4, 48, 128), BF16),
        ((2, 2, 4, 4, 48, 128), F32),
        ((2, 2, 4, 4, 48, 128), BF16),
        ((2, 2, 3, 4, 48, 128), BF16),
        ((2, 2, 4, 48, 128), F32),
        ((2, 2, 4, 48, 128), BF16),
        ((2, 2, 3, 48, 128), BF16),
        ((2, 4, 2, 48, 128), BF16),
        ((3, 4, 4, 8, 128), F32),
        ((2, 48, 128), F32),
        ((2, 48, 128), F32),
        ((2, 2, 4, 4, 48, 128), BF16),
        ((24, 128), F32),
        ((24, 128), F32),
    ]
    both = pl.pallas_call(
        kernel,
        out_shape=jax.ShapeDtypeStruct((48, ACT), F32),
        in_specs=[vmem] * 8,
        out_specs=vmem,
        scratch_shapes=[pltpu.VMEM(s, t) for s, t in shapes]
        + [pltpu.SemaphoreType.DMA((N_SEND,)), pltpu.SemaphoreType.DMA((N_RECV,))],
        compiler_params=pltpu.CompilerParams(
            collective_id=0, has_side_effects=True, vmem_limit_bytes=62 * 2**20
        ),
        name="natural_step",
    )(
        states,
        policy,
        action_embed,
        norm_gain.reshape(1, -1),
        hidden_in,
        hidden_out,
        precision.reshape(1, ACT),
        gradient,
    )
    return both[0:24], both[24:48]


def solution(mesh):
    placed = (
        P(("dp", "fsdp"), None),
        P("fsdp", None),
        P("fsdp", None),
        P("fsdp"),
        P("fsdp", None),
        P("fsdp", None),
        P(),
        P("fsdp", None),
    )
    return jax.shard_map(
        body,
        mesh=mesh,
        in_specs=placed,
        out_specs=(P("fsdp", None), P("fsdp", None)),
        check_vma=False,
    )
```

```python
import functools

import jax
import jax.numpy as jnp
from jax import lax
from jax.experimental import pallas as pl
from jax.experimental.pallas import tpu as pltpu
from jax.sharding import PartitionSpec as P

MESH = pl.DeviceIdType.MESH
F32 = jnp.float32
BF16 = jnp.bfloat16
EPS = 1e-05
DAMPING = 0.1
ALL = slice(None)

ROWS = 256
D = 1536
FF = 3072
ACT = 256
TOTAL_ROWS = 32768
LAST = 4
N_SEND = 75
N_RECV = 108


def nn(left, right):
    return jnp.dot(left, right, preferred_element_type=F32)


def nt(left, right):
    return lax.dot_general(left, right, (((1,), (1,)), ((), ())), preferred_element_type=F32)


def swish_slope(pre, sigma):
    return sigma * (1.0 + pre * (1.0 - sigma))


def kernel(
    states,
    policy_in,
    embed_in,
    gain_in,
    inner_in,
    outer_in,
    precision,
    gradient,
    out,
    S,
    HI,
    HO,
    pack,
    pack_far,
    embed_near,
    inner_wide,
    inner_far,
    policy,
    embed,
    gain,
    gain_tall,
    going,
    start_t,
    later_t,
    NT,
    AA,
    slope,
    mixed,
    unit,
    scale,
    tmix,
    first_d,
    second_d,
    tfirst,
    later,
    tlater,
    cot_later,
    cot_b,
    cot_pre,
    cot_first,
    cot_second,
    IP,
    IPW,
    RB,
    ACC,
    ACCW,
    R1,
    T2,
    T2W,
    R2,
    T3,
    SC,
    g32,
    res32,
    RG,
    res_near,
    res_far,
    send_sem,
    recv_sem,
):
    lo = lax.axis_index("dp")
    f = lax.axis_index("fsdp")
    c = f % 2
    y = (f // 2) % 4
    z = (f // 8) % 4
    hi = f // 32
    x = hi * 2 + lo

    def dev(dx=None, dy=0, dz=0, core=None):
        xx = x if dx is None else (x + dx) % 4
        yy, zz = (y + dy) % 4, (z + dz) % 4
        cc = c if core is None else core
        return (xx % 2, (((xx // 2) * 4 + zz) * 4 + yy) * 2 + cc)

    def axis_dev(axis, d):
        return dev(**{"d" + axis: d})

    opp = ((3 - x) % 2, ((((3 - x) // 2) * 4 + z) * 4 + y) * 2 + c)
    partner = dev(core=1 - c)

    used = [0, 0]
    sent = []

    def fresh(which, n=1):
        used[which] += n
        assert used[which] <= (N_SEND, N_RECV)[which]
        return used[which] - n

    def describe(src, dst, s_sem, r_sem, to):
        return pltpu.make_async_remote_copy(
            src_ref=src,
            dst_ref=dst,
            send_sem=send_sem.at[s_sem],
            recv_sem=recv_sem.at[r_sem],
            device_id=to,
            device_id_type=MESH,
        )

    def copy(src, dst, s_sem, r_sem, to):
        describe(src, dst, s_sem, r_sem, to).start()

    def take(r_sem, ref):
        describe(ref, ref, 0, r_sem, partner).wait_recv()

    def sending(ref):
        s_sem = fresh(0)
        sent.append((s_sem, ref))
        return s_sem

    barrier = pltpu.get_barrier_semaphore()
    peers = [partner] + [axis_dev(a, d) for a in ("x", "y", "z") for d in (1, 2, 3)]
    for peer in peers:
        pl.semaphore_signal(barrier, inc=1, device_id=peer, device_id_type=MESH)
    inner_wide[...] = inner_in[...].astype(F32)
    diagonal = lax.broadcasted_iota(jnp.int32, (24, 24), 0) == lax.broadcasted_iota(jnp.int32, (24, 24), 1)
    gain_row = jnp.broadcast_to(gain_in[...].astype(F32), (24, 24))
    gain_column = jnp.sum(jnp.where(diagonal, gain_row, 0.0), axis=1, keepdims=True)
    for core in range(2):
        pack[:, 384 * core : 384 * core + 128] = policy_in[:, 128 * core : 128 * core + 128].astype(F32)
        pack[:, 384 * core + 128 : 384 * core + 256] = gradient[:, 128 * core : 128 * core + 128]
        pack[:, 384 * core + 256 : 384 * core + 384] = jnp.broadcast_to(gain_column, (24, 128))
    wide = embed_in[...].astype(F32)
    for q in range(4):
        for s in range(3):
            column = 384 * q + 128 * s
            embed_near[16 * s + 4 * q : 16 * s + 4 * q + 4, :] = wide[:, column : column + 128]
    pl.semaphore_wait(barrier, len(peers))

    near_half = pl.ds(pl.multiple_of(c * 384, 128), 384)
    far_half = pl.ds(pl.multiple_of((1 - c) * 384, 128), 384)
    pack_sem = fresh(1)
    copy(pack.at[:, far_half], pack_far, sending(pack_far), pack_sem, partner)
    half = pl.ds(pl.multiple_of((1 - c) * 1536, 128), 1536)
    inner_sem = fresh(1)
    copy(inner_wide.at[:, half], inner_far, sending(inner_far), inner_sem, partner)

    def part(item, t, place, core):
        h, zz, yy, side = place
        if item == 0:
            rows = ALL if side is None else pl.ds(pl.multiple_of(side * 32, 32), 32)
            return S.at[core, t, h, zz, yy, rows, :]
        cols = ALL if side is None else pl.ds(pl.multiple_of(side * 128, 128), 128)
        if item == 1:
            return HI.at[core, :, t, h, zz, yy, :, cols]
        if item >= 5:
            return HI.at[core, item - 5, t, h, zz, yy, :, cols]
        return HO.at[ALL if item == 2 else item - 3, t, h, zz, yy, core, :, cols]

    one = lambda i: pl.ds(i, 1)
    low, high = pl.ds(0, 2), pl.ds(2, 2)
    h0, h1 = pl.ds(0, 1), pl.ds(1, 1)
    first_two, first_three = pl.ds(0, 2), pl.ds(0, 3)
    here, zh, yh = one(hi), one(z), one(y)
    ring_axis = {(0, 2): "y", (0, 3): "z", (1, 2): "z", (1, 3): "x", (2, 2): "x", (2, 3): "y"}

    def piece(t, p, d, sub=None):
        xx, zd, yd = (x + d) % 4, one((z + d) % 4), one((y + d) % 4)
        hs = ALL if sub is None else (h0, h1)[sub]
        pair = ALL if sub is None else (low, high)[sub]
        return {
            (0, 2): (hs, zh, yd, None),
            (0, 3): (hs, zd, ALL, None),
            (1, 2): (here, zd, pair, lo),
            (1, 3): (one(xx // 2), pair, ALL, xx % 2),
            (2, 2): (one(xx // 2), pair, yh, xx % 2),
            (2, 3): (hs, ALL, yd, None),
        }[(t, p)]

    two_pieces = {
        (0, 2): (ALL, zh, first_two, None),
        (0, 3): (ALL, first_two, ALL, None),
        (1, 2): (here, first_two, ALL, lo),
        (1, 3): (here, ALL, ALL, None),
        (2, 2): (here, ALL, yh, None),
        (2, 3): (ALL, ALL, first_two, None),
    }
    three_pieces = {
        (0, 2): (ALL, zh, first_three, None),
        (0, 3): (ALL, first_three, ALL, None),
        (1, 2): (here, first_three, ALL, lo),
        (1, 3): (ALL, first_three, ALL, None),
        (2, 2): (ALL, first_three, yh, None),
        (2, 3): (ALL, ALL, first_three, None),
    }
    recv_of = {}
    send_of = {}

    def ship(k, t, place, s_sem, r_sem, to):
        ref = part(k, t, place, c)
        copy(ref, ref, s_sem, r_sem, to)

    def arrived(k, t, place, key):
        take(recv_of[key], part(k, t, place, c))

    first_places = (
        (here, zh, yh, None),
        (here, zh, first_three, lo),
        (here, first_three, yh, lo),
    )

    def stage_a(k):
        for t in range(3):
            s_sem = sending(part(k, t, first_places[t], c))
            recv_of[(k, t, 1)] = r_sem = fresh(1)
            if t == 0:
                ship(k, t, (here, zh, yh, None), s_sem, r_sem, opp)
            else:
                for d in (1, 3, 2):
                    ship(k, t, (here, zh, yh, lo), s_sem, r_sem, axis_dev("yz"[t - 1], d))

    def ring_start(k, t, p):
        axis = ring_axis[(t, p)]
        s_sem = sending(part(k, t, three_pieces[(t, p)], c))
        send_of[(k, t, p)] = s_sem
        base = fresh(1, 2)
        recv_of[(k, t, p, "near")], recv_of[(k, t, p, "far")] = base, base + 1
        if p == 3 and k == LAST:
            recv_of[(k, t, p, "rest")] = rest = fresh(1)
            for sub, sem in ((0, base), (1, rest)):
                ship(k, t, piece(t, p, 0, sub), s_sem, sem, axis_dev(axis, 1))
                ship(k, t, piece(t, p, 0, 1 - sub), s_sem, sem, axis_dev(axis, 3))
        else:
            ship(k, t, piece(t, p, 0), s_sem, base, axis_dev(axis, 1))
            ship(k, t, piece(t, p, 0), s_sem, base, axis_dev(axis, 3))

    def ring_pass(k, t, p):
        axis = ring_axis[(t, p)]
        s_sem, r_sem = send_of[(k, t, p)], recv_of[(k, t, p, "far")]
        place = piece(t, p, 2) if (k, t, p, "rest") in recv_of else two_pieces[(t, p)]
        arrived(k, t, place, (k, t, p, "near"))
        ship(k, t, piece(t, p, 3, 0), s_sem, r_sem, axis_dev(axis, 1))
        ship(k, t, piece(t, p, 1, 1), s_sem, r_sem, axis_dev(axis, 3))

    def item_whole(k, core):
        if k == 0:
            return S.at[core]
        if k >= 5:
            return HI.at[core, k - 5]
        return HO.at[k - 3, :, :, :, :, core]

    def hand(k, t, d):
        ship(k, t, piece(t, 3, d), send_of[k], recv_of[(k, t, "hand")], partner)

    def stage_b(k):
        for t in range(3):
            arrived(k, t, first_places[t], (k, t, 1))
            ring_start(k, t, 2)

    def stage_g(k):
        for t in range(3):
            ring_pass(k, t, 2)

    before = {0: 0, 5: 1, 3: 2}

    def stage_c(k):
        for t in range(3):
            if k in before:
                arrived(before[k], t, piece(t, 2, 2), (before[k], t, 2, "far"))
            ring_start(k, t, 3)
        send_of[k] = sending(item_whole(k, c))
        shared = None if k == LAST else fresh(1)
        for t in range(3):
            recv_of[(k, t, "hand")] = fresh(1) if k == LAST else shared
            hand(k, t, 0)

    def stage_pass(k):
        for t in range(3):
            ring_pass(k, t, 3)

    def stage_d(k):
        for t in range(3):
            if (k, t, 3, "rest") in recv_of:
                arrived(k, t, piece(t, 3, 2), (k, t, 3, "rest"))
            hand(k, t, 3)
            hand(k, t, 1)

    def stage_e(k):
        for t in range(3):
            arrived(k, t, piece(t, 3, 2), (k, t, 3, "far"))
            hand(k, t, 2)

    def stage_f(k):
        take(recv_of[(k, 0, "hand")], item_whole(k, 1 - c))

    scalar_sems = {}
    places = (("core", c, 2), ("y", y, 4), ("z", z, 4), ("x", x, 4))

    def total_send(which, phase, value):
        axis, own, n = places[phase]
        SC[which, phase, own] = value
        ref = SC.at[which, phase, own]
        others = SC.at[which, phase, pl.ds(0, n - 1)]
        s_sem = sending(others)
        scalar_sems[(which, phase)] = r_sem = fresh(1)
        for d in range(1, n):
            to = partner if axis == "core" else axis_dev(axis, d)
            copy(ref, ref, s_sem, r_sem, to)

    def total_take(which, phase):
        n = places[phase][2]
        take(scalar_sems[(which, phase)], SC.at[which, phase, pl.ds(0, n - 1)])
        value = SC[which, phase, 0]
        for i in range(1, n):
            value = value + SC[which, phase, i]
        return value

    def total_step(which, phase):
        value = total_take(which, phase)
        if phase < 3:
            total_send(which, phase + 1, value)
        return value

    def fold(value):
        value = value.reshape(-1, 8, value.shape[-1]).sum(axis=0)
        tile = value[:, 0:128]
        for i in range(1, value.shape[-1] // 128):
            tile = tile + value[:, 128 * i : 128 * i + 128]
        return tile

    def whole(tile):
        return jnp.sum(jnp.sum(tile, axis=1, keepdims=True), axis=0, keepdims=True)

    weigh_rows = outer_in
    for ct in range(6):
        if ct % 3:
            left = weigh_rows[:, 256 * ct : 256 * ct + 128]
            right = weigh_rows[:, 256 * ct + 128 : 256 * ct + 256]
            HO[ct // 3, ct % 3, hi, z, y, c, :, pl.ds(pl.multiple_of(lo * 128, 128), 128)] = jnp.where(lo == 0, left, right)
        else:
            HO[ct // 3, ct % 3, hi, z, y, c] = weigh_rows[:, 256 * ct : 256 * ct + 256]

    stage_a(2)
    near = pack[:, near_half]
    g_own = gradient[...]
    total_send(0, 0, fold(g_own * g_own))
    take(pack_sem, pack_far)
    far = pack_far[...]
    pair = jnp.concatenate([jnp.where(c == 0, near, far), jnp.where(c == 0, far, near)], axis=0)
    g32[hi] = pair[:, 128:256]
    gains = pair[:, 256:384].astype(BF16)
    S[c, 0, hi, z, y, 0:48] = pair[:, 0:128].astype(BF16)
    S[c, 0, hi, z, y, 48:64] = gains[0:16]
    gb = pair[:, 128:256]
    both = jnp.concatenate([gb, pair[16:32, 256:384]], axis=0)
    S[c, 1, hi, z, y, pl.ds(pl.multiple_of(lo * 32, 32), 32)] = jnp.where(lo == 0, both[0:32], both[32:64]).astype(BF16)
    both = jnp.concatenate([embed_near[...], pair[32:48, 256:384]], axis=0)
    S[c, 2, hi, z, y, pl.ds(pl.multiple_of(lo * 32, 32), 32)] = jnp.where(lo == 0, both[0:32], both[32:64]).astype(BF16)
    stage_a(0)
    g_sem = fresh(1)
    copy(g32.at[hi], g32.at[hi], sending(g32.at[hi]), g_sem, opp)

    take(inner_sem, inner_far)
    near = inner_wide[:, pl.ds(pl.multiple_of(c * 1536, 128), 1536)]
    far = inner_far[...]
    pair = jnp.concatenate([jnp.where(c == 0, near, far), jnp.where(c == 0, far, near)], axis=0)
    for ct in range(6):
        if ct % 3:
            left = pair[:, 256 * ct : 256 * ct + 128]
            right = pair[:, 256 * ct + 128 : 256 * ct + 256]
            HI[c, ct // 3, ct % 3, hi, z, y, :, pl.ds(pl.multiple_of(lo * 128, 128), 128)] = jnp.where(lo == 0, left, right).astype(BF16)
        else:
            HI[c, ct // 3, ct % 3, hi, z, y] = pair[:, 256 * ct : 256 * ct + 256].astype(BF16)
    stage_a(1)
    stage_b(2)
    stage_b(0)
    stage_b(1)
    stage_g(2)
    stage_g(0)
    stage_g(1)
    stage_c(0)
    total_step(0, 0)
    stage_c(5)
    total_step(0, 1)
    stage_pass(0)
    stage_d(0)

    @pl.loop(0, 6)
    def _(i):
        s = pl.ds(pl.multiple_of(i * 256, 256), 256)
        start_t[s, :] = states[:, s].astype(F32).T.astype(BF16)

    stage_c(6)
    stage_e(0)
    total_step(0, 2)
    stage_f(0)
    rr = whole(total_step(0, 3)) * 0.5

    for t in range(3):
        for a in range(2):
            for b in range(4):
                gain_tall[a, b, :, 16 * t : 16 * t + 16] = S[0, t, a, b, :, 48:64]
    pick = (lax.broadcasted_iota(jnp.int32, (16, 128), 1) == 0).astype(BF16)
    gain[...] = nt(pick, gain_tall[...].reshape(D, 128))[0:8]
    for cc in range(2):
        for a in range(2):
            policy[768 * a : 768 * a + 768, 128 * cc : 128 * cc + 128] = S[cc, 0, a, :, :, 0:48].reshape(768, 128)
            going[768 * a : 768 * a + 768, 128 * cc : 128 * cc + 128] = S[cc, 1, a, :, :, 0:48].reshape(768, 128)
    for q in range(4):
        total = jnp.zeros((ACT, 384), F32)
        for cc in range(2):
            out_row = lax.broadcasted_iota(jnp.int32, (ACT, 512), 0)
            in_row = lax.broadcasted_iota(jnp.int32, (ACT, 512), 1)
            want = (lax.div(out_row, 8) * 16) + 4 * q + lax.rem(out_row, 4)
            mine = lax.rem(lax.div(out_row, 4), 2) == cc
            choose = jnp.where(mine & (in_row == want), 1.0, 0.0).astype(BF16)
            block = jnp.concatenate(
                [S[cc, 2, :, :, :, 16 * s : 16 * s + 16].reshape(512, 128) for s in range(3)], axis=1
            )
            total = total + nn(choose, block)
        embed[:, 384 * q : 384 * q + 384] = total.astype(BF16)

    def blocks(n):
        return pl.loop(0, ROWS // n)

    stage_pass(5)
    stage_d(5)
    stage_c(3)

    first = jnp.tanh(nn(states[...], policy[...]))
    first_d[...] = 1.0 - first * first
    mixed[...] = nn(first.astype(BF16), embed[...])
    tfirst[...] = first_d[...] * nn(states[...], going[...])
    tmix[...] = nn(tfirst[...].astype(BF16), embed[...])

    @blocks(32)
    def _(i):
        s = pl.ds(pl.multiple_of(i * 32, 32), 32)
        m = states[s, :].astype(F32) + mixed[s, :]
        mixed[s, :] = m
        r = lax.rsqrt(jnp.mean(m * m, axis=-1, keepdims=True) + EPS)
        scale[s, :] = jnp.broadcast_to(r, (32, 128))
        u = m * r
        unit[s, :] = u
        g = gain[0:1, :]
        NT[s, :] = (u * g).astype(BF16)

    def tangent_norm(offset):
        @blocks(32)
        def _(i):
            s = pl.ds(pl.multiple_of(i * 32, 32), 32)
            o = pl.ds(pl.multiple_of(i * 32 + offset, 32), 32)
            u, v, g = unit[s, :], tmix[s, :], gain[0:1, :]
            w = scale[s, 0:1] * (v - u * jnp.mean(u * v, axis=-1, keepdims=True))
            NT[o, :] = (w * g).astype(BF16)

    tangent_norm(256)

    stage_e(5)
    stage_pass(6)
    stage_d(6)
    stage_c(4)
    stage_f(5)

    def take_inner(ch, cc):
        @pl.loop(0, 3, unroll=True)
        def _(t):
            w = HI[cc, ch, t].reshape(D, 256)
            cols = pl.ds(pl.multiple_of(cc * 1536 + ch * 768 + t * 256, 256), 256)
            pre = nn(NT[0:256, :], w)
            sigma = jax.nn.sigmoid(pre)
            AA[0:256, cols] = (pre * sigma).astype(BF16)
            sl = swish_slope(pre, sigma)
            slope[:, cols] = sl
            AA[256:512, cols] = (sl * nn(NT[256:512, :], w)).astype(BF16)

    take_inner(0, 0)
    take_inner(0, 1)
    stage_e(6)
    stage_pass(3)
    stage_d(3)
    stage_f(6)
    take_inner(1, 0)
    stage_e(3)
    stage_pass(4)
    take_inner(1, 1)
    stage_d(4)
    stage_f(3)

    def take_outer(ch, t):
        w = HO[ch, t].reshape(FF, 256)
        cols = pl.ds(pl.multiple_of(ch * 768 + t * 256, 256), 256)
        l = (mixed[:, cols] + nn(AA[0:256, :], w)).astype(BF16)
        later[:, cols] = l
        later_t[cols, :] = l.astype(F32).T.astype(BF16)
        tlater[:, cols] = (tmix[:, cols] + nn(AA[256:512, :], w)).astype(BF16)

    @pl.loop(0, 3, unroll=True)
    def _(t):
        take_outer(0, t)

    stage_e(4)
    for t in range(3):
        take(recv_of[(LAST, t, "hand")], part(LAST, t, (ALL, ALL, ALL, None), 1 - c))
        take_outer(1, t)
    take(g_sem, g32.at[1 - hi])

    second = jnp.tanh(nn(later[...], policy[...]))
    second_d[...] = 1.0 - second * second
    weighting = precision[...] * (1.0 / TOTAL_ROWS)

    def finish_sweep(it):
        tsecond = second_d[...] * (nn(tlater[...], policy[...]) + nn(later[...], going[...]))
        tf = tfirst[...]
        total_send(1 + it, 0, fold(weighting * (tf * tf + tsecond * tsecond)))
        cs = (second_d[...] * (weighting * tsecond)).astype(BF16)
        cot_second[...] = cs
        cl = nt(cs, policy[...])
        cot_later[...] = cl
        cot_b[...] = cl.astype(BF16)

        @pl.loop(0, 4, unroll=True)
        def _(i):
            a, b = i // 2, i % 2
            acc = jnp.zeros((ROWS, 768), F32)
            for ct in range(6):
                w = HO[ct // 3, ct % 3, a, pl.ds(b * 2, 2)].reshape(768, 256)
                acc = acc + nt(cot_b[:, 256 * ct : 256 * ct + 256], w)
            cols = pl.ds(pl.multiple_of(i * 768, 256), 768)
            cot_pre[:, cols] = (slope[:, cols] * acc).astype(BF16)

        total_step(1 + it, 0)

        @pl.loop(0, 2, unroll=True)
        def _(a):
            acc = jnp.zeros((ROWS, 768), F32)
            for n in range(12):
                w = HI[n // 6, n // 3 % 2, n % 3, a].reshape(768, 256)
                acc = acc + nt(cot_pre[:, 256 * n : 256 * n + 256], w)
            cols = pl.ds(pl.multiple_of(a * 768, 256), 768)
            tmix[:, cols] = acc

        total_step(1 + it, 1)

        @blocks(32)
        def _(i):
            s = pl.ds(pl.multiple_of(i * 32, 32), 32)
            u, g = unit[s, :], gain[0:1, :]
            v = tmix[s, :] * g
            w = scale[s, 0:1] * (v - u * jnp.mean(u * v, axis=-1, keepdims=True))
            cot_b[s, :] = (cot_later[s, :] + w).astype(BF16)

        cf = (first_d[...] * (weighting * tfirst[...] + nt(cot_b[...], embed[...]))).astype(BF16)
        cot_first[...] = cf

    def halves(v, it):
        if it == 0:
            low_half, high_half = v[:, 0:128], v[:, 128:256]
            low_half, high_half = low_half.reshape(16, 48, 128), high_half.reshape(16, 48, 128)
        else:
            v = v.reshape(16, 48, 256)
            low_half = jnp.concatenate([v[:, 0:24, 0:128], v[:, 0:24, 128:256]], axis=1)
            high_half = jnp.concatenate([v[:, 24:48, 0:128], v[:, 24:48, 128:256]], axis=1)
        return jnp.where(c == 0, low_half, high_half), jnp.where(c == 0, high_half, low_half)

    def sum_image(it):
        swap = []
        for a in range(2):
            rows = slice(768 * a, 768 * a + 768)
            v = nn(start_t[rows, :], cot_first[...]) + nn(later_t[rows, :], cot_second[...])
            keep, give = halves(v, it)
            IPW[it, a] = give.reshape(4, 4, 48, 128).astype(BF16)
            swap.append(fresh(1))
            copy(IPW.at[it, a], RB.at[it, a], sending(IPW.at[it, a]), swap[a], partner)
            IP[it, a] = keep.reshape(4, 4, 48, 128)
        total_step(1 + it, 2)
        sems = []
        for a in range(2):
            take(swap[a], RB.at[it, a])
            v = IP[it, a] + RB[it, a].astype(F32)
            ACC[it, a] = v
            ACCW[it, a] = v.astype(BF16)
            s_sem = sending(R1.at[it, a])
            sems.append(fresh(1))
            for d in (2, 1, 3):
                if a == 0:
                    copy(ACCW.at[it, 0, :, (y + d) % 4], R1.at[it, 0, d - 1], s_sem, sems[a], axis_dev("y", d))
                else:
                    copy(ACCW.at[it, 1, (z + d) % 4], R1.at[it, 1, d - 1], s_sem, sems[a], axis_dev("z", d))
        total = whole(total_step(1 + it, 3))
        second_sems = []
        for a in range(2):
            take(sems[a], R1.at[it, a])
            v = ACC[it, 0, :, y] if a == 0 else ACC[it, 1, z]
            for d in range(3):
                v = v + R1[it, a, d].astype(F32)
            T2[it, a] = v
            T2W[it, a] = v.astype(BF16)
            s_sem = sending(R2.at[it, a])
            second_sems.append(fresh(1))
            axis, own = ("z", z) if a == 0 else ("y", y)
            for d in (2, 1, 3):
                copy(T2W.at[it, a, (own + d) % 4], R2.at[it, a, d - 1], s_sem, second_sems[a], axis_dev(axis, d))
        third_sems = []
        for a in range(2):
            take(second_sems[a], R2.at[it, a])
            v = T2[it, a, z if a == 0 else y]
            for d in range(3):
                v = v + R2[it, a, d].astype(F32)
            T3[it, x, a] = v.astype(BF16)
            three = T3.at[it, pl.ds(0, 3), a]
            s_sem = sending(three)
            third_sems.append(fresh(1))
            for d in (2, 1, 3):
                copy(T3.at[it, x, a], T3.at[it, x, a], s_sem, third_sems[a], axis_dev("x", d))
        for a in range(2):
            take(third_sems[a], T3.at[it, pl.ds(0, 3), a])
        return total

    def summed(it, h):
        v = T3[it, 0, h].astype(F32)
        for i in range(1, 4):
            v = v + T3[it, i, h].astype(F32)
        return v

    finish_sweep(0)
    bend = sum_image(0) + DAMPING * rr
    alpha1 = rr / bend
    for a in range(2):
        g = g32[a]
        residual = g - alpha1 * (summed(0, a) + DAMPING * g)
        res32[a] = residual
        RG[c, a, z, y] = residual.astype(BF16)
    three = (RG.at[c, 0, z, first_three], RG.at[c, 1, first_three, y])
    sems = (fresh(1), fresh(1))
    s_sems = (sending(three[0]), sending(three[1]))
    for d in (2, 1, 3):
        ref = RG.at[c, 0, z, y]
        copy(ref, ref, s_sems[0], sems[0], axis_dev("y", d))
        ref = RG.at[c, 1, z, y]
        copy(ref, ref, s_sems[1], sems[1], axis_dev("z", d))
    swap_send, swap_recv = sending(RG.at[c]), fresh(1)
    s_sems = (sending(RG.at[c, 0, first_three]), sending(RG.at[c, 1, :, first_three]))
    last = {}
    for a in range(2):
        take(sems[a], three[a])
        ref = RG.at[c, 0, z] if a == 0 else RG.at[c, 1, :, y]
        for d in (2, 1, 3):
            last[(a, d)] = fresh(1)
            copy(ref, ref, s_sems[a], last[(a, d)], axis_dev("zy"[a], d))
        copy(ref, ref, swap_send, swap_recv, partner)
    mine = res32[hi]
    res_near[...] = jnp.where(c == 0, mine[24:48], mine[0:24])
    res_sem = fresh(1)
    copy(res_near, res_far, sending(res_near), res_sem, partner)
    for d in (1, 3, 2):
        for a in range(2):
            ref = RG.at[c, 0, (z - d + 4) % 4] if a == 0 else RG.at[c, 1, :, (y - d + 4) % 4]
            take(last[(a, d)], ref)
            copy(ref, ref, swap_send, swap_recv, partner)
    take(swap_recv, RG.at[1 - c])

    tile = jnp.zeros((8, 128), F32)
    for cc in range(2):
        r = RG[cc].astype(F32).reshape(D, 128)
        tile = tile + fold(r * r)
    new = whole(tile)
    beta = new / rr
    tile = jnp.zeros((8, 128), F32)
    for cc in range(2):
        r = RG[cc].astype(F32).reshape(D, 128)
        cols = slice(128 * cc, 128 * cc + 128)
        v = r + beta * going[:, cols].astype(F32)
        tile = tile + fold(v * v)
        going[:, cols] = v.astype(BF16)
    dd = whole(tile)

    tfirst[...] = first_d[...] * nn(states[...], going[...])
    tmix[...] = nn(tfirst[...].astype(BF16), embed[...])
    tangent_norm(256)
    for cc in range(2):
        @pl.loop(0, 6, unroll=True)
        def _(t):
            cols = pl.ds(pl.multiple_of(cc * 1536 + t * 256, 256), 256)
            w = HI[cc, t // 3, t % 3].reshape(D, 256)
            AA[256:512, cols] = (slope[:, cols] * nn(NT[256:512, :], w)).astype(BF16)

    @pl.loop(0, 6, unroll=True)
    def _(t):
        cols = pl.ds(pl.multiple_of(t * 256, 256), 256)
        w = HO[t // 3, t % 3].reshape(FF, 256)
        tlater[:, cols] = (tmix[:, cols] + nn(AA[256:512, :], w)).astype(BF16)

    finish_sweep(1)
    bend = sum_image(1) + DAMPING * dd
    alpha2 = new / bend
    image = summed(1, hi)
    image = jnp.concatenate([image[0:24], image[24:48]], axis=1)
    g = gradient[...]
    take(res_sem, res_far)
    mine = res32[hi]
    mine = jnp.where(c == 0, mine[0:24], mine[24:48])
    other = res_far[...]
    res = jnp.concatenate([jnp.where(c == 0, mine, other), jnp.where(c == 0, other, mine)], axis=1)
    direction = res + beta * g
    out[0:24, :] = alpha1 * g + alpha2 * direction
    out[24:48, :] = res - alpha2 * (image + DAMPING * direction)
    for s_sem, ref in sent:
        describe(ref, ref, s_sem, 0, partner).wait_send()


def body(states, policy, action_embed, norm_gain, hidden_in, hidden_out, precision, gradient):
    vmem = pl.BlockSpec(memory_space=pltpu.VMEM)
    shapes = [
        ((2, 3, 2, 4, 4, 64, 128), BF16),
        ((2, 2, 3, 2, 4, 4, 48, 256), BF16),
        ((2, 3, 2, 4, 4, 2, 48, 256), BF16),
        ((24, 768), F32),
        ((24, 384), F32),
        ((48, 128), F32),
        ((24, 3072), F32),
        ((24, 1536), F32),
        ((D, ACT), BF16),
        ((ACT, D), BF16),
        ((8, D), F32),
        ((2, 4, 4, 48, 128), BF16),
        ((D, ACT), BF16),
        ((D, ROWS), BF16),
        ((D, ROWS), BF16),
        ((512, D), BF16),
        ((512, FF), BF16),
        ((ROWS, FF), F32),
        ((ROWS, D), F32),
        ((ROWS, D), F32),
        ((ROWS, 128), F32),
        ((ROWS, D), F32),
        ((ROWS, ACT), F32),
        ((ROWS, ACT), F32),
        ((ROWS, ACT), F32),
        ((ROWS, D), BF16),
        ((ROWS, D), BF16),
        ((ROWS, D), F32),
        ((ROWS, D), BF16),
        ((ROWS, FF), BF16),
        ((ROWS, ACT), BF16),
        ((ROWS, ACT), BF16),
        ((2, 2, 4, 4, 48, 128), F32),
        ((2, 2, 4, 4, 48, 128), BF16),
        ((2, 2, 4, 4, 48, 128), BF16),
        ((2, 2, 4, 4, 48, 128), F32),
        ((2, 2, 4, 4, 48, 128), BF16),
        ((2, 2, 3, 4, 48, 128), BF16),
        ((2, 2, 4, 48, 128), F32),
        ((2, 2, 4, 48, 128), BF16),
        ((2, 2, 3, 48, 128), BF16),
        ((2, 4, 2, 48, 128), BF16),
        ((3, 4, 4, 8, 128), F32),
        ((2, 48, 128), F32),
        ((2, 48, 128), F32),
        ((2, 2, 4, 4, 48, 128), BF16),
        ((24, 128), F32),
        ((24, 128), F32),
    ]
    both = pl.pallas_call(
        kernel,
        out_shape=jax.ShapeDtypeStruct((48, ACT), F32),
        in_specs=[vmem] * 8,
        out_specs=vmem,
        scratch_shapes=[pltpu.VMEM(s, t) for s, t in shapes]
        + [pltpu.SemaphoreType.DMA((N_SEND,)), pltpu.SemaphoreType.DMA((N_RECV,))],
        compiler_params=pltpu.CompilerParams(
            collective_id=0, has_side_effects=True, vmem_limit_bytes=62 * 2**20
        ),
        name="natural_step",
    )(
        states,
        policy,
        action_embed,
        norm_gain.reshape(1, -1),
        hidden_in,
        hidden_out,
        precision.reshape(1, ACT),
        gradient,
    )
    return both[0:24], both[24:48]


def solution(mesh):
    placed = (
        P(("dp", "fsdp"), None),
        P("fsdp", None),
        P("fsdp", None),
        P("fsdp"),
        P("fsdp", None),
        P("fsdp", None),
        P(),
        P("fsdp", None),
    )
    return jax.shard_map(
        body,
        mesh=mesh,
        in_specs=placed,
        out_specs=(P("fsdp", None), P("fsdp", None)),
        check_vma=False,
    )
```
